512 devices in a mesh: lon: 32 (over z, core), lat: 8 (over y, x_hi), dp: 2 (over x_lo).
Axes of the slice: x: 4 (x_hi: 2, x_lo: 2; x = x_hi * 2 + x_lo), y: 4, z: 16, core: 2. Of those that a mesh axis runs over, the one named last changes fastest.
Arguments:
- states: bfloat16 [2, 128, 2048, 192], P('dp', 'lat', 'lon'), may hold values from -6 to 6
- cotangent: bfloat16 [2, 128, 2048, 192], P('dp', 'lat', 'lon'), may hold values from -6 to 6
- kernel: bfloat16 [3, 3, 192, 192], replicated, may hold values from -0.15625 to 0.15625
- land_mask: int32 [128, 2048], P('lat', 'lon'), may hold values 0 or 1
- ocean_tiles: int32 [8, 32, 3], P('lat', 'lon'), may hold values from 0 to 4, as said below
Outputs:
- output: bfloat16 [2, 128, 2048, 192], P('dp', 'lat', 'lon')
- state_grad: bfloat16 [2, 128, 2048, 192], P('dp', 'lat', 'lon')
- weight_grad: float32 [3, 3, 192, 192], replicated
The draws below stay inside these ranges and needn't reach their ends.
Inputs may be any that keep to these rules, and one draw needn't show every extreme that they name: `ocean_tiles`: each device's 3 entries are distinct tile numbers of its block in increasing order, followed by the value 4 in unused slots; at least one slot is used, and some device uses all of them.
All inputs are finite; a program needn't handle non-finite values. No bound on the sum of `land_mask` on one device may be relied on, other than what follows from the above.
Results may differ from the reference program's by a relative error of at most 0.0049.
Values may be sent and summed in bfloat16 or wider, within the bound.
No kernel may reach another device: no remote copies, remote signals or barrier semaphores. Data moves between devices by JAX's collectives and lax.ppermute only.
A program may use at most 64 MiB of HBM per device.

```python
import math
import jax
import jax.numpy as jnp
from jax import lax

C = 192
TS = 16
CY = 16
CX = 64
BATCH = 2
NY = 128
NX = 2048
TPD = 4
CAP = 3
N_LON = 32
N_LAT = 8


def draw_ocean_tiles(key, part):
    key = jax.random.fold_in(key, 17)
    devices_all = N_LAT * N_LON
    score_key, count_key, pick_key = jax.random.split(key, 3)
    score_table = jax.random.randint(score_key, (devices_all, TPD), 0, 1 << 30)
    tile_order = jnp.argsort(score_table, axis=1, stable=True).astype(jnp.int32)
    chosen = jnp.sort(tile_order[:, :CAP], axis=1)
    lowest = max(CAP // 2, 1)
    live_count = jax.random.randint(count_key, (devices_all,), lowest, CAP + 1)
    fullest = jax.random.randint(pick_key, (), 0, devices_all)
    device_ids = jnp.arange(devices_all)
    live_count = jnp.where(device_ids == fullest, CAP, live_count)
    live_count = jnp.where(device_ids == (fullest + 1) % devices_all, lowest, live_count)
    slot_index = jnp.arange(CAP)[None, :]
    listed = jnp.where(slot_index < live_count[:, None], chosen, TPD)
    return listed.reshape(N_LAT, N_LON, CAP).astype(jnp.int32)


def touch_ends(values, own_key, smallest, largest):
    index_at = [jax.random.randint(jax.random.fold_in(own_key, axis), (), 0, length) for axis, length in enumerate(values.shape)]
    widest = values.shape.index(max(values.shape))
    beside = index_at[:widest] + [(index_at[widest] + 1) % values.shape[widest]] + index_at[widest + 1:]
    return values.at[tuple(index_at)].set(smallest).at[tuple(beside)].set(largest)


def steps_of(key, shape, cuts, smallest, high):
    def one(axis_at, parts):
        steps = jax.random.uniform(jax.random.fold_in(jax.random.fold_in(key, 6), axis_at), (parts,), jnp.float32, smallest / len(cuts), high / len(cuts))
        return jnp.repeat(jnp.exp(steps), shape[axis_at] // parts).reshape((-1,) + (1,) * (len(shape) - axis_at - 1))

    level = one(*cuts[0])
    for cut in cuts[1:]:
        level = level * one(*cut)
    return level


def scatter_about(rng, extent, width, most, cuts=(), kind=jnp.bfloat16):
    result = jax.random.normal(rng, extent, jnp.float32) * width
    if len(cuts) > 0:
        result = steps_of(rng, extent, cuts, -0.22, 0.18) * result
    return jnp.clip(result, min=-most, max=most).astype(kind)


def setup_inputs(seed: int = 0) -> dict:
    key_list = jax.random.split(jax.random.key(seed), 6)
    return {
        "states": scatter_about(key_list[0], (BATCH, NY, NX, C), 1.0, 6.0, ((0, 2), (1, 8), (2, 32))),
        "cotangent": scatter_about(key_list[1], (BATCH, NY, NX, C), 1.0, 6.0, ((0, 2), (1, 8), (2, 32))),
        "kernel": scatter_about(key_list[2], (3, 3, C, C), (9 * C) ** -0.5, 0.15625),
        "land_mask": touch_ends((jax.random.randint(key_list[3], (NY, NX), 0, 4) < 3).astype(jnp.int32), jax.random.fold_in(key_list[3], 1), 0, 1),
        "ocean_tiles": draw_ocean_tiles(jax.random.fold_in(key_list[5], 71), 0),
    }


def live_cells(ocean_tiles):
    tile_rows = CY // TS
    tile_cols = CX // TS
    numbers = jnp.arange(TPD, dtype=jnp.int32)
    hit = jnp.any(ocean_tiles[..., None] == numbers, axis=2)
    table = hit.reshape(N_LAT, N_LON, tile_rows, tile_cols).transpose(0, 2, 1, 3)
    table = table.reshape(N_LAT * tile_rows, N_LON * tile_cols).astype(jnp.float32)
    return jnp.repeat(jnp.repeat(table, TS, axis=0), TS, axis=1)

def pad_fold(masked):
    wrapped = jnp.concatenate([masked[:, :, -1:], masked, masked[:, :, :1]], axis=2)
    north = jnp.flip(wrapped[:, -1:], axis=2)
    return jnp.concatenate([jnp.zeros_like(north), wrapped, north], axis=1)

def reference(states, cotangent, kernel, land_mask, ocean_tiles):
    keep_cells = land_mask.astype(jnp.float32) * live_cells(ocean_tiles)
    keep_full = keep_cells[None, :, :, None]
    masked = jnp.where(keep_full > 0, states, jnp.zeros_like(states))
    padded = pad_fold(masked)
    channels = states.shape[3]
    flat_count = BATCH * NY * NX
    preact = jnp.zeros((BATCH, NY, NX, channels), jnp.float32)
    for row_shift in range(3):
        for col_shift in range(3):
            window = padded[:, row_shift:row_shift + NY, col_shift:col_shift + NX].reshape(flat_count, channels)
            term = jnp.dot(window, kernel[row_shift, col_shift], preferred_element_type=jnp.float32)
            preact = preact + term.reshape(BATCH, NY, NX, channels)
    sigmoid_h = jax.nn.sigmoid(preact)
    output = (keep_full * preact * sigmoid_h).astype(jnp.bfloat16)
    slope = sigmoid_h * (1.0 + preact * (1.0 - sigmoid_h))
    grad_pre = (keep_full * cotangent.astype(jnp.float32) * slope).astype(jnp.bfloat16)
    grad_flat = grad_pre.reshape(flat_count, channels)
    grad_pad = jnp.zeros((BATCH, NY + 2, NX + 2, channels), jnp.float32)
    kernel_terms = []
    for row_shift in range(3):
        for col_shift in range(3):
            window = padded[:, row_shift:row_shift + NY, col_shift:col_shift + NX].reshape(flat_count, channels)
            kernel_terms.append(lax.dot_general(window, grad_flat, (((0,), (0,)), ((), ())), preferred_element_type=jnp.float32))
            backed = jnp.dot(grad_flat, kernel[row_shift, col_shift].T, preferred_element_type=jnp.float32)
            grad_pad = grad_pad.at[:, row_shift:row_shift + NY, col_shift:col_shift + NX].add(backed.reshape(BATCH, NY, NX, channels))
    weight_grad = jnp.stack(kernel_terms).reshape(3, 3, channels, channels) / math.sqrt(flat_count)
    unfolded = grad_pad[:, 1:NY + 1]
    unfolded = unfolded.at[:, NY - 1].add(jnp.flip(grad_pad[:, NY + 1], axis=1))
    inner = unfolded[:, :, 1:NX + 1]
    inner = inner.at[:, :, NX - 1].add(unfolded[:, :, 0])
    inner = inner.at[:, :, 0].add(unfolded[:, :, NX + 1])
    state_grad = (keep_full * inner).astype(jnp.bfloat16)
    return (output, state_grad, weight_grad)
```

```python
import math

import jax
import jax.numpy as jnp
from jax import lax
from jax.experimental import pallas as pl
from jax.experimental.pallas import tpu as pltpu
from jax.sharding import Mesh
from jax.sharding import PartitionSpec as P

BF = jnp.bfloat16
F32 = jnp.float32
TS = 16
ROWS = 16
COLS = 64
C = 192
S = 80
LEAD = 96
PACKED = 2592


def iota(shape, dim):
    return lax.broadcasted_iota(jnp.int32, shape, dim)


def params(mib):
    return pltpu.CompilerParams(vmem_limit_bytes=mib * 2**20)


def keep_plane(mask_ref, tiles_ref):
    tile = iota((ROWS, COLS), 1) // TS
    listed = jnp.zeros((ROWS, COLS), F32)
    for slot in range(tiles_ref.shape[-1]):
        listed = jnp.where(tile == tiles_ref[0, 0, slot], 1.0, listed)
    return jnp.where(mask_ref[...] > 0, listed, 0.0)


def edge_kernel(states_ref, cot_ref, mask_ref, tiles_ref, east_ref, west_ref):
    keep = keep_plane(mask_ref, tiles_ref)

    def column(ref, col):
        base = col // 16 * 16
        part = jnp.concatenate([ref[0, r, base : base + 16, :] for r in range(ROWS)], axis=0)
        spot = iota((ROWS, 256), 1) == iota((ROWS, 256), 0) * 16 + (col - base)
        picked = jnp.dot(spot.astype(F32).astype(BF), part, preferred_element_type=F32)
        return jnp.where(keep[:, col : col + 1] > 0, picked, 0.0).astype(BF)

    east_ref[0] = column(states_ref, COLS - 2)
    east_ref[1] = column(states_ref, COLS - 1)
    east_ref[2] = column(cot_ref, COLS - 1)
    west_ref[0] = column(states_ref, 0)
    west_ref[1] = column(states_ref, 1)
    west_ref[2] = column(cot_ref, 0)


def rows_kernel(
    states_ref, cot_ref, mask_ref, tiles_ref, from_west, from_east, place_ref,
    xrow_ref, crow_ref, ahead_ref, back_ref,
):
    keep_t = keep_plane(mask_ref, tiles_ref).T
    halo = jnp.concatenate(
        [from_west[i] for i in range(3)] + [from_east[i] for i in range(3)], axis=0
    )
    row = iota((256, 96), 0) // 16
    spot = iota((256, 96), 0) % 16
    source = iota((256, 96), 1)

    def chunk(at):
        want = jnp.full((256, 96), -1, jnp.int32)
        for where, plane in at:
            want = jnp.where(spot == where, plane * 16 + row, want)
        pick = (source == want).astype(F32).astype(BF)
        return jnp.dot(pick, halo, preferred_element_type=F32).astype(BF)

    x_chunk = chunk([(0, 3), (1, 4), (14, 0), (15, 1)])
    c_chunk = chunk([(0, 5), (15, 2)])
    for r in range(ROWS):
        kept = keep_t[:, r : r + 1] > 0
        xrow_ref[r, 0:COLS, :] = jnp.where(kept, states_ref[0, r].astype(F32), 0.0).astype(BF)
        crow_ref[r, 0:COLS, :] = jnp.where(kept, cot_ref[0, r].astype(F32), 0.0).astype(BF)
        xrow_ref[r, COLS:S, :] = x_chunk[r * 16 : r * 16 + 16]
        crow_ref[r, COLS:S, :] = c_chunk[r * 16 : r * 16 + 16]
    top = [xrow_ref.at[ROWS - 1], xrow_ref.at[ROWS - 2], crow_ref.at[ROWS - 1]]
    bottom = [xrow_ref.at[0], xrow_ref.at[1], crow_ref.at[0]]

    @pl.when(place_ref[0] == 1)
    def _():
        for i in range(3):
            ahead_ref[i] = top[i][...]
            back_ref[i] = bottom[i][...]

    @pl.when(place_ref[0] == 0)
    def _():
        for i in range(3):
            ahead_ref[i] = bottom[i][...]
            back_ref[i] = top[i][...]


def main_kernel(
    xrow_ref, crow_ref, ahead_ref, back_ref, kernel_ref, mask_ref, tiles_ref, place_ref,
    out_ref, sgrad_ref, wgrad_ref,
    xe, ce, ga, go, ys, xt, north, south,
):
    first_half = place_ref[0] == 1
    fold = place_ref[1] == 1
    keep_t = keep_plane(mask_ref, tiles_ref).T

    @pl.when(first_half)
    def _():
        north[...] = back_ref[...]
        south[...] = ahead_ref[...]

    @pl.when(jnp.logical_not(first_half))
    def _():
        north[...] = ahead_ref[...]
        south[...] = back_ref[...]

    down = iota((S, S), 0)
    across = iota((S, S), 1)
    turned = ((down + across == COLS - 1) | (down + across == COLS - 1 + S)).astype(F32)
    straight = (down == across).astype(F32)
    turn = jnp.where(fold, turned, straight).astype(BF)
    for i in range(3):
        north[i] = jnp.dot(turn, north[i], preferred_element_type=F32).astype(BF)

    low = iota((16, C), 0) < 8
    nothing = jnp.zeros((16, C), BF)

    def lay(dest, base, rows, first):
        n = len(rows)
        tails = [nothing] + [r[COLS:S, :] for r in rows] + [nothing]
        for k in range(-1, n):
            at = base + (first + k) * S
            if k >= 0:
                dest[at : at + COLS, :] = rows[k][0:COLS, :]
            joined = jnp.where(low, tails[k + 1].astype(F32), tails[k + 2].astype(F32))
            dest[at + COLS : at + S, :] = joined.astype(BF)

    x_rows = [south.at[1], south.at[0]] + [xrow_ref.at[r] for r in range(ROWS)]
    x_rows += [north.at[0], north.at[1]]
    xe[0:LEAD, :] = jnp.zeros((LEAD, C), BF)
    xe[LEAD + 20 * S :, :] = jnp.zeros((xe.shape[0] - LEAD - 20 * S, C), BF)
    lay(xe, LEAD, x_rows, 0)
    c_rows = [south.at[2]] + [crow_ref.at[r] for r in range(ROWS)] + [north.at[2]]
    ce[0:S, :] = jnp.zeros((S, C), BF)
    lay(ce, 0, c_rows, 1)

    def weight(r, c):
        return kernel_ref[3 * r + c]

    def far_weight(r, c):
        return kernel_ref[jnp.where(fold, 8 - (3 * r + c), 3 * r + c)]

    def taps(ref, base, at, size, c, weights, sign, contract):
        total = None
        for r in range(3):
            start = base + at + sign * (r - 1) * S
            term = lax.dot_general(
                ref[start : start + size, :], weights[r](r, c),
                (((1,), (contract,)), ((), ())), preferred_element_type=F32,
            )
            total = term if total is None else total + term
        return total

    for c in range(3):
        plain = [weight] * 3
        for k in range(3):
            ys[c, 8 + k * 480 : 8 + (k + 1) * 480, :] = taps(xe, LEAD, k * 480, 480, c, plain, 1, 0)
        edge = taps(xe, LEAD, 18 * S - 16, 96, c, [far_weight] * 3, 1, 0)
        ys[c, 8 + 18 * S - 8 : 8 + 19 * S, :] = edge[8:]
        ys[c, 0:8, :] = jnp.zeros((8, C), F32)
        ys[c, 8 + 19 * S : 16 + 19 * S, :] = jnp.zeros((8, C), F32)
    go[...] = jnp.zeros_like(go)
    for w in range(19):
        at = 8 + w * S
        pre = ys[0, at - 1 : at - 1 + S, :] + ys[1, at : at + S, :] + ys[2, at + 1 : at + 1 + S, :]
        s = jax.nn.sigmoid(pre)
        slope = s * (1.0 + pre * (1.0 - s))
        grad = (ce[w * S : w * S + S, :].astype(F32) * slope).astype(BF)
        ga[w * S : w * S + S, :] = grad
        if 2 <= w < 18:
            r = w - 2
            go[at : at + COLS, :] = grad[0:COLS].astype(F32)
            kept = keep_t[:, r : r + 1]
            out_ref[0, r] = (kept * pre[0:COLS] * s[0:COLS]).astype(BF)

    lo, span = 128, 1408
    for r in range(3):
        start = LEAD + lo + (r - 1) * S
        xt[r * C : (r + 1) * C, :] = xe[start : start + span, :].T
    tails = []
    for c in range(3):
        start = 8 + lo - (c - 1)
        moved = go[start : start + span, :].astype(BF)
        grad = jnp.dot(xt[...], moved, preferred_element_type=F32)
        wgrad_ref[c * 576 : (c + 1) * 576, :] = grad[:, 0:128].astype(BF)
        tails.append(grad[:, 128:C])
    wgrad_ref[1728:2304, :] = jnp.concatenate(tails[0:2], axis=1).astype(BF)
    wgrad_ref[2304:2592, :] = jnp.concatenate([tails[2][0:288], tails[2][288:576]], axis=1).astype(BF)
    if wgrad_ref.shape[0] > PACKED:
        wgrad_ref[PACKED:, :] = jnp.zeros((wgrad_ref.shape[0] - PACKED, 128), BF)

    for c in range(3):
        for k in range(4):
            at = S + k * 320
            ys[c, 8 + at : 8 + at + 320, :] = taps(ga, 0, at, 320, c, [weight] * 3, -1, 1)
        edge = taps(ga, 0, 17 * S - 16, 96, c, [far_weight, weight, weight], -1, 1)
        ys[c, 8 + 17 * S - 8 : 8 + 18 * S, :] = edge[8:]
    for r in range(ROWS):
        at = 8 + (r + 2) * S
        total = (
            ys[0, at + 1 : at + 1 + COLS, :]
            + ys[1, at : at + COLS, :]
            + ys[2, at - 1 : at - 1 + COLS, :]
        )
        sgrad_ref[0, r] = jnp.where(keep_t[:, r : r + 1] > 0, total, 0.0).astype(BF)


def sum_kernel(parts_ref, out_ref):
    total = parts_ref[0].astype(F32)
    for i in range(1, parts_ref.shape[0]):
        total = total + parts_ref[i].astype(F32)
    total = total.astype(BF)
    for i in range(out_ref.shape[0]):
        out_ref[i] = total


def unpack_kernel(scale, packed_ref, out_ref):
    for c in range(3):
        for r in range(3):
            at = c * 576 + r * C
            out_ref[r, c, :, 0:128] = packed_ref[at : at + C, :].astype(F32) * scale
    for r in range(3):
        both = packed_ref[1728 + r * C : 1728 + (r + 1) * C, :].astype(F32) * scale
        out_ref[r, 0, :, 128:C] = both[:, 0:64]
        out_ref[r, 1, :, 128:C] = both[:, 64:128]
    last = packed_ref[2304:2592, :].astype(F32) * scale
    out_ref[0, 2, :, 128:C] = last[0:192, 0:64]
    out_ref[1, 2, 0:96, 128:C] = last[192:288, 0:64]
    out_ref[1, 2, 96:192, 128:C] = last[0:96, 64:128]
    out_ref[2, 2, :, 128:C] = last[96:288, 64:128]


def solution(mesh):
    lon_count, lat_count, dp_count = (mesh.shape[n] for n in ("lon", "lat", "dp"))
    z_count = lon_count // 2
    fine = Mesh(
        mesh.devices.reshape(z_count, 2, lat_count, dp_count), ("z", "core", "lat", "dp")
    )
    lon = ("z", "core")
    plane = ("core", "lat", "dp")
    plane_count = 2 * lat_count * dp_count
    half = lon_count // 2
    eastward = [(i, (i + 1) % lon_count) for i in range(lon_count)]
    westward = [(b, a) for a, b in eastward]
    ahead_pairs = []
    for b in range(half):
        line = [(b, a) for a in range(lat_count)]
        line += [(lon_count - 1 - b, a) for a in reversed(range(lat_count))]
        number = [column * lat_count + a for column, a in line]
        ahead_pairs += list(zip(number[:-1], number[1:]))
    back_pairs = [(b, a) for a, b in ahead_pairs]
    scale = 1.0 / math.sqrt(dp_count * lat_count * ROWS * lon_count * COLS)
    part = -(-PACKED // (8 * plane_count)) * 8
    packed_rows = plane_count * part
    smem = pl.BlockSpec(memory_space=pltpu.SMEM)
    vmem = pl.BlockSpec(memory_space=pltpu.VMEM)

    def shaped(shape, kind=BF):
        return jax.ShapeDtypeStruct(shape, kind)

    def body(states, cotangent, kernel, land_mask, ocean_tiles):
        lon_at = lax.axis_index("z") * 2 + lax.axis_index("core")
        lat_at = lax.axis_index("lat")
        place = jnp.stack([lon_at < half, lat_at == lat_count - 1]).astype(jnp.int32)
        east, west = pl.pallas_call(
            edge_kernel,
            out_shape=(shaped((3, ROWS, C)), shaped((3, ROWS, C))),
            in_specs=[vmem, vmem, vmem, smem],
            out_specs=(vmem, vmem),
            name="edges",
        )(states, cotangent, land_mask, ocean_tiles)
        from_west = lax.ppermute(east, lon, eastward)
        from_east = lax.ppermute(west, lon, westward)
        xrow, crow, ahead, back = pl.pallas_call(
            rows_kernel,
            out_shape=(
                shaped((ROWS, S, C)), shaped((ROWS, S, C)), shaped((3, S, C)), shaped((3, S, C)),
            ),
            in_specs=[vmem, vmem, vmem, smem, vmem, vmem, smem],
            out_specs=(vmem,) * 4,
            name="rows",
        )(states, cotangent, land_mask, ocean_tiles, from_west, from_east, place)
        ahead = lax.ppermute(ahead, lon + ("lat",), ahead_pairs)
        back = lax.ppermute(back, lon + ("lat",), back_pairs)
        output, state_grad, packed = pl.pallas_call(
            main_kernel,
            out_shape=(
                shaped((1, ROWS, COLS, C)), shaped((1, ROWS, COLS, C)), shaped((packed_rows, 128)),
            ),
            in_specs=[vmem] * 6 + [smem, smem],
            out_specs=(vmem,) * 3,
            scratch_shapes=[
                pltpu.VMEM((LEAD + 20 * S + 32, C), BF),
                pltpu.VMEM((19 * S, C), BF),
                pltpu.VMEM((19 * S, C), BF),
                pltpu.VMEM((8 + 1536 + 16, C), F32),
                pltpu.VMEM((3, 19 * S + 16, C), F32),
                pltpu.VMEM((576, 1408), BF),
                pltpu.VMEM((3, S, C), BF),
                pltpu.VMEM((3, S, C), BF),
            ],
            compiler_params=params(40),
            name="main",
        )(xrow, crow, ahead, back, kernel.reshape(9, C, C), land_mask, ocean_tiles, place)

        def summed(parts, copies):
            return pl.pallas_call(
                sum_kernel,
                out_shape=shaped((copies, part, 128)),
                in_specs=[vmem],
                out_specs=vmem,
                name="sum",
            )(parts)

        parts = lax.all_to_all(packed.reshape(plane_count, part, 128), plane, 0, 0, tiled=True)
        parts = lax.all_to_all(summed(parts, z_count), "z", 0, 0, tiled=True)
        parts = lax.all_to_all(summed(parts, plane_count), plane, 0, 0, tiled=True)
        weight_grad = pl.pallas_call(
            lambda *refs: unpack_kernel(scale, *refs),
            out_shape=shaped((3, 3, C, C), F32),
            in_specs=[vmem],
            out_specs=vmem,
            name="unpack",
        )(parts.reshape(packed_rows, 128))
        return output, state_grad, weight_grad

    cells = P("dp", "lat", lon, None)
    return jax.shard_map(
        body,
        mesh=fine,
        in_specs=(cells, cells, P(), P("lat", lon), P("lat", lon, None)),
        out_specs=(cells, cells, P()),
        check_vma=False,
    )
```

```python
import math

import jax
import jax.numpy as jnp
from jax import lax
from jax.experimental import pallas as pl
from jax.experimental.pallas import tpu as pltpu
from jax.sharding import Mesh
from jax.sharding import PartitionSpec as P

BF = jnp.bfloat16
F32 = jnp.float32
TS = 16
ROWS = 16
COLS = 64
C = 192
S = 80
LEAD = 32
LINE = 72
HALF = 1296


def iota(shape, dim):
    return lax.broadcasted_iota(jnp.int32, shape, dim)


def keep_plane(mask_ref, tiles_ref):
    tile = iota((ROWS, COLS), 1) // TS
    listed = jnp.zeros((ROWS, COLS), F32)
    for slot in range(tiles_ref.shape[-1]):
        listed = jnp.where(tile == tiles_ref[0, 0, slot], 1.0, listed)
    return jnp.where(mask_ref[...] > 0, listed, 0.0)


def fetch(copies):
    started = [pltpu.make_async_copy(*copy) for copy in copies]
    for copy in started:
        copy.start()
    for copy in started:
        copy.wait()


def edge_kernel(
    states_ref, cot_ref, mask_hbm, tiles_hbm, east_ref, west_ref, x_ref, c_ref, keep_ref,
    mask_ref, tiles_ref, sems,
):
    fetch([
        (mask_hbm, mask_ref, sems.at[0]),
        (tiles_hbm, tiles_ref, sems.at[1]),
        (states_ref.at[0], x_ref, sems.at[2]),
        (cot_ref.at[0], c_ref, sems.at[3]),
    ])
    keep = keep_plane(mask_ref, tiles_ref)
    keep_t = keep.T
    keep_ref[...] = keep_t
    for r in range(ROWS):
        x_ref[r] = keep_cells(x_ref[r], keep_t[:, r : r + 1])
        c_ref[r] = keep_cells(c_ref[r], keep_t[:, r : r + 1])
    first, last = slice(0, 16), slice(COLS - 16, COLS)

    def column(ref, part, spot):
        cells = jnp.concatenate([ref[r, part, :] for r in range(ROWS)], axis=0)
        pick = iota((ROWS, 256), 1) == iota((ROWS, 256), 0) * 16 + spot
        picked = jnp.dot(pick.astype(F32).astype(BF), cells, preferred_element_type=F32)
        return picked.astype(BF)

    east_ref[0] = column(x_ref, last, 14)
    east_ref[1] = column(x_ref, last, 15)
    east_ref[2] = column(c_ref, last, 15)
    west_ref[0] = column(x_ref, first, 0)
    west_ref[1] = column(x_ref, first, 1)
    west_ref[2] = column(c_ref, first, 0)


def halo_chunks(from_west, from_east, size):
    halo = jnp.concatenate(
        [from_west[i] for i in range(3)] + [from_east[i] for i in range(3)], axis=0
    )
    shape = (ROWS * size, 96)
    row = iota(shape, 0) // size
    spot = iota(shape, 0) % size
    source = iota(shape, 1)

    def chunk(at):
        want = jnp.full(shape, -1, jnp.int32)
        for where, plane in at:
            want = jnp.where(spot == where, plane * 16 + row, want)
        pick = (source == want).astype(F32).astype(BF)
        picked = jnp.dot(pick, halo, preferred_element_type=F32)
        return [picked[r * size : r * size + size] for r in range(ROWS)]

    return (
        chunk([(0, 3), (1, 4), (size - 2, 0), (size - 1, 1)]),
        chunk([(0, 5), (size - 1, 2)]),
    )


def keep_cells(cells, column):
    return jnp.where(column > 0, cells.astype(F32), 0.0).astype(BF)


def line_kernel(x_ref, c_ref, from_west, from_east, fold_ref, pair_ref):
    x_chunk, c_chunk = halo_chunks(from_west, from_east, 8)
    even = lax.axis_index("lat") % 2 == 0

    def full(ref, r, chunk):
        return jnp.concatenate([ref[r].astype(F32), chunk[r]], axis=0)

    def pack(one, two, three):
        rest = jnp.concatenate([one[:, 128:], two[:, 128:]], axis=1)
        last = jnp.concatenate([three[:, 128:], jnp.zeros((LINE, 64), F32)], axis=1)
        return one[:, :128], two[:, :128], three[:, :128], rest, last

    top = pack(full(x_ref, 15, x_chunk), full(x_ref, 14, x_chunk), full(c_ref, 15, c_chunk))
    bottom = pack(full(x_ref, 0, x_chunk), full(x_ref, 1, x_chunk), full(c_ref, 0, c_chunk))
    for i in range(5):
        fold_ref[i] = jnp.where(even, bottom[i], top[i]).astype(BF)
        pair_ref[i] = jnp.where(even, top[i], bottom[i]).astype(BF)


def lay(dest, base, rows):
    low = iota((16, C), 0) < 8
    none = jnp.zeros((16, C), F32)
    tails = [none] + [none if r is None else r[1].astype(F32) for r in rows] + [none]
    for k in range(-1, len(rows)):
        at = base + k * S
        if k >= 0:
            dest[at : at + COLS, :] = jnp.zeros((COLS, C), BF) if rows[k] is None else rows[k][0]
        dest[at + COLS : at + S, :] = jnp.where(low, tails[k + 1], tails[k + 2]).astype(BF)


def window(ref):
    return ref[0:COLS, :], ref[COLS:S, :]


def taps(ref, base, at, size, c, weights, sign, contract):
    total = None
    for r in range(3):
        start = base + at + sign * (r - 1) * S
        term = lax.dot_general(
            ref[start : start + size, :], weights[r](r, c),
            (((1,), (contract,)), ((), ())), preferred_element_type=F32,
        )
        total = term if total is None else total + term
    return total


def shifted(ys, at, size, sign):
    at = at + 8
    return (
        ys[0, at - sign : at - sign + size, :]
        + ys[1, at : at + size, :]
        + ys[2, at + sign : at + sign + size, :]
    )


def weight_sums(xe, base, go, xt, lo, span, emit):
    for r in range(3):
        start = base + lo + (r - 1) * S
        xt[r * C : (r + 1) * C, :] = xe[start : start + span, :].T
    for c in range(3):
        start = 8 + lo - (c - 1)
        moved = go[start : start + span, :].astype(BF)
        emit(c, jnp.dot(xt[...], moved, preferred_element_type=F32))


def inner_kernel(
    x_ref, c_ref, kernel_ref, keep_ref, from_west, from_east,
    out_ref, sgrad_ref, part_ref, gedge_ref,
    xe, ce, ga, go, ys, xt,
):
    keep_t = keep_ref[...]
    x_chunk, c_chunk = halo_chunks(from_west, from_east, 16)

    def own(ref, chunk):
        return [(ref[r], chunk[r]) for r in range(ROWS)]

    xe[0:LEAD, :] = jnp.zeros((LEAD, C), BF)
    xe[LEAD + ROWS * S :, :] = jnp.zeros((xe.shape[0] - LEAD - ROWS * S, C), BF)
    lay(xe, LEAD, own(x_ref, x_chunk))
    lay(ce, LEAD, own(c_ref, c_chunk))

    def weight(r, c):
        return kernel_ref[3 * r + c]

    plain = [weight] * 3
    for c in range(3):
        for k in range(3):
            at = 48 + k * 384
            ys[c, 8 + at : 8 + at + 384, :] = taps(xe, LEAD, at, 384, c, plain, 1, 0)
        ys[c, 1208:1216, :] = jnp.zeros((8, C), F32)
    go[...] = jnp.zeros_like(go)
    ga[0:64, :] = jnp.zeros((64, C), BF)
    for w in range(15):
        at, size = (w * S, S) if w else (64, 16)
        pre = shifted(ys, at, size, 1)
        s = jax.nn.sigmoid(pre)
        slope = s * (1.0 + pre * (1.0 - s))
        grad = (ce[LEAD + at : LEAD + at + size, :].astype(F32) * slope).astype(BF)
        ga[at : at + size, :] = grad
        if w:
            go[8 + at : 8 + at + COLS, :] = grad[0:COLS].astype(F32)
            kept = keep_t[:, w : w + 1]
            out_ref[0, w] = (kept * pre[0:COLS] * s[0:COLS]).astype(BF)
    low = iota((16, C), 0) < 8
    for i, r in enumerate((1, 2, 13, 14)):
        gedge_ref[i, 0:COLS, :] = ga[r * S : r * S + COLS, :]
        east = ga[r * S + COLS : r * S + S, :].astype(F32)
        west = ga[(r - 1) * S + COLS : r * S, :].astype(F32)
        gedge_ref[i, COLS:S, :] = jnp.where(low, east, west).astype(BF)

    def emit(c, grad):
        part_ref[c] = grad

    weight_sums(xe, LEAD, go, xt, 64, 1152, emit)
    for c in range(3):
        for k in range(3):
            at = 112 + k * 336
            ys[c, 8 + at : 8 + at + 336, :] = taps(ga, 0, at, 336, c, plain, -1, 1)
    for r in range(2, 14):
        total = shifted(ys, r * S, COLS, -1)
        sgrad_ref[0, r] = keep_cells(total, keep_t[:, r : r + 1])
    for r in (0, 15):
        out_ref[0, r] = jnp.zeros((COLS, C), BF)
    for r in (0, 1, 14, 15):
        sgrad_ref[0, r] = jnp.zeros((COLS, C), BF)


def far_of(kernel_ref, fold):
    def far_weight(r, c):
        return kernel_ref[jnp.where(fold, 8 - (3 * r + c), 3 * r + c)]

    return far_weight


def border_rows(fold, fold_ref, pair_ref, own_fold, own_pair):
    even = lax.axis_index("lat") % 2 == 0
    down = iota((LINE, LINE), 0)
    across = iota((LINE, LINE), 1)
    turned = ((down + across == COLS - 1) | (down + across == COLS - 1 + LINE)).astype(F32)
    straight = (down == across).astype(F32)
    turn = jnp.where(fold, turned, straight).astype(BF)

    def choose(a, b):
        return [jnp.where(even, a[i].astype(F32), b[i].astype(F32)) for i in range(5)]

    def split(blocks):
        one, two, three, rest, last = blocks
        rows = (
            jnp.concatenate([one, rest[:, 0:64]], axis=1),
            jnp.concatenate([two, rest[:, 64:128]], axis=1),
            jnp.concatenate([three, last[:, 0:64]], axis=1),
        )
        return [
            (r[0:COLS].astype(BF), jnp.concatenate([r[COLS:LINE], r[COLS:LINE]], axis=0))
            for r in rows
        ]

    south = split(choose(fold_ref, pair_ref))
    north = split([
        jnp.dot(turn, v.astype(BF), preferred_element_type=F32) for v in choose(pair_ref, fold_ref)
    ])
    top = split(choose(own_pair, own_fold))
    bottom = split(choose(own_fold, own_pair))
    return south, bottom, top, north


def slope_at(ys, at, size):
    pre = shifted(ys, at, size, 1)
    s = jax.nn.sigmoid(pre)
    return pre, s, s * (1.0 + pre * (1.0 - s))


def row_of(ga, slot, dest):
    low = iota((16, C), 0) < 8
    dest[0:COLS, :] = ga[slot * S : slot * S + COLS, :]
    east = ga[slot * S + COLS : slot * S + S, :].astype(F32)
    west = ga[(slot - 1) * S + COLS : slot * S, :].astype(F32)
    dest[COLS:S, :] = jnp.where(low, east, west).astype(BF)


def border_kernel(
    lat_count,
    fold_ref, pair_ref, own_fold, own_pair, kernel_ref, keep_ref, part_ref, out_in,
    out_ref, gown_ref, give_ref, hold_ref,
    xb, cb, ga, go, ys, xt, packed, edge_out, sems,
):
    del out_in
    core = lax.axis_index("core")
    fold = lax.axis_index("lat") == lat_count - 1
    keep_t = keep_ref[...]
    south, bottom, top, north = border_rows(fold, fold_ref, pair_ref, own_fold, own_pair)
    xb[0:S, :] = jnp.zeros((S, C), BF)
    xb[7 * S :, :] = jnp.zeros((xb.shape[0] - 7 * S, C), BF)
    lay(xb, S, [south[0], bottom[0], bottom[1], top[1], top[0], north[0]])
    lay(cb, S, [None, bottom[2], None, None, top[2], None])

    def weight(r, c):
        return kernel_ref[3 * r + c]

    for c in range(3):
        ys[c, 8 + 144 : 8 + 480, :] = taps(xb, 0, 144, 336, c, [weight] * 3, 1, 0)
        ys[c, 144:152, :] = jnp.zeros((8, C), F32)
        ys[c, 488:496, :] = jnp.zeros((8, C), F32)
    go[...] = jnp.zeros_like(go)
    for slot in (1, 2, 4, 5):
        at, size = (slot * S + COLS, 16) if slot in (1, 4) else (slot * S, S)
        pre, s, slope = slope_at(ys, at, size)
        grad = (cb[at : at + size, :].astype(F32) * slope).astype(BF)
        ga[at : at + size, :] = grad
        if slot in (2, 5):
            go[8 + at : 8 + at + COLS, :] = grad[0:COLS].astype(F32)
            r = 0 if slot == 2 else ROWS - 1
            kept = keep_t[:, r : r + 1]
            edge_out[slot // 5] = (kept * pre[0:COLS] * s[0:COLS]).astype(BF)
    copies = [
        pltpu.make_async_copy(edge_out.at[i], out_ref.at[0, r], sems.at[i])
        for i, r in enumerate((0, ROWS - 1))
    ]
    for copy in copies:
        copy.start()
    row_of(ga, 2, gown_ref.at[0])
    row_of(ga, 5, gown_ref.at[1])

    tails = []

    def emit(c, grad):
        grad = grad + part_ref[c]
        where = ((0, 0), (0, 576), (1, 0))[c]
        packed[where[0], where[1] : where[1] + 576, :] = grad[:, 0:128]
        tails.append(grad[:, 128:C])

    weight_sums(xb, 0, go, xt, 144, 384, emit)
    packed[1, 576:1152, :] = jnp.concatenate(tails[0:2], axis=1)
    rest = jnp.concatenate([tails[2][0:288], tails[2][288:576]], axis=1)
    packed[0, 1152:HALF, :] = rest[0:144]
    packed[1, 1152:HALF, :] = rest[144:288]
    for i in range(2):
        if packed.shape[1] > HALF:
            packed[i, HALF:, :] = jnp.zeros((packed.shape[1] - HALF, 128), F32)
    give_ref[...] = packed[1 - core].astype(BF)
    hold_ref[...] = packed[core]
    for copy in copies:
        copy.wait()


def ghost_kernel(
    lat_count, fold_ref, pair_ref, own_fold, own_pair, kernel_ref, ghost_ref, xb, cb, ga, ys,
):
    fold = lax.axis_index("lat") == lat_count - 1
    south, bottom, top, north = border_rows(fold, fold_ref, pair_ref, own_fold, own_pair)
    xb[0:S, :] = jnp.zeros((S, C), BF)
    xb[7 * S :, :] = jnp.zeros((xb.shape[0] - 7 * S, C), BF)
    lay(xb, S, [south[1], south[0], bottom[0], top[0], north[0], north[1]])
    lay(cb, S, [None, south[2], None, None, north[2], None])

    def weight(r, c):
        return kernel_ref[3 * r + c]

    far_weight = far_of(kernel_ref, fold)
    for c in range(3):
        ys[c, 152:248, :] = taps(xb, 0, 144, 96, c, [weight] * 3, 1, 0)
        ys[c, 392:488, :] = taps(xb, 0, 384, 96, c, [far_weight] * 3, 1, 0)
        for at in (144, 248, 384, 488):
            ys[c, at : at + 8, :] = jnp.zeros((8, C), F32)
    for at in (144, 384):
        grad = cb[at : at + 96, :].astype(F32) * slope_at(ys, at, 96)[2]
        ga[at : at + 96, :] = grad.astype(BF)
    row_of(ga, 2, ghost_ref.at[0])
    row_of(ga, 5, ghost_ref.at[1])


def state_kernel(
    lat_count, gedge_ref, gown_ref, ghost_ref, kernel_ref, keep_ref, sgrad_in,
    sgrad_ref, gb, ys, edge_out, sems,
):
    del sgrad_in
    fold = lax.axis_index("lat") == lat_count - 1
    keep_t = keep_ref[...]
    gb[0:S, :] = jnp.zeros((S, C), BF)
    gb[9 * S :, :] = jnp.zeros((gb.shape[0] - 9 * S, C), BF)
    lay(
        gb, S,
        [window(ref.at[i]) for ref, i in (
            (ghost_ref, 0), (gown_ref, 0), (gedge_ref, 0), (gedge_ref, 1),
            (gedge_ref, 2), (gedge_ref, 3), (gown_ref, 1), (ghost_ref, 1),
        )],
    )

    def weight(r, c):
        return kernel_ref[3 * r + c]

    for c in range(3):
        ys[c, 8 + 144 : 8 + 640, :] = taps(gb, 0, 144, 496, c, [weight] * 3, -1, 1)
        edge = taps(gb, 0, 7 * S - 16, 96, c, [far_of(kernel_ref, fold), weight, weight], -1, 1)
        ys[c, 7 * S : 8 + 8 * S, :] = edge[8:]
    copies = []
    for i, (slot, r) in enumerate(((2, 0), (3, 1), (6, 14), (7, 15))):
        total = shifted(ys, slot * S, COLS, -1)
        edge_out[i] = keep_cells(total, keep_t[:, r : r + 1])
        copies.append(pltpu.make_async_copy(edge_out.at[i], sgrad_ref.at[0, r], sems.at[i]))
        copies[-1].start()
    for copy in copies:
        copy.wait()


def add_kernel(hold_ref, came_ref, ghost_ref, out_ref):
    del ghost_ref
    out_ref[...] = (hold_ref[...] + came_ref[...].astype(F32)).astype(BF)


def sum_kernel(parts_ref, out_ref):
    total = parts_ref[0].astype(F32)
    for i in range(1, parts_ref.shape[0]):
        total = total + parts_ref[i].astype(F32)
    total = total.astype(BF)
    for i in range(out_ref.shape[0]):
        out_ref[i] = total


def unpack_kernel(scale, mine_ref, other_ref, out_ref):
    mine_first = lax.axis_index("core") == 0

    def get(half, at, size):
        a = mine_ref[at : at + size, :].astype(F32)
        b = other_ref[at : at + size, :].astype(F32)
        return jnp.where(mine_first == (half == 0), a, b) * scale

    for c, (half, base) in enumerate(((0, 0), (0, 576), (1, 0))):
        for r in range(3):
            out_ref[r, c, :, 0:128] = get(half, base + r * C, C)
    for r in range(3):
        both = get(1, 576 + r * C, C)
        out_ref[r, 0, :, 128:C] = both[:, 0:64]
        out_ref[r, 1, :, 128:C] = both[:, 64:128]
    one, two = get(0, 1152, 144), get(1, 1152, 144)
    out_ref[0, 2, 0:144, 128:C] = one[:, 0:64]
    out_ref[0, 2, 144:192, 128:C] = two[0:48, 0:64]
    out_ref[1, 2, 0:96, 128:C] = two[48:144, 0:64]
    out_ref[1, 2, 96:192, 128:C] = one[0:96, 64:128]
    out_ref[2, 2, 0:48, 128:C] = one[96:144, 64:128]
    out_ref[2, 2, 48:192, 128:C] = two[:, 64:128]


def solution(mesh):
    lon_count, lat_count, dp_count = (mesh.shape[n] for n in ("lon", "lat", "dp"))
    z_count = lon_count // 2
    fine = Mesh(
        mesh.devices.reshape(z_count, 2, lat_count, dp_count), ("z", "core", "lat", "dp")
    )
    lon = ("z", "core")
    sheet = ("lat", "dp")
    sheet_count = lat_count * dp_count
    eastward = [(i, (i + 1) % lon_count) for i in range(lon_count)]
    westward = [(b, a) for a, b in eastward]
    lat_pairs, fold_pairs = [], []
    for b in range(lon_count):
        for a in range(lat_count):
            lat_pairs.append((b * lat_count + a, b * lat_count + (a ^ 1)))
            if a == lat_count - 1:
                fold_pairs.append((b * lat_count + a, (lon_count - 1 - b) * lat_count + a))
            elif a > 0:
                fold_pairs.append((b * lat_count + a, b * lat_count + (a + 1 if a % 2 else a - 1)))
    scale = 1.0 / math.sqrt(dp_count * lat_count * ROWS * lon_count * COLS)
    part = -(-HALF // (8 * sheet_count)) * 8
    half_rows = sheet_count * part
    smem = pl.BlockSpec(memory_space=pltpu.SMEM)
    vmem = pl.BlockSpec(memory_space=pltpu.VMEM)
    hbm = pl.BlockSpec(memory_space=pltpu.HBM)
    whole = jax.ShapeDtypeStruct((1, ROWS, COLS, C), BF)

    def shaped(shape, kind=BF):
        return jax.ShapeDtypeStruct(shape, kind)

    def call(kernel, name, ins, out_shape, outs, scratch=(), aliases=None, cost=0):
        return pl.pallas_call(
            kernel,
            out_shape=out_shape,
            in_specs=ins,
            out_specs=outs,
            scratch_shapes=list(scratch),
            input_output_aliases=aliases or {},
            compiler_params=pltpu.CompilerParams(vmem_limit_bytes=40 * 2**20),
            cost_estimate=pl.CostEstimate(
                flops=cost, bytes_accessed=2**20, transcendentals=0
            ) if cost else None,
            name=name,
        )

    def body(states, cotangent, kernel, land_mask, ocean_tiles):
        taps9 = kernel.reshape(9, C, C)
        cells = shaped((ROWS, COLS, C))
        east, west, x, c, keep = call(
            edge_kernel, "edges", [hbm] * 4,
            (shaped((3, ROWS, C)),) * 2 + (cells, cells, shaped((COLS, ROWS), F32)), (vmem,) * 5,
            scratch=[
                pltpu.VMEM((ROWS, COLS), jnp.int32),
                pltpu.SMEM(ocean_tiles.shape, jnp.int32),
                pltpu.SemaphoreType.DMA((4,)),
            ],
        )(*(pltpu.with_memory_space_constraint(v, pltpu.HBM)
            for v in (states, cotangent, land_mask, ocean_tiles)))
        from_west = lax.ppermute(east, lon, eastward)
        from_east = lax.ppermute(west, lon, westward)
        own_fold, own_pair = call(
            line_kernel, "lines", [vmem] * 4, (shaped((5, LINE, 128)),) * 2, (vmem,) * 2,
        )(x, c, from_west, from_east)
        pair = lax.ppermute(own_pair, lon + ("lat",), lat_pairs)
        fold = lax.ppermute(own_fold, lon + ("lat",), fold_pairs)
        output, state_grad, sums, gedge = call(
            inner_kernel, "inner", [vmem] * 6,
            (whole, whole, shaped((3, 576, C), F32), shaped((4, S, C))), (vmem,) * 4,
            scratch=[
                pltpu.VMEM((LEAD + ROWS * S + 32, C), BF),
                pltpu.VMEM((LEAD + ROWS * S, C), BF),
                pltpu.VMEM((15 * S, C), BF),
                pltpu.VMEM((8 + ROWS * S + 16, C), F32),
                pltpu.VMEM((3, ROWS * S + 16, C), F32),
                pltpu.VMEM((576, 1152), BF),
            ],
            cost=2 * 10**9,
        )(x, c, taps9, keep, from_west, from_east)
        lines = (fold, pair, own_fold, own_pair)
        output, gown, give, hold = call(
            lambda *refs: border_kernel(lat_count, *refs), "border", [vmem] * 7 + [hbm],
            (whole, shaped((2, S, C)), shaped((half_rows, 128)), shaped((half_rows, 128), F32)),
            (hbm, vmem, vmem, vmem),
            scratch=[
                pltpu.VMEM((8 * S, C), BF),
                pltpu.VMEM((7 * S, C), BF),
                pltpu.VMEM((7 * S, C), BF),
                pltpu.VMEM((7 * S, C), F32),
                pltpu.VMEM((3, 7 * S + 16, C), F32),
                pltpu.VMEM((576, 384), BF),
                pltpu.VMEM((2, half_rows, 128), F32),
                pltpu.VMEM((2, COLS, C), BF),
                pltpu.SemaphoreType.DMA((2,)),
            ],
            aliases={7: 0}, cost=5 * 10**8,
        )(*lines, taps9, keep, sums, output)
        came = lax.ppermute(give, "core", [(0, 1), (1, 0)])
        ghost = call(
            lambda *refs: ghost_kernel(lat_count, *refs), "ghost", [vmem] * 5,
            shaped((2, S, C)), vmem,
            scratch=[
                pltpu.VMEM((8 * S, C), BF),
                pltpu.VMEM((7 * S, C), BF),
                pltpu.VMEM((7 * S, C), BF),
                pltpu.VMEM((3, 7 * S + 16, C), F32),
            ],
            cost=5 * 10**8,
        )(*lines, taps9)
        state_grad = call(
            lambda *refs: state_kernel(lat_count, *refs), "state", [vmem] * 5 + [hbm], whole, hbm,
            scratch=[
                pltpu.VMEM((10 * S, C), BF),
                pltpu.VMEM((3, 8 * S + 16, C), F32),
                pltpu.VMEM((4, COLS, C), BF),
                pltpu.SemaphoreType.DMA((4,)),
            ],
            aliases={5: 0}, cost=5 * 10**8,
        )(gedge, gown, ghost, taps9, keep, state_grad)

        def summed(parts, copies):
            return call(sum_kernel, "sum", [vmem], shaped((copies, part, 128)), vmem)(parts)

        parts = call(add_kernel, "add", [vmem] * 2 + [hbm], shaped((half_rows, 128)), vmem)(hold, came, ghost)
        parts = lax.all_to_all(parts.reshape(sheet_count, part, 128), sheet, 0, 0, tiled=True)
        parts = lax.all_to_all(summed(parts, z_count), "z", 0, 0, tiled=True)
        parts = lax.all_to_all(summed(parts, sheet_count), sheet, 0, 0, tiled=True)
        mine = parts.reshape(half_rows, 128)
        other = lax.ppermute(mine, "core", [(0, 1), (1, 0)])
        weight_grad = call(
            lambda *refs: unpack_kernel(scale, *refs), "unpack", [vmem] * 2,
            shaped((3, 3, C, C), F32), vmem,
        )(mine, other)
        return output, state_grad, weight_grad

    cells = P("dp", "lat", lon, None)
    return jax.shard_map(
        body,
        mesh=fine,
        in_specs=(cells, cells, P(), P("lat", lon), P("lat", lon, None)),
        out_specs=(cells, cells, P()),
        check_vma=False,
    )
```

```python
import math

import jax
import jax.numpy as jnp
from jax import lax
from jax.experimental import pallas as pl
from jax.experimental.pallas import tpu as pltpu
from jax.sharding import Mesh
from jax.sharding import PartitionSpec as P

BF = jnp.bfloat16
F32 = jnp.float32
TS = 16
ROWS = 16
COLS = 64
C = 192
S = 80
LEAD = 32
LINE = 72
HALF = 1296


def iota(shape, dim):
    return lax.broadcasted_iota(jnp.int32, shape, dim)


def keep_plane(mask_ref, tiles_ref):
    tile = iota((ROWS, COLS), 1) // TS
    listed = jnp.zeros((ROWS, COLS), F32)
    for slot in range(tiles_ref.shape[-1]):
        listed = jnp.where(tile == tiles_ref[0, 0, slot], 1.0, listed)
    return jnp.where(mask_ref[...] > 0, listed, 0.0)


def fetch(copies):
    started = [pltpu.make_async_copy(*copy) for copy in copies]
    for copy in started:
        copy.start()
    for copy in started:
        copy.wait()


def edge_kernel(
    states_ref, cot_ref, mask_hbm, tiles_hbm, east_ref, west_ref, x_ref, c_ref, keep_ref,
    mask_ref, tiles_ref, sems,
):
    fetch([
        (mask_hbm, mask_ref, sems.at[0]),
        (tiles_hbm, tiles_ref, sems.at[1]),
        (states_ref.at[0], x_ref, sems.at[2]),
        (cot_ref.at[0], c_ref, sems.at[3]),
    ])
    keep = keep_plane(mask_ref, tiles_ref)
    keep_t = keep.T
    keep_ref[...] = keep_t
    for r in range(ROWS):
        x_ref[r] = keep_cells(x_ref[r], keep_t[:, r : r + 1])
        c_ref[r] = keep_cells(c_ref[r], keep_t[:, r : r + 1])
    first, last = slice(0, 16), slice(COLS - 16, COLS)

    def column(ref, part, spot):
        cells = jnp.concatenate([ref[r, part, :] for r in range(ROWS)], axis=0)
        pick = iota((ROWS, 256), 1) == iota((ROWS, 256), 0) * 16 + spot
        picked = jnp.dot(pick.astype(F32).astype(BF), cells, preferred_element_type=F32)
        return picked.astype(BF)

    east_ref[0] = column(x_ref, last, 14)
    east_ref[1] = column(x_ref, last, 15)
    east_ref[2] = column(c_ref, last, 15)
    west_ref[0] = column(x_ref, first, 0)
    west_ref[1] = column(x_ref, first, 1)
    west_ref[2] = column(c_ref, first, 0)


def halo_chunks(from_west, from_east, size):
    halo = jnp.concatenate(
        [from_west[i] for i in range(3)] + [from_east[i] for i in range(3)], axis=0
    )
    shape = (ROWS * size, 96)
    row = iota(shape, 0) // size
    spot = iota(shape, 0) % size
    source = iota(shape, 1)

    def chunk(at):
        want = jnp.full(shape, -1, jnp.int32)
        for where, plane in at:
            want = jnp.where(spot == where, plane * 16 + row, want)
        pick = (source == want).astype(F32).astype(BF)
        picked = jnp.dot(pick, halo, preferred_element_type=F32)
        return [picked[r * size : r * size + size] for r in range(ROWS)]

    return (
        chunk([(0, 3), (1, 4), (size - 2, 0), (size - 1, 1)]),
        chunk([(0, 5), (size - 1, 2)]),
    )


def keep_cells(cells, column):
    return jnp.where(column > 0, cells.astype(F32), 0.0).astype(BF)


def line_kernel(x_ref, c_ref, from_west, from_east, fold_ref, pair_ref):
    x_chunk, c_chunk = halo_chunks(from_west, from_east, 8)
    even = lax.axis_index("lat") % 2 == 0

    def full(ref, r, chunk):
        return jnp.concatenate([ref[r].astype(F32), chunk[r]], axis=0)

    def pack(one, two, three):
        rest = jnp.concatenate([one[:, 128:], two[:, 128:]], axis=1)
        last = jnp.concatenate([three[:, 128:], jnp.zeros((LINE, 64), F32)], axis=1)
        return one[:, :128], two[:, :128], three[:, :128], rest, last

    top = pack(full(x_ref, 15, x_chunk), full(x_ref, 14, x_chunk), full(c_ref, 15, c_chunk))
    bottom = pack(full(x_ref, 0, x_chunk), full(x_ref, 1, x_chunk), full(c_ref, 0, c_chunk))
    for i in range(5):
        fold_ref[i] = jnp.where(even, bottom[i], top[i]).astype(BF)
        pair_ref[i] = jnp.where(even, top[i], bottom[i]).astype(BF)


def lay(dest, base, rows):
    low = iota((16, C), 0) < 8
    none = jnp.zeros((16, C), F32)
    tails = [none] + [none if r is None else r[1].astype(F32) for r in rows] + [none]
    for k in range(-1, len(rows)):
        at = base + k * S
        if k >= 0:
            dest[at : at + COLS, :] = jnp.zeros((COLS, C), BF) if rows[k] is None else rows[k][0]
        dest[at + COLS : at + S, :] = jnp.where(low, tails[k + 1], tails[k + 2]).astype(BF)


def window(ref):
    return ref[0:COLS, :], ref[COLS:S, :]


def taps(ref, base, at, size, c, weights, sign, contract):
    total = None
    for r in range(3):
        start = base + at + sign * (r - 1) * S
        term = lax.dot_general(
            ref[start : start + size, :], weights[r](r, c),
            (((1,), (contract,)), ((), ())), preferred_element_type=F32,
        )
        total = term if total is None else total + term
    return total


def shifted(ys, at, size, sign):
    at = at + 8
    return (
        ys[0, at - sign : at - sign + size, :]
        + ys[1, at : at + size, :]
        + ys[2, at + sign : at + sign + size, :]
    )


def weight_sums(xe, base, go, xt, lo, span, emit):
    for r in range(3):
        start = base + lo + (r - 1) * S
        xt[r * C : (r + 1) * C, :] = xe[start : start + span, :].T
    for c in range(3):
        start = 8 + lo - (c - 1)
        moved = go[start : start + span, :].astype(BF)
        emit(c, jnp.dot(xt[...], moved, preferred_element_type=F32))


def inner_kernel(
    x_ref, c_ref, kernel_ref, keep_ref, from_west, from_east,
    out_ref, sgrad_ref, part_ref, gedge_ref,
    xe, ce, ga, go, ys, xt,
):
    keep_t = keep_ref[...]
    x_chunk, c_chunk = halo_chunks(from_west, from_east, 16)

    def own(ref, chunk):
        return [(ref[r], chunk[r]) for r in range(ROWS)]

    xe[0:LEAD, :] = jnp.zeros((LEAD, C), BF)
    xe[LEAD + ROWS * S :, :] = jnp.zeros((xe.shape[0] - LEAD - ROWS * S, C), BF)
    lay(xe, LEAD, own(x_ref, x_chunk))
    lay(ce, LEAD, own(c_ref, c_chunk))

    def weight(r, c):
        return kernel_ref[3 * r + c]

    plain = [weight] * 3
    for c in range(3):
        for k in range(3):
            at = 48 + k * 384
            ys[c, 8 + at : 8 + at + 384, :] = taps(xe, LEAD, at, 384, c, plain, 1, 0)
        ys[c, 1208:1216, :] = jnp.zeros((8, C), F32)
    go[...] = jnp.zeros_like(go)
    ga[0:64, :] = jnp.zeros((64, C), BF)
    for w in range(15):
        at, size = (w * S, S) if w else (64, 16)
        pre = shifted(ys, at, size, 1)
        s = jax.nn.sigmoid(pre)
        slope = s * (1.0 + pre * (1.0 - s))
        grad = (ce[LEAD + at : LEAD + at + size, :].astype(F32) * slope).astype(BF)
        ga[at : at + size, :] = grad
        if w:
            go[8 + at : 8 + at + COLS, :] = grad[0:COLS].astype(F32)
            kept = keep_t[:, w : w + 1]
            out_ref[0, w] = (kept * pre[0:COLS] * s[0:COLS]).astype(BF)
    low = iota((16, C), 0) < 8
    for i, r in enumerate((1, 2, 13, 14)):
        gedge_ref[i, 0:COLS, :] = ga[r * S : r * S + COLS, :]
        east = ga[r * S + COLS : r * S + S, :].astype(F32)
        west = ga[(r - 1) * S + COLS : r * S, :].astype(F32)
        gedge_ref[i, COLS:S, :] = jnp.where(low, east, west).astype(BF)

    def emit(c, grad):
        part_ref[c] = grad

    weight_sums(xe, LEAD, go, xt, 64, 1152, emit)
    for c in range(3):
        for k in range(3):
            at = 112 + k * 336
            ys[c, 8 + at : 8 + at + 336, :] = taps(ga, 0, at, 336, c, plain, -1, 1)
    for r in range(2, 14):
        total = shifted(ys, r * S, COLS, -1)
        sgrad_ref[0, r] = keep_cells(total, keep_t[:, r : r + 1])
    for r in (0, 15):
        out_ref[0, r] = jnp.zeros((COLS, C), BF)
    for r in (0, 1, 14, 15):
        sgrad_ref[0, r] = jnp.zeros((COLS, C), BF)


def far_of(kernel_ref, fold):
    def far_weight(r, c):
        return kernel_ref[jnp.where(fold, 8 - (3 * r + c), 3 * r + c)]

    return far_weight


def border_rows(fold, fold_ref, pair_ref, own_fold, own_pair):
    even = lax.axis_index("lat") % 2 == 0
    down = iota((LINE, LINE), 0)
    across = iota((LINE, LINE), 1)
    turned = ((down + across == COLS - 1) | (down + across == COLS - 1 + LINE)).astype(F32)
    straight = (down == across).astype(F32)
    turn = jnp.where(fold, turned, straight).astype(BF)

    def choose(a, b):
        return [jnp.where(even, a[i].astype(F32), b[i].astype(F32)) for i in range(5)]

    def split(blocks):
        one, two, three, rest, last = blocks
        rows = (
            jnp.concatenate([one, rest[:, 0:64]], axis=1),
            jnp.concatenate([two, rest[:, 64:128]], axis=1),
            jnp.concatenate([three, last[:, 0:64]], axis=1),
        )
        return [
            (r[0:COLS].astype(BF), jnp.concatenate([r[COLS:LINE], r[COLS:LINE]], axis=0))
            for r in rows
        ]

    south = split(choose(fold_ref, pair_ref))
    north = split([
        jnp.dot(turn, v.astype(BF), preferred_element_type=F32) for v in choose(pair_ref, fold_ref)
    ])
    top = split(choose(own_pair, own_fold))
    bottom = split(choose(own_fold, own_pair))
    return south, bottom, top, north


def slope_at(ys, at, size):
    pre = shifted(ys, at, size, 1)
    s = jax.nn.sigmoid(pre)
    return pre, s, s * (1.0 + pre * (1.0 - s))


def row_of(ga, slot, dest):
    low = iota((16, C), 0) < 8
    dest[0:COLS, :] = ga[slot * S : slot * S + COLS, :]
    east = ga[slot * S + COLS : slot * S + S, :].astype(F32)
    west = ga[(slot - 1) * S + COLS : slot * S, :].astype(F32)
    dest[COLS:S, :] = jnp.where(low, east, west).astype(BF)


def border_kernel(
    lat_count,
    fold_ref, pair_ref, own_fold, own_pair, kernel_ref, keep_ref, part_ref, out_in,
    out_ref, gown_ref, give_ref, hold_ref,
    xb, cb, ga, go, ys, xt, packed, edge_out, sems,
):
    del out_in
    core = lax.axis_index("core")
    fold = lax.axis_index("lat") == lat_count - 1
    keep_t = keep_ref[...]
    south, bottom, top, north = border_rows(fold, fold_ref, pair_ref, own_fold, own_pair)
    xb[0:S, :] = jnp.zeros((S, C), BF)
    xb[7 * S :, :] = jnp.zeros((xb.shape[0] - 7 * S, C), BF)
    lay(xb, S, [south[0], bottom[0], bottom[1], top[1], top[0], north[0]])
    lay(cb, S, [None, bottom[2], None, None, top[2], None])

    def weight(r, c):
        return kernel_ref[3 * r + c]

    for c in range(3):
        ys[c, 8 + 144 : 8 + 480, :] = taps(xb, 0, 144, 336, c, [weight] * 3, 1, 0)
        ys[c, 144:152, :] = jnp.zeros((8, C), F32)
        ys[c, 488:496, :] = jnp.zeros((8, C), F32)
    go[...] = jnp.zeros_like(go)
    for slot in (1, 2, 4, 5):
        at, size = (slot * S + COLS, 16) if slot in (1, 4) else (slot * S, S)
        pre, s, slope = slope_at(ys, at, size)
        grad = (cb[at : at + size, :].astype(F32) * slope).astype(BF)
        ga[at : at + size, :] = grad
        if slot in (2, 5):
            go[8 + at : 8 + at + COLS, :] = grad[0:COLS].astype(F32)
            r = 0 if slot == 2 else ROWS - 1
            kept = keep_t[:, r : r + 1]
            edge_out[slot // 5] = (kept * pre[0:COLS] * s[0:COLS]).astype(BF)
    copies = [
        pltpu.make_async_copy(edge_out.at[i], out_ref.at[0, r], sems.at[i])
        for i, r in enumerate((0, ROWS - 1))
    ]
    for copy in copies:
        copy.start()
    row_of(ga, 2, gown_ref.at[0])
    row_of(ga, 5, gown_ref.at[1])

    tails = []

    def emit(c, grad):
        grad = grad + part_ref[c]
        where = ((0, 0), (0, 576), (1, 0))[c]
        packed[where[0], where[1] : where[1] + 576, :] = grad[:, 0:128]
        tails.append(grad[:, 128:C])

    weight_sums(xb, 0, go, xt, 144, 384, emit)
    packed[1, 576:1152, :] = jnp.concatenate(tails[0:2], axis=1)
    rest = jnp.concatenate([tails[2][0:288], tails[2][288:576]], axis=1)
    packed[0, 1152:HALF, :] = rest[0:144]
    packed[1, 1152:HALF, :] = rest[144:288]
    for i in range(2):
        if packed.shape[1] > HALF:
            packed[i, HALF:, :] = jnp.zeros((packed.shape[1] - HALF, 128), F32)
    give_ref[...] = packed[1 - core].astype(BF)
    hold_ref[...] = packed[core]
    for copy in copies:
        copy.wait()


def ghost_kernel(
    lat_count, fold_ref, pair_ref, own_fold, own_pair, kernel_ref, ghost_ref, xb, cb, ga, ys,
):
    fold = lax.axis_index("lat") == lat_count - 1
    south, bottom, top, north = border_rows(fold, fold_ref, pair_ref, own_fold, own_pair)
    xb[0:S, :] = jnp.zeros((S, C), BF)
    xb[7 * S :, :] = jnp.zeros((xb.shape[0] - 7 * S, C), BF)
    lay(xb, S, [south[1], south[0], bottom[0], top[0], north[0], north[1]])
    lay(cb, S, [None, south[2], None, None, north[2], None])

    def weight(r, c):
        return kernel_ref[3 * r + c]

    far_weight = far_of(kernel_ref, fold)
    for c in range(3):
        ys[c, 152:248, :] = taps(xb, 0, 144, 96, c, [weight] * 3, 1, 0)
        ys[c, 392:488, :] = taps(xb, 0, 384, 96, c, [far_weight] * 3, 1, 0)
        for at in (144, 248, 384, 488):
            ys[c, at : at + 8, :] = jnp.zeros((8, C), F32)
    for at in (144, 384):
        grad = cb[at : at + 96, :].astype(F32) * slope_at(ys, at, 96)[2]
        ga[at : at + 96, :] = grad.astype(BF)
    row_of(ga, 2, ghost_ref.at[0])
    row_of(ga, 5, ghost_ref.at[1])


def state_kernel(
    lat_count, gedge_ref, gown_ref, ghost_ref, kernel_ref, keep_ref, sgrad_in,
    sgrad_ref, gb, ys, edge_out, sems,
):
    del sgrad_in
    fold = lax.axis_index("lat") == lat_count - 1
    keep_t = keep_ref[...]
    gb[0:S, :] = jnp.zeros((S, C), BF)
    gb[9 * S :, :] = jnp.zeros((gb.shape[0] - 9 * S, C), BF)
    lay(
        gb, S,
        [window(ref.at[i]) for ref, i in (
            (ghost_ref, 0), (gown_ref, 0), (gedge_ref, 0), (gedge_ref, 1),
            (gedge_ref, 2), (gedge_ref, 3), (gown_ref, 1), (ghost_ref, 1),
        )],
    )

    def weight(r, c):
        return kernel_ref[3 * r + c]

    for c in range(3):
        ys[c, 8 + 144 : 8 + 640, :] = taps(gb, 0, 144, 496, c, [weight] * 3, -1, 1)
        edge = taps(gb, 0, 7 * S - 16, 96, c, [far_of(kernel_ref, fold), weight, weight], -1, 1)
        ys[c, 7 * S : 8 + 8 * S, :] = edge[8:]
    copies = []
    for i, (slot, r) in enumerate(((2, 0), (3, 1), (6, 14), (7, 15))):
        total = shifted(ys, slot * S, COLS, -1)
        edge_out[i] = keep_cells(total, keep_t[:, r : r + 1])
        copies.append(pltpu.make_async_copy(edge_out.at[i], sgrad_ref.at[0, r], sems.at[i]))
        copies[-1].start()
    for copy in copies:
        copy.wait()


def add_kernel(hold_ref, came_ref, ghost_ref, out_ref):
    del ghost_ref
    out_ref[...] = (hold_ref[...] + came_ref[...].astype(F32)).astype(BF)


def sum_kernel(parts_ref, out_ref):
    total = parts_ref[0].astype(F32)
    for i in range(1, parts_ref.shape[0]):
        total = total + parts_ref[i].astype(F32)
    total = total.astype(BF)
    for i in range(out_ref.shape[0]):
        out_ref[i] = total


def unpack_kernel(scale, mine_ref, other_ref, out_ref):
    mine_first = lax.axis_index("core") == 0

    def get(half, at, size):
        a = mine_ref[at : at + size, :].astype(F32)
        b = other_ref[at : at + size, :].astype(F32)
        return jnp.where(mine_first == (half == 0), a, b) * scale

    for c, (half, base) in enumerate(((0, 0), (0, 576), (1, 0))):
        for r in range(3):
            out_ref[r, c, :, 0:128] = get(half, base + r * C, C)
    for r in range(3):
        both = get(1, 576 + r * C, C)
        out_ref[r, 0, :, 128:C] = both[:, 0:64]
        out_ref[r, 1, :, 128:C] = both[:, 64:128]
    one, two = get(0, 1152, 144), get(1, 1152, 144)
    out_ref[0, 2, 0:144, 128:C] = one[:, 0:64]
    out_ref[0, 2, 144:192, 128:C] = two[0:48, 0:64]
    out_ref[1, 2, 0:96, 128:C] = two[48:144, 0:64]
    out_ref[1, 2, 96:192, 128:C] = one[0:96, 64:128]
    out_ref[2, 2, 0:48, 128:C] = one[96:144, 64:128]
    out_ref[2, 2, 48:192, 128:C] = two[:, 64:128]


def solution(mesh):
    lon_count, lat_count, dp_count = (mesh.shape[n] for n in ("lon", "lat", "dp"))
    z_count = lon_count // 4
    fine = Mesh(
        mesh.devices.reshape(z_count, 2, 2, lat_count, dp_count),
        ("z", "twin", "core", "lat", "dp"),
    )
    lon = ("z", "twin", "core")
    sheet = ("twin", "lat", "dp")
    sheet_count = 2 * lat_count * dp_count
    eastward = [(i, (i + 1) % lon_count) for i in range(lon_count)]
    westward = [(b, a) for a, b in eastward]
    lat_pairs, fold_pairs = [], []
    for b in range(lon_count):
        for a in range(lat_count):
            lat_pairs.append((b * lat_count + a, b * lat_count + (a ^ 1)))
            if a == lat_count - 1:
                fold_pairs.append((b * lat_count + a, (lon_count - 1 - b) * lat_count + a))
            elif a > 0:
                fold_pairs.append((b * lat_count + a, b * lat_count + (a + 1 if a % 2 else a - 1)))
    scale = 1.0 / math.sqrt(dp_count * lat_count * ROWS * lon_count * COLS)
    part = -(-HALF // (8 * sheet_count)) * 8
    half_rows = sheet_count * part
    smem = pl.BlockSpec(memory_space=pltpu.SMEM)
    vmem = pl.BlockSpec(memory_space=pltpu.VMEM)
    hbm = pl.BlockSpec(memory_space=pltpu.HBM)
    whole = jax.ShapeDtypeStruct((1, ROWS, COLS, C), BF)

    def shaped(shape, kind=BF):
        return jax.ShapeDtypeStruct(shape, kind)

    def call(kernel, name, ins, out_shape, outs, scratch=(), aliases=None, cost=0):
        return pl.pallas_call(
            kernel,
            out_shape=out_shape,
            in_specs=ins,
            out_specs=outs,
            scratch_shapes=list(scratch),
            input_output_aliases=aliases or {},
            compiler_params=pltpu.CompilerParams(vmem_limit_bytes=40 * 2**20),
            cost_estimate=pl.CostEstimate(
                flops=cost, bytes_accessed=2**20, transcendentals=0
            ) if cost else None,
            name=name,
        )

    def body(states, cotangent, kernel, land_mask, ocean_tiles):
        taps9 = kernel.reshape(9, C, C)
        cells = shaped((ROWS, COLS, C))
        east, west, x, c, keep = call(
            edge_kernel, "edges", [hbm] * 4,
            (shaped((3, ROWS, C)),) * 2 + (cells, cells, shaped((COLS, ROWS), F32)), (vmem,) * 5,
            scratch=[
                pltpu.VMEM((ROWS, COLS), jnp.int32),
                pltpu.SMEM(ocean_tiles.shape, jnp.int32),
                pltpu.SemaphoreType.DMA((4,)),
            ],
        )(*(pltpu.with_memory_space_constraint(v, pltpu.HBM)
            for v in (states, cotangent, land_mask, ocean_tiles)))
        from_west = lax.ppermute(east, lon, eastward)
        from_east = lax.ppermute(west, lon, westward)
        own_fold, own_pair = call(
            line_kernel, "lines", [vmem] * 4, (shaped((5, LINE, 128)),) * 2, (vmem,) * 2,
        )(x, c, from_west, from_east)
        pair = lax.ppermute(own_pair, lon + ("lat",), lat_pairs)
        fold = lax.ppermute(own_fold, lon + ("lat",), fold_pairs)
        output, state_grad, sums, gedge = call(
            inner_kernel, "inner", [vmem] * 6,
            (whole, whole, shaped((3, 576, C), F32), shaped((4, S, C))), (vmem,) * 4,
            scratch=[
                pltpu.VMEM((LEAD + ROWS * S + 32, C), BF),
                pltpu.VMEM((LEAD + ROWS * S, C), BF),
                pltpu.VMEM((15 * S, C), BF),
                pltpu.VMEM((8 + ROWS * S + 16, C), F32),
                pltpu.VMEM((3, ROWS * S + 16, C), F32),
                pltpu.VMEM((576, 1152), BF),
            ],
            cost=2 * 10**9,
        )(x, c, taps9, keep, from_west, from_east)
        lines = (fold, pair, own_fold, own_pair)
        output, gown, give, hold = call(
            lambda *refs: border_kernel(lat_count, *refs), "border", [vmem] * 7 + [hbm],
            (whole, shaped((2, S, C)), shaped((half_rows, 128)), shaped((half_rows, 128), F32)),
            (hbm, vmem, vmem, vmem),
            scratch=[
                pltpu.VMEM((8 * S, C), BF),
                pltpu.VMEM((7 * S, C), BF),
                pltpu.VMEM((7 * S, C), BF),
                pltpu.VMEM((7 * S, C), F32),
                pltpu.VMEM((3, 7 * S + 16, C), F32),
                pltpu.VMEM((576, 384), BF),
                pltpu.VMEM((2, half_rows, 128), F32),
                pltpu.VMEM((2, COLS, C), BF),
                pltpu.SemaphoreType.DMA((2,)),
            ],
            aliases={7: 0}, cost=5 * 10**8,
        )(*lines, taps9, keep, sums, output)
        came = lax.ppermute(give, "core", [(0, 1), (1, 0)])
        ghost = call(
            lambda *refs: ghost_kernel(lat_count, *refs), "ghost", [vmem] * 5,
            shaped((2, S, C)), vmem,
            scratch=[
                pltpu.VMEM((8 * S, C), BF),
                pltpu.VMEM((7 * S, C), BF),
                pltpu.VMEM((7 * S, C), BF),
                pltpu.VMEM((3, 7 * S + 16, C), F32),
            ],
            cost=5 * 10**8,
        )(*lines, taps9)
        state_grad = call(
            lambda *refs: state_kernel(lat_count, *refs), "state", [vmem] * 5 + [hbm], whole, hbm,
            scratch=[
                pltpu.VMEM((10 * S, C), BF),
                pltpu.VMEM((3, 8 * S + 16, C), F32),
                pltpu.VMEM((4, COLS, C), BF),
                pltpu.SemaphoreType.DMA((4,)),
            ],
            aliases={5: 0}, cost=5 * 10**8,
        )(gedge, gown, ghost, taps9, keep, state_grad)

        def summed(parts, copies):
            return call(sum_kernel, "sum", [vmem], shaped((copies, part, 128)), vmem)(parts)

        parts = call(add_kernel, "add", [vmem] * 2 + [hbm], shaped((half_rows, 128)), vmem)(hold, came, ghost)
        parts = lax.all_to_all(parts.reshape(sheet_count, part, 128), sheet, 0, 0, tiled=True)
        parts = lax.all_to_all(summed(parts, z_count), "z", 0, 0, tiled=True)
        parts = lax.all_to_all(summed(parts, sheet_count), sheet, 0, 0, tiled=True)
        mine = parts.reshape(half_rows, 128)
        other = lax.ppermute(mine, "core", [(0, 1), (1, 0)])
        weight_grad = call(
            lambda *refs: unpack_kernel(scale, *refs), "unpack", [vmem] * 2,
            shaped((3, 3, C, C), F32), vmem,
        )(mine, other)
        return output, state_grad, weight_grad

    cells = P("dp", "lat", lon, None)
    return jax.shard_map(
        body,
        mesh=fine,
        in_specs=(cells, cells, P(), P("lat", lon), P("lat", lon, None)),
        out_specs=(cells, cells, P()),
        check_vma=False,
    )
```

```python
import math

import jax
import jax.numpy as jnp
from jax import lax
from jax.experimental import pallas as pl
from jax.experimental.pallas import tpu as pltpu
from jax.sharding import Mesh
from jax.sharding import PartitionSpec as P

BF = jnp.bfloat16
F32 = jnp.float32
TS = 16
ROWS = 16
COLS = 64
C = 192
S = 80
LEAD = 32
LINE = 72
MESSAGE = 4 * LINE + 40
HALF = 1296


def iota(shape, dim):
    return lax.broadcasted_iota(jnp.int32, shape, dim)


def keep_plane(mask_ref, tiles_ref):
    tile = iota((ROWS, COLS), 1) // TS
    listed = jnp.zeros((ROWS, COLS), F32)
    for slot in range(tiles_ref.shape[-1]):
        listed = jnp.where(tile == tiles_ref[0, 0, slot], 1.0, listed)
    return jnp.where(mask_ref[...] > 0, listed, 0.0)


def fetch(copies):
    started = [pltpu.make_async_copy(*copy) for copy in copies]
    for copy in started:
        copy.start()
    for copy in started:
        copy.wait()


def edge_kernel(
    states_ref, cot_ref, mask_hbm, tiles_hbm, east_ref, west_ref, x_ref, c_ref, keep_ref,
    mask_ref, tiles_ref, sems,
):
    fetch([
        (mask_hbm, mask_ref, sems.at[0]),
        (tiles_hbm, tiles_ref, sems.at[1]),
        (states_ref.at[0], x_ref, sems.at[2]),
        (cot_ref.at[0], c_ref, sems.at[3]),
    ])
    keep = keep_plane(mask_ref, tiles_ref)
    keep_t = keep.T
    keep_ref[...] = keep_t
    for r in range(ROWS):
        x_ref[r] = keep_cells(x_ref[r], keep_t[:, r : r + 1])
        c_ref[r] = keep_cells(c_ref[r], keep_t[:, r : r + 1])
    first, last = slice(0, 16), slice(COLS - 16, COLS)

    def column(ref, part, spot):
        cells = jnp.concatenate([ref[r, part, :] for r in range(ROWS)], axis=0)
        pick = iota((ROWS, 256), 1) == iota((ROWS, 256), 0) * 16 + spot
        picked = jnp.dot(pick.astype(F32).astype(BF), cells, preferred_element_type=F32)
        return picked.astype(BF)

    east_ref[0] = column(x_ref, last, 14)
    east_ref[1] = column(x_ref, last, 15)
    east_ref[2] = column(c_ref, last, 15)
    west_ref[0] = column(x_ref, first, 0)
    west_ref[1] = column(x_ref, first, 1)
    west_ref[2] = column(c_ref, first, 0)


def halo_chunks(from_west, from_east, size):
    halo = jnp.concatenate(
        [from_west[i] for i in range(3)] + [from_east[i] for i in range(3)], axis=0
    )
    shape = (ROWS * size, 96)
    row = iota(shape, 0) // size
    spot = iota(shape, 0) % size
    source = iota(shape, 1)

    def chunk(at):
        want = jnp.full(shape, -1, jnp.int32)
        for where, plane in at:
            want = jnp.where(spot == where, plane * 16 + row, want)
        pick = (source == want).astype(F32).astype(BF)
        picked = jnp.dot(pick, halo, preferred_element_type=F32)
        return [picked[r * size : r * size + size] for r in range(ROWS)]

    return (
        chunk([(0, 3), (1, 4), (size - 2, 0), (size - 1, 1)]),
        chunk([(0, 5), (size - 1, 2)]),
    )


def keep_cells(cells, column):
    return jnp.where(column > 0, cells.astype(F32), 0.0).astype(BF)


def line_kernel(x_ref, c_ref, from_west, from_east, fold_ref, pair_ref):
    x_chunk, c_chunk = halo_chunks(from_west, from_east, 8)
    even = lax.axis_index("lat") % 2 == 0

    def full(ref, r, chunk):
        return jnp.concatenate([ref[r].astype(F32), chunk[r]], axis=0)

    def pack(one, two, three):
        rest = jnp.concatenate([one[:, 128:], two[:, 128:]], axis=1)
        wide = jnp.concatenate([three[40:, 128:], jnp.zeros((80 - LINE, 64), F32)], axis=0)
        last = jnp.concatenate([three[:40, 128:], wide], axis=1)
        return jnp.concatenate([one[:, :128], two[:, :128], three[:, :128], rest, last], axis=0)

    top = pack(full(x_ref, 15, x_chunk), full(x_ref, 14, x_chunk), full(c_ref, 15, c_chunk))
    bottom = pack(full(x_ref, 0, x_chunk), full(x_ref, 1, x_chunk), full(c_ref, 0, c_chunk))
    fold_ref[...] = jnp.where(even, bottom, top).astype(BF)
    pair_ref[...] = jnp.where(even, top, bottom).astype(BF)


def lay(dest, base, rows):
    low = iota((16, C), 0) < 8
    none = jnp.zeros((16, C), F32)
    tails = [none] + [none if r is None else r[1].astype(F32) for r in rows] + [none]
    for k in range(-1, len(rows)):
        at = base + k * S
        if k >= 0:
            dest[at : at + COLS, :] = jnp.zeros((COLS, C), BF) if rows[k] is None else rows[k][0]
        dest[at + COLS : at + S, :] = jnp.where(low, tails[k + 1], tails[k + 2]).astype(BF)


def window(ref):
    return ref[0:COLS, :], ref[COLS:S, :]


def taps(ref, base, at, size, c, weights, sign, contract):
    total = None
    for r in range(3):
        start = base + at + sign * (r - 1) * S
        term = lax.dot_general(
            ref[start : start + size, :], weights[r](r, c),
            (((1,), (contract,)), ((), ())), preferred_element_type=F32,
        )
        total = term if total is None else total + term
    return total


def shifted(ys, at, size, sign):
    at = at + 8
    return (
        ys[0, at - sign : at - sign + size, :]
        + ys[1, at : at + size, :]
        + ys[2, at + sign : at + sign + size, :]
    )


def weight_terms(xe, base, go, xt, lo, span):
    for r in range(3):
        start = base + lo + (r - 1) * S
        xt[r * C : (r + 1) * C, :] = xe[start : start + span, :].T
    starts = [8 + lo - (c - 1) for c in range(3)]
    return [go[start : start + span, :].astype(BF) for start in starts]


def inner_kernel(
    x_ref, c_ref, kernel_ref, keep_ref, from_west, from_east,
    out_ref, sgrad_ref, part_ref, ga,
    xe, ce, go, ys, xt,
):
    keep_t = keep_ref[...]
    x_chunk, c_chunk = halo_chunks(from_west, from_east, 16)

    def own(ref, chunk):
        return [(ref[r], chunk[r]) for r in range(ROWS)]

    xe[0:LEAD, :] = jnp.zeros((LEAD, C), BF)
    xe[LEAD + ROWS * S :, :] = jnp.zeros((xe.shape[0] - LEAD - ROWS * S, C), BF)
    lay(xe, LEAD, own(x_ref, x_chunk))
    lay(ce, LEAD, own(c_ref, c_chunk))

    def weight(r, c):
        return kernel_ref[3 * r + c]

    plain = [weight] * 3
    for c in range(3):
        for k in range(3):
            at = 48 + k * 384
            ys[c, 8 + at : 8 + at + 384, :] = taps(xe, LEAD, at, 384, c, plain, 1, 0)
        ys[c, 1208:1216, :] = jnp.zeros((8, C), F32)
    go[...] = jnp.zeros_like(go)
    ga[0:64, :] = jnp.zeros((64, C), BF)
    for w in range(15):
        at, size = (w * S, S) if w else (64, 16)
        pre = shifted(ys, at, size, 1)
        s = jax.nn.sigmoid(pre)
        slope = s * (1.0 + pre * (1.0 - s))
        grad = (ce[LEAD + at : LEAD + at + size, :].astype(F32) * slope).astype(BF)
        ga[at : at + size, :] = grad
        if w:
            go[8 + at : 8 + at + COLS, :] = grad[0:COLS].astype(F32)
            kept = keep_t[:, w : w + 1]
            out_ref[0, w] = (kept * pre[0:COLS] * s[0:COLS]).astype(BF)
    for c in range(3):
        for k in range(3):
            at = 112 + k * 336
            ys[c, 8 + at : 8 + at + 336, :] = taps(ga, 0, at, 336, c, plain, -1, 1)
    for r in range(2, 14):
        sgrad_ref[0, r] = keep_cells(shifted(ys, r * S, COLS, -1), keep_t[:, r : r + 1])
    for r in (0, 15):
        out_ref[0, r] = jnp.zeros((COLS, C), BF)
    for r in (0, 1, 14, 15):
        sgrad_ref[0, r] = jnp.zeros((COLS, C), BF)
    moved = weight_terms(xe, LEAD, go, xt, 64, 1152)
    for c in range(3):
        part_ref[c] = jnp.dot(xt[...], moved[c], preferred_element_type=F32)


def far_of(kernel_ref, fold):
    def far_weight(r, c):
        return kernel_ref[jnp.where(fold, 8 - (3 * r + c), 3 * r + c)]

    return far_weight


def border_rows(fold, fold_ref, pair_ref, own_fold, own_pair):
    even = lax.axis_index("lat") % 2 == 0
    down = iota((LINE, LINE), 0)
    across = iota((LINE, LINE), 1)
    turned = ((down + across == COLS - 1) | (down + across == COLS - 1 + LINE)).astype(F32)
    straight = (down == across).astype(F32)
    turn = jnp.where(fold, turned, straight).astype(BF)

    def choose(a, b):
        return jnp.where(even, a[...].astype(F32), b[...].astype(F32))

    def split(message, turned_by=None):
        blocks = [message[i * LINE : (i + 1) * LINE] for i in range(4)]
        last = message[4 * LINE :]
        rows = [
            jnp.concatenate([blocks[0], blocks[3][:, 0:64]], axis=1),
            jnp.concatenate([blocks[1], blocks[3][:, 64:128]], axis=1),
            jnp.concatenate([
                blocks[2], jnp.concatenate([last[:, 0:64], last[0 : LINE - 40, 64:128]], axis=0)
            ], axis=1),
        ]
        if turned_by is not None:
            rows = [
                jnp.dot(turned_by, r.astype(BF), preferred_element_type=F32) for r in rows
            ]
        return [
            (r[0:COLS].astype(BF), jnp.concatenate([r[COLS:LINE], r[COLS:LINE]], axis=0))
            for r in rows
        ]

    south = split(choose(fold_ref, pair_ref))
    north = split(choose(pair_ref, fold_ref), turn)
    top = split(choose(own_pair, own_fold))
    bottom = split(choose(own_fold, own_pair))
    return south, bottom, top, north


def slope_at(ys, at, size):
    pre = shifted(ys, at, size, 1)
    s = jax.nn.sigmoid(pre)
    return pre, s, s * (1.0 + pre * (1.0 - s))


def row_parts(ga, slot):
    low = iota((16, C), 0) < 8
    east = ga[slot * S + COLS : slot * S + S, :].astype(F32)
    west = ga[(slot - 1) * S + COLS : slot * S, :].astype(F32)
    return ga[slot * S : slot * S + COLS, :], jnp.where(low, east, west).astype(BF)


def row_of(ga, slot, dest):
    dest[0:COLS, :], dest[COLS:S, :] = row_parts(ga, slot)


def pack_half(half, xt, moved, part_ref, dest):
    mine = pl.ds(pl.multiple_of(half * 288, 288), 288)
    tails = []
    for c in range(3):
        grad = jnp.dot(xt[mine, :], moved[c], preferred_element_type=F32) + part_ref[c, mine, :]
        dest[c * 288 : (c + 1) * 288, :] = grad[:, 0:128].astype(dest.dtype)
        tails.append(grad[:, 128:C])
    dest[864:1152, :] = jnp.concatenate(tails[0:2], axis=1).astype(dest.dtype)
    rest = jnp.concatenate([tails[2][0:144], tails[2][144:288]], axis=1)
    dest[1152:HALF, :] = rest.astype(dest.dtype)
    if dest.shape[0] > HALF:
        dest[HALF:, :] = jnp.zeros((dest.shape[0] - HALF, 128), dest.dtype)


def border_kernel(
    lat_count,
    fold_ref, pair_ref, own_fold, own_pair, kernel_ref, keep_ref, part_ref,
    edge_ref, gown_ref, give_ref, xt, moved_ref,
    xb, cb, ga, go, ys,
):
    fold = lax.axis_index("lat") == lat_count - 1
    keep_t = keep_ref[...]
    south, bottom, top, north = border_rows(fold, fold_ref, pair_ref, own_fold, own_pair)
    xb[0:S, :] = jnp.zeros((S, C), BF)
    xb[7 * S :, :] = jnp.zeros((xb.shape[0] - 7 * S, C), BF)
    lay(xb, S, [south[0], bottom[0], bottom[1], top[1], top[0], north[0]])
    lay(cb, S, [None, bottom[2], None, None, top[2], None])

    def weight(r, c):
        return kernel_ref[3 * r + c]

    for c in range(3):
        ys[c, 8 + 144 : 8 + 480, :] = taps(xb, 0, 144, 336, c, [weight] * 3, 1, 0)
        ys[c, 144:152, :] = jnp.zeros((8, C), F32)
        ys[c, 488:496, :] = jnp.zeros((8, C), F32)
    go[...] = jnp.zeros_like(go)
    for slot in (1, 2, 4, 5):
        at, size = (slot * S + COLS, 16) if slot in (1, 4) else (slot * S, S)
        pre, s, slope = slope_at(ys, at, size)
        grad = (cb[at : at + size, :].astype(F32) * slope).astype(BF)
        ga[at : at + size, :] = grad
        if slot in (2, 5):
            go[8 + at : 8 + at + COLS, :] = grad[0:COLS].astype(F32)
            r = 0 if slot == 2 else ROWS - 1
            kept = keep_t[:, r : r + 1]
            edge_ref[slot // 5] = (kept * pre[0:COLS] * s[0:COLS]).astype(BF)
    row_of(ga, 2, gown_ref.at[0])
    row_of(ga, 5, gown_ref.at[1])
    moved = weight_terms(xb, 0, go, xt, 144, 384)
    for c in range(3):
        moved_ref[c] = moved[c]
    pack_half(1 - lax.axis_index("core"), xt, moved, part_ref, give_ref)


def ghost_kernel(
    lat_count, fold_ref, pair_ref, own_fold, own_pair, kernel_ref,
    xt, moved_ref, part_ref, edge_ref, out_in,
    ghost_ref, hold_ref, out_ref, xb, cb, ga, ys, sems,
):
    del out_in
    copies = [
        pltpu.make_async_copy(edge_ref.at[i], out_ref.at[0, r], sems.at[i])
        for i, r in enumerate((0, ROWS - 1))
    ]
    for copy in copies:
        copy.start()
    pack_half(lax.axis_index("core"), xt, [moved_ref[c] for c in range(3)], part_ref, hold_ref)
    fold = lax.axis_index("lat") == lat_count - 1
    south, bottom, top, north = border_rows(fold, fold_ref, pair_ref, own_fold, own_pair)
    xb[0:S, :] = jnp.zeros((S, C), BF)
    xb[7 * S :, :] = jnp.zeros((xb.shape[0] - 7 * S, C), BF)
    lay(xb, S, [south[1], south[0], bottom[0], top[0], north[0], north[1]])
    lay(cb, S, [None, south[2], None, None, north[2], None])

    def weight(r, c):
        return kernel_ref[3 * r + c]

    far_weight = far_of(kernel_ref, fold)
    for c in range(3):
        ys[c, 152:248, :] = taps(xb, 0, 144, 96, c, [weight] * 3, 1, 0)
        ys[c, 392:488, :] = taps(xb, 0, 384, 96, c, [far_weight] * 3, 1, 0)
        for at in (144, 248, 384, 488):
            ys[c, at : at + 8, :] = jnp.zeros((8, C), F32)
    for at in (144, 384):
        grad = cb[at : at + 96, :].astype(F32) * slope_at(ys, at, 96)[2]
        ga[at : at + 96, :] = grad.astype(BF)
    row_of(ga, 2, ghost_ref.at[0])
    row_of(ga, 5, ghost_ref.at[1])
    for copy in copies:
        copy.wait()


def state_kernel(
    lat_count, inner_ref, gown_ref, ghost_ref, kernel_ref, keep_ref, sgrad_in,
    sgrad_ref, gb, ys, rows_out, sems,
):
    del sgrad_in
    fold = lax.axis_index("lat") == lat_count - 1
    keep_t = keep_ref[...]
    gb[0:S, :] = jnp.zeros((S, C), BF)
    gb[9 * S :, :] = jnp.zeros((gb.shape[0] - 9 * S, C), BF)
    lay(
        gb, S,
        [
            window(ghost_ref.at[0]), window(gown_ref.at[0]),
            row_parts(inner_ref, 1), row_parts(inner_ref, 2),
            row_parts(inner_ref, 13), row_parts(inner_ref, 14),
            window(gown_ref.at[1]), window(ghost_ref.at[1]),
        ],
    )

    def weight(r, c):
        return kernel_ref[3 * r + c]

    for c in range(3):
        ys[c, 8 + 144 : 8 + 640, :] = taps(gb, 0, 144, 496, c, [weight] * 3, -1, 1)
        edge = taps(gb, 0, 7 * S - 16, 96, c, [far_of(kernel_ref, fold), weight, weight], -1, 1)
        ys[c, 7 * S : 8 + 8 * S, :] = edge[8:]
    copies = []
    for i, (slot, r) in enumerate(((2, 0), (3, 1), (6, 14), (7, 15))):
        total = shifted(ys, slot * S, COLS, -1)
        rows_out[i] = keep_cells(total, keep_t[:, r : r + 1])
        copies.append(pltpu.make_async_copy(rows_out.at[i], sgrad_ref.at[0, r], sems.at[i]))
        copies[-1].start()
    for copy in copies:
        copy.wait()


def add_kernel(hold_ref, came_ref, out_ref):
    out_ref[...] = (hold_ref[...] + came_ref[...].astype(F32)).astype(BF)


def sum_kernel(parts_ref, out_ref):
    total = parts_ref[0].astype(F32)
    for i in range(1, parts_ref.shape[0]):
        total = total + parts_ref[i].astype(F32)
    total = total.astype(BF)
    for i in range(out_ref.shape[0]):
        out_ref[i] = total


def unpack_kernel(scale, mine_ref, other_ref, out_ref, held, sems):
    mine_first = lax.axis_index("core") == 0

    def get(half, at, size):
        a = mine_ref[at : at + size, :].astype(F32)
        b = other_ref[at : at + size, :].astype(F32)
        return jnp.where(mine_first == (half == 0), a, b) * scale

    pieces = (
        ((0, 0, 0, 192),),
        ((0, 192, 0, 96), (1, 0, 96, 96)),
        ((1, 96, 0, 192),),
    )
    one, two = get(0, 1152, 144), get(1, 1152, 144)
    rests = (
        ((0, one[:, 0:64]), (144, one[0:48, 64:128])),
        ((0, one[48:144, 64:128]), (96, two[0:96, 0:64])),
        ((0, two[96:144, 0:64]), (48, two[:, 64:128])),
    )
    copies = []
    for r in range(3):
        for half, source, at, size in pieces[r]:
            to = slice(at, at + size)
            for c in range(3):
                held[r, c, to, 0:128] = get(half, c * 288 + source, size)
            both = get(half, 864 + source, size)
            held[r, 0, to, 128:C] = both[:, 0:64]
            held[r, 1, to, 128:C] = both[:, 64:128]
        for at, rest in rests[r]:
            held[r, 2, at : at + rest.shape[0], 128:C] = rest
        copies.append(pltpu.make_async_copy(held.at[r], out_ref.at[r], sems.at[r]))
        copies[-1].start()
    for copy in copies:
        copy.wait()


def solution(mesh):
    lon_count, lat_count, dp_count = (mesh.shape[n] for n in ("lon", "lat", "dp"))
    z_count = lon_count // 4
    fine = Mesh(
        mesh.devices.reshape(z_count, 2, 2, lat_count, dp_count),
        ("z", "twin", "core", "lat", "dp"),
    )
    lon = ("z", "twin", "core")
    sheet = ("twin", "lat", "dp")
    sheet_count = 2 * lat_count * dp_count
    eastward = [(i, (i + 1) % lon_count) for i in range(lon_count)]
    westward = [(b, a) for a, b in eastward]
    lat_pairs, fold_pairs = [], []
    for b in range(lon_count):
        for a in range(lat_count):
            lat_pairs.append((b * lat_count + a, b * lat_count + (a ^ 1)))
            if a == lat_count - 1:
                fold_pairs.append((b * lat_count + a, (lon_count - 1 - b) * lat_count + a))
            elif a > 0:
                fold_pairs.append((b * lat_count + a, b * lat_count + (a + 1 if a % 2 else a - 1)))
    scale = 1.0 / math.sqrt(dp_count * lat_count * ROWS * lon_count * COLS)
    part = -(-HALF // (8 * sheet_count)) * 8
    half_rows = sheet_count * part
    smem = pl.BlockSpec(memory_space=pltpu.SMEM)
    vmem = pl.BlockSpec(memory_space=pltpu.VMEM)
    hbm = pl.BlockSpec(memory_space=pltpu.HBM)
    whole = jax.ShapeDtypeStruct((1, ROWS, COLS, C), BF)

    def shaped(shape, kind=BF):
        return jax.ShapeDtypeStruct(shape, kind)

    def call(kernel, name, ins, out_shape, outs, scratch=(), aliases=None, cost=0):
        return pl.pallas_call(
            kernel,
            out_shape=out_shape,
            in_specs=ins,
            out_specs=outs,
            scratch_shapes=list(scratch),
            input_output_aliases=aliases or {},
            compiler_params=pltpu.CompilerParams(vmem_limit_bytes=40 * 2**20),
            cost_estimate=pl.CostEstimate(
                flops=cost, bytes_accessed=2**20, transcendentals=0
            ) if cost else None,
            name=name,
        )

    def body(states, cotangent, kernel, land_mask, ocean_tiles):
        taps9 = kernel.reshape(9, C, C)
        cells = shaped((ROWS, COLS, C))
        east, west, x, c, keep = call(
            edge_kernel, "edges", [hbm] * 4,
            (shaped((3, ROWS, C)),) * 2 + (cells, cells, shaped((COLS, ROWS), F32)), (vmem,) * 5,
            scratch=[
                pltpu.VMEM((ROWS, COLS), jnp.int32),
                pltpu.SMEM(ocean_tiles.shape, jnp.int32),
                pltpu.SemaphoreType.DMA((4,)),
            ],
        )(*(pltpu.with_memory_space_constraint(v, pltpu.HBM)
            for v in (states, cotangent, land_mask, ocean_tiles)))
        from_west = lax.ppermute(east, lon, eastward)
        from_east = lax.ppermute(west, lon, westward)
        own_fold, own_pair = call(
            line_kernel, "lines", [vmem] * 4, (shaped((MESSAGE, 128)),) * 2, (vmem,) * 2,
        )(x, c, from_west, from_east)
        pair = lax.ppermute(own_pair, lon + ("lat",), lat_pairs)
        fold = lax.ppermute(own_fold, lon + ("lat",), fold_pairs)
        output, state_grad, sums, inner_grad = call(
            inner_kernel, "inner", [vmem] * 6,
            (whole, whole, shaped((3, 576, C), F32), shaped((15 * S, C))), (vmem,) * 4,
            scratch=[
                pltpu.VMEM((LEAD + ROWS * S + 32, C), BF),
                pltpu.VMEM((LEAD + ROWS * S, C), BF),
                pltpu.VMEM((8 + ROWS * S + 16, C), F32),
                pltpu.VMEM((3, ROWS * S + 16, C), F32),
                pltpu.VMEM((576, 1152), BF),
            ],
            cost=2 * 10**9,
        )(x, c, taps9, keep, from_west, from_east)
        lines = (fold, pair, own_fold, own_pair)
        edge, gown, give, xt, moved = call(
            lambda *refs: border_kernel(lat_count, *refs), "border", [vmem] * 7,
            (
                shaped((2, COLS, C)), shaped((2, S, C)), shaped((half_rows, 128)),
                shaped((576, 384)), shaped((3, 384, C)),
            ),
            (vmem,) * 5,
            scratch=[
                pltpu.VMEM((8 * S, C), BF),
                pltpu.VMEM((7 * S, C), BF),
                pltpu.VMEM((7 * S, C), BF),
                pltpu.VMEM((7 * S, C), F32),
                pltpu.VMEM((3, 7 * S + 16, C), F32),
            ],
            cost=5 * 10**8,
        )(*lines, taps9, keep, sums)
        came = lax.ppermute(give, "core", [(0, 1), (1, 0)])
        ghost, hold, output = call(
            lambda *refs: ghost_kernel(lat_count, *refs), "ghost", [vmem] * 9 + [hbm],
            (shaped((2, S, C)), shaped((half_rows, 128), F32), whole), (vmem, vmem, hbm),
            scratch=[
                pltpu.VMEM((8 * S, C), BF),
                pltpu.VMEM((7 * S, C), BF),
                pltpu.VMEM((7 * S, C), BF),
                pltpu.VMEM((3, 7 * S + 16, C), F32),
                pltpu.SemaphoreType.DMA((2,)),
            ],
            aliases={9: 2}, cost=5 * 10**8,
        )(*lines, taps9, xt, moved, sums, edge, output)
        state_grad = call(
            lambda *refs: state_kernel(lat_count, *refs), "state",
            [vmem] * 5 + [hbm], whole, hbm,
            scratch=[
                pltpu.VMEM((10 * S, C), BF),
                pltpu.VMEM((3, 8 * S + 16, C), F32),
                pltpu.VMEM((4, COLS, C), BF),
                pltpu.SemaphoreType.DMA((4,)),
            ],
            aliases={5: 0}, cost=5 * 10**8,
        )(inner_grad, gown, ghost, taps9, keep, state_grad)

        def summed(parts, copies):
            return call(sum_kernel, "sum", [vmem], shaped((copies, part, 128)), vmem)(parts)

        parts = call(add_kernel, "add", [vmem] * 2, shaped((half_rows, 128)), vmem)(hold, came)
        parts = lax.all_to_all(parts.reshape(sheet_count, part, 128), sheet, 0, 0, tiled=True)
        parts = lax.all_to_all(summed(parts, z_count), "z", 0, 0, tiled=True)
        parts = lax.all_to_all(summed(parts, sheet_count), sheet, 0, 0, tiled=True)
        mine = parts.reshape(half_rows, 128)
        other = lax.ppermute(mine, "core", [(0, 1), (1, 0)])
        weight_grad = call(
            lambda *refs: unpack_kernel(scale, *refs), "unpack", [vmem] * 2,
            shaped((3, 3, C, C), F32), hbm,
            scratch=[pltpu.VMEM((3, 3, C, C), F32), pltpu.SemaphoreType.DMA((3,))],
        )(mine, other)
        return output, state_grad, weight_grad

    cells = P("dp", "lat", lon, None)
    return jax.shard_map(
        body,
        mesh=fine,
        in_specs=(cells, cells, P(), P("lat", lon), P("lat", lon, None)),
        out_specs=(cells, cells, P()),
        check_vma=False,
    )
```

```python
import math

import jax
import jax.numpy as jnp
from jax import lax
from jax.experimental import pallas as pl
from jax.experimental.pallas import tpu as pltpu
from jax.sharding import Mesh
from jax.sharding import PartitionSpec as P

BF = jnp.bfloat16
F32 = jnp.float32
TS = 16
ROWS = 16
COLS = 64
C = 192
S = 80
LEAD = 32
LINE = 72
MESSAGE = 4 * LINE + 40
HALF = 1296


def iota(shape, dim):
    return lax.broadcasted_iota(jnp.int32, shape, dim)


def keep_plane(mask_ref, tiles_ref):
    tile = iota((ROWS, COLS), 1) // TS
    listed = jnp.zeros((ROWS, COLS), F32)
    for slot in range(tiles_ref.shape[-1]):
        listed = jnp.where(tile == tiles_ref[0, 0, slot], 1.0, listed)
    return jnp.where(mask_ref[...] > 0, listed, 0.0)


def fetch(copies):
    started = [pltpu.make_async_copy(*copy) for copy in copies]
    for copy in started:
        copy.start()
    for copy in started:
        copy.wait()


def edge_kernel(
    states_ref, cot_ref, mask_hbm, tiles_hbm, east_ref, west_ref, x_ref, c_ref, keep_ref,
    mask_ref, tiles_ref, sems,
):
    fetch([
        (mask_hbm, mask_ref, sems.at[0]),
        (tiles_hbm, tiles_ref, sems.at[1]),
        (states_ref.at[0], x_ref, sems.at[2]),
        (cot_ref.at[0], c_ref, sems.at[3]),
    ])
    keep = keep_plane(mask_ref, tiles_ref)
    keep_t = keep.T
    keep_ref[...] = keep_t
    for r in range(ROWS):
        x_ref[r] = keep_cells(x_ref[r], keep_t[:, r : r + 1])
        c_ref[r] = keep_cells(c_ref[r], keep_t[:, r : r + 1])
    first, last = slice(0, 16), slice(COLS - 16, COLS)

    def column(ref, part, spot):
        cells = jnp.concatenate([ref[r, part, :] for r in range(ROWS)], axis=0)
        pick = iota((ROWS, 256), 1) == iota((ROWS, 256), 0) * 16 + spot
        picked = jnp.dot(pick.astype(F32).astype(BF), cells, preferred_element_type=F32)
        return picked.astype(BF)

    east_ref[0] = column(x_ref, last, 14)
    east_ref[1] = column(x_ref, last, 15)
    east_ref[2] = column(c_ref, last, 15)
    west_ref[0] = column(x_ref, first, 0)
    west_ref[1] = column(x_ref, first, 1)
    west_ref[2] = column(c_ref, first, 0)


def halo_chunks(from_west, from_east, size):
    halo = jnp.concatenate(
        [from_west[i] for i in range(3)] + [from_east[i] for i in range(3)], axis=0
    )
    shape = (ROWS * size, 96)
    row = iota(shape, 0) // size
    spot = iota(shape, 0) % size
    source = iota(shape, 1)

    def chunk(at):
        want = jnp.full(shape, -1, jnp.int32)
        for where, plane in at:
            want = jnp.where(spot == where, plane * 16 + row, want)
        pick = (source == want).astype(F32).astype(BF)
        picked = jnp.dot(pick, halo, preferred_element_type=F32)
        return [picked[r * size : r * size + size] for r in range(ROWS)]

    return (
        chunk([(0, 3), (1, 4), (size - 2, 0), (size - 1, 1)]),
        chunk([(0, 5), (size - 1, 2)]),
    )


def keep_cells(cells, column):
    return jnp.where(column > 0, cells.astype(F32), 0.0).astype(BF)


def line_kernel(x_ref, c_ref, from_west, from_east, fold_ref, pair_ref):
    x_chunk, c_chunk = halo_chunks(from_west, from_east, 8)
    even = lax.axis_index("lat") % 2 == 0

    def full(ref, r, chunk):
        return jnp.concatenate([ref[r].astype(F32), chunk[r]], axis=0)

    def pack(one, two, three):
        rest = jnp.concatenate([one[:, 128:], two[:, 128:]], axis=1)
        wide = jnp.concatenate([three[40:, 128:], jnp.zeros((80 - LINE, 64), F32)], axis=0)
        last = jnp.concatenate([three[:40, 128:], wide], axis=1)
        return jnp.concatenate([one[:, :128], two[:, :128], three[:, :128], rest, last], axis=0)

    top = pack(full(x_ref, 15, x_chunk), full(x_ref, 14, x_chunk), full(c_ref, 15, c_chunk))
    bottom = pack(full(x_ref, 0, x_chunk), full(x_ref, 1, x_chunk), full(c_ref, 0, c_chunk))
    fold_ref[...] = jnp.where(even, bottom, top).astype(BF)
    pair_ref[...] = jnp.where(even, top, bottom).astype(BF)


def lay(dest, base, rows):
    low = iota((16, C), 0) < 8
    none = jnp.zeros((16, C), F32)
    tails = [none] + [none if r is None else r[1].astype(F32) for r in rows] + [none]
    for k in range(-1, len(rows)):
        at = base + k * S
        if k >= 0:
            dest[at : at + COLS, :] = jnp.zeros((COLS, C), BF) if rows[k] is None else rows[k][0]
        dest[at + COLS : at + S, :] = jnp.where(low, tails[k + 1], tails[k + 2]).astype(BF)


def window(ref):
    return ref[0:COLS, :], ref[COLS:S, :]


def taps(ref, base, at, size, c, weights, sign, contract):
    total = None
    for r in range(3):
        start = base + at + sign * (r - 1) * S
        term = lax.dot_general(
            ref[start : start + size, :], weights[r](r, c),
            (((1,), (contract,)), ((), ())), preferred_element_type=F32,
        )
        total = term if total is None else total + term
    return total


def shifted(ys, at, size, sign):
    at = at + 8
    return (
        ys[0, at - sign : at - sign + size, :]
        + ys[1, at : at + size, :]
        + ys[2, at + sign : at + sign + size, :]
    )


def weight_terms(xe, base, go, xt, lo, span):
    for r in range(3):
        start = base + lo + (r - 1) * S
        xt[r * C : (r + 1) * C, :] = xe[start : start + span, :].T
    starts = [8 + lo - (c - 1) for c in range(3)]
    return [go[start : start + span, :].astype(BF) for start in starts]


def inner_kernel(
    x_ref, c_ref, kernel_ref, keep_ref, from_west, from_east,
    out_ref, sgrad_ref, part_ref, ga,
    xe, ce, go, ys, xt,
):
    keep_t = keep_ref[...]
    x_chunk, c_chunk = halo_chunks(from_west, from_east, 16)

    def own(ref, chunk):
        return [(ref[r], chunk[r]) for r in range(ROWS)]

    xe[0:LEAD, :] = jnp.zeros((LEAD, C), BF)
    xe[LEAD + ROWS * S :, :] = jnp.zeros((xe.shape[0] - LEAD - ROWS * S, C), BF)
    lay(xe, LEAD, own(x_ref, x_chunk))
    lay(ce, LEAD, own(c_ref, c_chunk))

    def weight(r, c):
        return kernel_ref[3 * r + c]

    plain = [weight] * 3
    for c in range(3):
        for k in range(3):
            at = 48 + k * 384
            ys[c, 8 + at : 8 + at + 384, :] = taps(xe, LEAD, at, 384, c, plain, 1, 0)
        ys[c, 1208:1216, :] = jnp.zeros((8, C), F32)
    go[...] = jnp.zeros_like(go)
    ga[0:64, :] = jnp.zeros((64, C), BF)
    for w in range(15):
        at, size = (w * S, S) if w else (64, 16)
        pre = shifted(ys, at, size, 1)
        s = jax.nn.sigmoid(pre)
        slope = s * (1.0 + pre * (1.0 - s))
        grad = (ce[LEAD + at : LEAD + at + size, :].astype(F32) * slope).astype(BF)
        ga[at : at + size, :] = grad
        if w:
            go[8 + at : 8 + at + COLS, :] = grad[0:COLS].astype(F32)
            kept = keep_t[:, w : w + 1]
            out_ref[0, w] = (kept * pre[0:COLS] * s[0:COLS]).astype(BF)
    for c in range(3):
        for k in range(3):
            at = 112 + k * 336
            ys[c, 8 + at : 8 + at + 336, :] = taps(ga, 0, at, 336, c, plain, -1, 1)
    for r in range(2, 14):
        sgrad_ref[0, r] = keep_cells(shifted(ys, r * S, COLS, -1), keep_t[:, r : r + 1])
    for r in (0, 15):
        out_ref[0, r] = jnp.zeros((COLS, C), BF)
    for r in (0, 1, 14, 15):
        sgrad_ref[0, r] = jnp.zeros((COLS, C), BF)
    moved = weight_terms(xe, LEAD, go, xt, 64, 1152)
    for c in range(3):
        part_ref[c] = jnp.dot(xt[...], moved[c], preferred_element_type=F32)


def far_of(kernel_ref, fold):
    def far_weight(r, c):
        return kernel_ref[jnp.where(fold, 8 - (3 * r + c), 3 * r + c)]

    return far_weight


def border_rows(fold, fold_ref, pair_ref, own_fold, own_pair):
    even = lax.axis_index("lat") % 2 == 0
    down = iota((LINE, LINE), 0)
    across = iota((LINE, LINE), 1)
    turned = ((down + across == COLS - 1) | (down + across == COLS - 1 + LINE)).astype(F32)
    straight = (down == across).astype(F32)
    turn = jnp.where(fold, turned, straight).astype(BF)

    def choose(a, b):
        return jnp.where(even, a[...].astype(F32), b[...].astype(F32))

    def split(message, turned_by=None):
        blocks = [message[i * LINE : (i + 1) * LINE] for i in range(4)]
        last = message[4 * LINE :]
        rows = [
            jnp.concatenate([blocks[0], blocks[3][:, 0:64]], axis=1),
            jnp.concatenate([blocks[1], blocks[3][:, 64:128]], axis=1),
            jnp.concatenate([
                blocks[2], jnp.concatenate([last[:, 0:64], last[0 : LINE - 40, 64:128]], axis=0)
            ], axis=1),
        ]
        if turned_by is not None:
            rows = [
                jnp.dot(turned_by, r.astype(BF), preferred_element_type=F32) for r in rows
            ]
        return [
            (r[0:COLS].astype(BF), jnp.concatenate([r[COLS:LINE], r[COLS:LINE]], axis=0))
            for r in rows
        ]

    south = split(choose(fold_ref, pair_ref))
    north = split(choose(pair_ref, fold_ref), turn)
    top = split(choose(own_pair, own_fold))
    bottom = split(choose(own_fold, own_pair))
    return south, bottom, top, north


def slope_at(ys, at, size):
    pre = shifted(ys, at, size, 1)
    s = jax.nn.sigmoid(pre)
    return pre, s, s * (1.0 + pre * (1.0 - s))


def row_parts(ga, slot):
    low = iota((16, C), 0) < 8
    east = ga[slot * S + COLS : slot * S + S, :].astype(F32)
    west = ga[(slot - 1) * S + COLS : slot * S, :].astype(F32)
    return ga[slot * S : slot * S + COLS, :], jnp.where(low, east, west).astype(BF)


def row_of(ga, slot, dest):
    dest[0:COLS, :], dest[COLS:S, :] = row_parts(ga, slot)


def pack_half(half, xt, moved, part_ref, dest):
    mine = pl.ds(pl.multiple_of(half * 288, 288), 288)
    tails = []
    for c in range(3):
        grad = jnp.dot(xt[mine, :], moved[c], preferred_element_type=F32) + part_ref[c, mine, :]
        dest[c * 288 : (c + 1) * 288, :] = grad[:, 0:128].astype(dest.dtype)
        tails.append(grad[:, 128:C])
    dest[864:1152, :] = jnp.concatenate(tails[0:2], axis=1).astype(dest.dtype)
    rest = jnp.concatenate([tails[2][0:144], tails[2][144:288]], axis=1)
    dest[1152:HALF, :] = rest.astype(dest.dtype)
    if dest.shape[0] > HALF:
        dest[HALF:, :] = jnp.zeros((dest.shape[0] - HALF, 128), dest.dtype)


def border_kernel(
    lat_count,
    fold_ref, pair_ref, own_fold, own_pair, kernel_ref, keep_ref, part_ref,
    edge_ref, gown_ref, give_ref, xt, moved_ref,
    xb, cb, ga, go, ys,
):
    fold = lax.axis_index("lat") == lat_count - 1
    keep_t = keep_ref[...]
    south, bottom, top, north = border_rows(fold, fold_ref, pair_ref, own_fold, own_pair)
    xb[0:S, :] = jnp.zeros((S, C), BF)
    xb[7 * S :, :] = jnp.zeros((xb.shape[0] - 7 * S, C), BF)
    lay(xb, S, [south[0], bottom[0], bottom[1], top[1], top[0], north[0]])
    lay(cb, S, [None, bottom[2], None, None, top[2], None])

    def weight(r, c):
        return kernel_ref[3 * r + c]

    for c in range(3):
        ys[c, 8 + 144 : 8 + 480, :] = taps(xb, 0, 144, 336, c, [weight] * 3, 1, 0)
        ys[c, 144:152, :] = jnp.zeros((8, C), F32)
        ys[c, 488:496, :] = jnp.zeros((8, C), F32)
    go[...] = jnp.zeros_like(go)
    for slot in (1, 2, 4, 5):
        at, size = (slot * S + COLS, 16) if slot in (1, 4) else (slot * S, S)
        pre, s, slope = slope_at(ys, at, size)
        grad = (cb[at : at + size, :].astype(F32) * slope).astype(BF)
        ga[at : at + size, :] = grad
        if slot in (2, 5):
            go[8 + at : 8 + at + COLS, :] = grad[0:COLS].astype(F32)
            r = 0 if slot == 2 else ROWS - 1
            kept = keep_t[:, r : r + 1]
            edge_ref[slot // 5] = (kept * pre[0:COLS] * s[0:COLS]).astype(BF)
    row_of(ga, 2, gown_ref.at[0])
    row_of(ga, 5, gown_ref.at[1])
    moved = weight_terms(xb, 0, go, xt, 144, 384)
    for c in range(3):
        moved_ref[c] = moved[c]
    pack_half(1 - lax.axis_index("core"), xt, moved, part_ref, give_ref)


def ghost_kernel(
    lat_count, fold_ref, pair_ref, own_fold, own_pair, kernel_ref,
    xt, moved_ref, part_ref, edge_ref, out_in,
    ghost_ref, hold_ref, out_ref, xb, cb, ga, ys, sems,
):
    del out_in
    copies = [
        pltpu.make_async_copy(edge_ref.at[i], out_ref.at[0, r], sems.at[i])
        for i, r in enumerate((0, ROWS - 1))
    ]
    for copy in copies:
        copy.start()
    pack_half(lax.axis_index("core"), xt, [moved_ref[c] for c in range(3)], part_ref, hold_ref)
    fold = lax.axis_index("lat") == lat_count - 1
    south, bottom, top, north = border_rows(fold, fold_ref, pair_ref, own_fold, own_pair)
    xb[0:S, :] = jnp.zeros((S, C), BF)
    xb[7 * S :, :] = jnp.zeros((xb.shape[0] - 7 * S, C), BF)
    lay(xb, S, [south[1], south[0], bottom[0], top[0], north[0], north[1]])
    lay(cb, S, [None, south[2], None, None, north[2], None])

    def weight(r, c):
        return kernel_ref[3 * r + c]

    far_weight = far_of(kernel_ref, fold)
    for c in range(3):
        ys[c, 152:248, :] = taps(xb, 0, 144, 96, c, [weight] * 3, 1, 0)
        ys[c, 392:488, :] = taps(xb, 0, 384, 96, c, [far_weight] * 3, 1, 0)
        for at in (144, 248, 384, 488):
            ys[c, at : at + 8, :] = jnp.zeros((8, C), F32)
    for at in (144, 384):
        grad = cb[at : at + 96, :].astype(F32) * slope_at(ys, at, 96)[2]
        ga[at : at + 96, :] = grad.astype(BF)
    row_of(ga, 2, ghost_ref.at[0])
    row_of(ga, 5, ghost_ref.at[1])
    for copy in copies:
        copy.wait()


def state_kernel(
    lat_count, inner_ref, gown_ref, ghost_ref, kernel_ref, keep_ref, sgrad_in,
    sgrad_ref, gb, ys, rows_out, sems,
):
    del sgrad_in
    fold = lax.axis_index("lat") == lat_count - 1
    keep_t = keep_ref[...]
    gb[0:S, :] = jnp.zeros((S, C), BF)
    gb[9 * S :, :] = jnp.zeros((gb.shape[0] - 9 * S, C), BF)
    lay(
        gb, S,
        [
            window(ghost_ref.at[0]), window(gown_ref.at[0]),
            row_parts(inner_ref, 1), row_parts(inner_ref, 2),
            row_parts(inner_ref, 13), row_parts(inner_ref, 14),
            window(gown_ref.at[1]), window(ghost_ref.at[1]),
        ],
    )

    def weight(r, c):
        return kernel_ref[3 * r + c]

    for c in range(3):
        ys[c, 8 + 144 : 8 + 640, :] = taps(gb, 0, 144, 496, c, [weight] * 3, -1, 1)
        edge = taps(gb, 0, 7 * S - 16, 96, c, [far_of(kernel_ref, fold), weight, weight], -1, 1)
        ys[c, 7 * S : 8 + 8 * S, :] = edge[8:]
    copies = []
    for i, (slot, r) in enumerate(((2, 0), (3, 1), (6, 14), (7, 15))):
        total = shifted(ys, slot * S, COLS, -1)
        rows_out[i] = keep_cells(total, keep_t[:, r : r + 1])
        copies.append(pltpu.make_async_copy(rows_out.at[i], sgrad_ref.at[0, r], sems.at[i]))
        copies[-1].start()
    for copy in copies:
        copy.wait()


def add_kernel(hold_ref, came_ref, out_ref):
    out_ref[...] = (hold_ref[...] + came_ref[...].astype(F32)).astype(BF)


def sum_kernel(parts_ref, out_ref):
    total = parts_ref[0].astype(F32)
    for i in range(1, parts_ref.shape[0]):
        total = total + parts_ref[i].astype(F32)
    total = total.astype(BF)
    for i in range(out_ref.shape[0]):
        out_ref[i] = total


def unpack_kernel(scale, mine_ref, other_ref, out_ref, held, sems):
    mine_first = lax.axis_index("core") == 0

    def get(half, at, size):
        a = mine_ref[at : at + size, :].astype(F32)
        b = other_ref[at : at + size, :].astype(F32)
        return jnp.where(mine_first == (half == 0), a, b) * scale

    pieces = (
        ((0, 0, 0, 192),),
        ((0, 192, 0, 96), (1, 0, 96, 96)),
        ((1, 96, 0, 192),),
    )
    one, two = get(0, 1152, 144), get(1, 1152, 144)
    rests = (
        ((0, one[:, 0:64]), (144, one[0:48, 64:128])),
        ((0, one[48:144, 64:128]), (96, two[0:96, 0:64])),
        ((0, two[96:144, 0:64]), (48, two[:, 64:128])),
    )
    copies = []
    for r in range(3):
        for half, source, at, size in pieces[r]:
            to = slice(at, at + size)
            for c in range(3):
                held[r, c, to, 0:128] = get(half, c * 288 + source, size)
            both = get(half, 864 + source, size)
            held[r, 0, to, 128:C] = both[:, 0:64]
            held[r, 1, to, 128:C] = both[:, 64:128]
        for at, rest in rests[r]:
            held[r, 2, at : at + rest.shape[0], 128:C] = rest
        copies.append(pltpu.make_async_copy(held.at[r], out_ref.at[r], sems.at[r]))
        copies[-1].start()
    for copy in copies:
        copy.wait()


def solution(mesh):
    lon_count, lat_count, dp_count = (mesh.shape[n] for n in ("lon", "lat", "dp"))
    z_count = lon_count // 4
    fine = Mesh(
        mesh.devices.reshape(z_count, 2, 2, lat_count, dp_count),
        ("z", "twin", "core", "lat", "dp"),
    )
    lon = ("z", "twin", "core")
    sheet = ("twin", "lat", "dp")
    sheet_count = 2 * lat_count * dp_count
    eastward = [(i, (i + 1) % lon_count) for i in range(lon_count)]
    westward = [(b, a) for a, b in eastward]
    lat_pairs, fold_pairs = [], []
    for b in range(lon_count):
        for a in range(lat_count):
            lat_pairs.append((b * lat_count + a, b * lat_count + (a ^ 1)))
            if a == lat_count - 1:
                fold_pairs.append((b * lat_count + a, (lon_count - 1 - b) * lat_count + a))
            elif a > 0:
                fold_pairs.append((b * lat_count + a, b * lat_count + (a + 1 if a % 2 else a - 1)))
    sheet_order = [[(i + sheet_count * 7 // 8) % sheet_count for i in range(sheet_count)]]
    z_order = [[(i + z_count // 2) % z_count for i in range(z_count)]]
    scale = 1.0 / math.sqrt(dp_count * lat_count * ROWS * lon_count * COLS)
    part = -(-HALF // (8 * sheet_count)) * 8
    half_rows = sheet_count * part
    smem = pl.BlockSpec(memory_space=pltpu.SMEM)
    vmem = pl.BlockSpec(memory_space=pltpu.VMEM)
    hbm = pl.BlockSpec(memory_space=pltpu.HBM)
    whole = jax.ShapeDtypeStruct((1, ROWS, COLS, C), BF)

    def shaped(shape, kind=BF):
        return jax.ShapeDtypeStruct(shape, kind)

    def call(kernel, name, ins, out_shape, outs, scratch=(), aliases=None, cost=0):
        return pl.pallas_call(
            kernel,
            out_shape=out_shape,
            in_specs=ins,
            out_specs=outs,
            scratch_shapes=list(scratch),
            input_output_aliases=aliases or {},
            compiler_params=pltpu.CompilerParams(vmem_limit_bytes=40 * 2**20),
            cost_estimate=pl.CostEstimate(
                flops=cost, bytes_accessed=2**20, transcendentals=0
            ) if cost else None,
            name=name,
        )

    def body(states, cotangent, kernel, land_mask, ocean_tiles):
        taps9 = kernel.reshape(9, C, C)
        cells = shaped((ROWS, COLS, C))
        east, west, x, c, keep = call(
            edge_kernel, "edges", [hbm] * 4,
            (shaped((3, ROWS, C)),) * 2 + (cells, cells, shaped((COLS, ROWS), F32)), (vmem,) * 5,
            scratch=[
                pltpu.VMEM((ROWS, COLS), jnp.int32),
                pltpu.SMEM(ocean_tiles.shape, jnp.int32),
                pltpu.SemaphoreType.DMA((4,)),
            ],
        )(*(pltpu.with_memory_space_constraint(v, pltpu.HBM)
            for v in (states, cotangent, land_mask, ocean_tiles)))
        from_west = lax.ppermute(east, lon, eastward)
        from_east = lax.ppermute(west, lon, westward)
        own_fold, own_pair = call(
            line_kernel, "lines", [vmem] * 4, (shaped((MESSAGE, 128)),) * 2, (vmem,) * 2,
        )(x, c, from_west, from_east)
        pair = lax.ppermute(own_pair, lon + ("lat",), lat_pairs)
        fold = lax.ppermute(own_fold, lon + ("lat",), fold_pairs)
        output, state_grad, sums, inner_grad = call(
            inner_kernel, "inner", [vmem] * 6,
            (whole, whole, shaped((3, 576, C), F32), shaped((15 * S, C))), (vmem,) * 4,
            scratch=[
                pltpu.VMEM((LEAD + ROWS * S + 32, C), BF),
                pltpu.VMEM((LEAD + ROWS * S, C), BF),
                pltpu.VMEM((8 + ROWS * S + 16, C), F32),
                pltpu.VMEM((3, ROWS * S + 16, C), F32),
                pltpu.VMEM((576, 1152), BF),
            ],
            cost=2 * 10**9,
        )(x, c, taps9, keep, from_west, from_east)
        lines = (fold, pair, own_fold, own_pair)
        edge, gown, give, xt, moved = call(
            lambda *refs: border_kernel(lat_count, *refs), "border", [vmem] * 7,
            (
                shaped((2, COLS, C)), shaped((2, S, C)), shaped((half_rows, 128)),
                shaped((576, 384)), shaped((3, 384, C)),
            ),
            (vmem,) * 5,
            scratch=[
                pltpu.VMEM((8 * S, C), BF),
                pltpu.VMEM((7 * S, C), BF),
                pltpu.VMEM((7 * S, C), BF),
                pltpu.VMEM((7 * S, C), F32),
                pltpu.VMEM((3, 7 * S + 16, C), F32),
            ],
            cost=5 * 10**8,
        )(*lines, taps9, keep, sums)
        came = lax.ppermute(give, "core", [(0, 1), (1, 0)])
        ghost, hold, output = call(
            lambda *refs: ghost_kernel(lat_count, *refs), "ghost", [vmem] * 9 + [hbm],
            (shaped((2, S, C)), shaped((half_rows, 128), F32), whole), (vmem, vmem, hbm),
            scratch=[
                pltpu.VMEM((8 * S, C), BF),
                pltpu.VMEM((7 * S, C), BF),
                pltpu.VMEM((7 * S, C), BF),
                pltpu.VMEM((3, 7 * S + 16, C), F32),
                pltpu.SemaphoreType.DMA((2,)),
            ],
            aliases={9: 2}, cost=5 * 10**8,
        )(*lines, taps9, xt, moved, sums, edge, output)
        state_grad = call(
            lambda *refs: state_kernel(lat_count, *refs), "state",
            [vmem] * 5 + [hbm], whole, hbm,
            scratch=[
                pltpu.VMEM((10 * S, C), BF),
                pltpu.VMEM((3, 8 * S + 16, C), F32),
                pltpu.VMEM((4, COLS, C), BF),
                pltpu.SemaphoreType.DMA((4,)),
            ],
            aliases={5: 0}, cost=5 * 10**8,
        )(inner_grad, gown, ghost, taps9, keep, state_grad)

        def summed(parts, copies):
            return call(sum_kernel, "sum", [vmem], shaped((copies, part, 128)), vmem)(parts)

        parts = call(add_kernel, "add", [vmem] * 2, shaped((half_rows, 128)), vmem)(hold, came)
        parts = lax.all_to_all(
            parts.reshape(sheet_count, part, 128), sheet, 0, 0, axis_index_groups=sheet_order, tiled=True
        )
        parts = lax.all_to_all(
            summed(parts, z_count), "z", 0, 0, axis_index_groups=z_order, tiled=True
        )
        parts = lax.all_to_all(
            summed(parts, sheet_count), sheet, 0, 0, axis_index_groups=sheet_order, tiled=True
        )
        mine = parts.reshape(half_rows, 128)
        other = lax.ppermute(mine, "core", [(0, 1), (1, 0)])
        weight_grad = call(
            lambda *refs: unpack_kernel(scale, *refs), "unpack", [vmem] * 2,
            shaped((3, 3, C, C), F32), hbm,
            scratch=[pltpu.VMEM((3, 3, C, C), F32), pltpu.SemaphoreType.DMA((3,))],
        )(mine, other)
        return output, state_grad, weight_grad

    cells = P("dp", "lat", lon, None)
    return jax.shard_map(
        body,
        mesh=fine,
        in_specs=(cells, cells, P(), P("lat", lon), P("lat", lon, None)),
        out_specs=(cells, cells, P()),
        check_vma=False,
    )
```

```python
import math

import jax
import jax.numpy as jnp
from jax import lax
from jax.experimental import pallas as pl
from jax.experimental.pallas import tpu as pltpu
from jax.sharding import Mesh
from jax.sharding import PartitionSpec as P

BF = jnp.bfloat16
F32 = jnp.float32
TS = 16
ROWS = 16
COLS = 64
C = 192
S = 80
LEAD = 32
LINE = 72
MESSAGE = 4 * LINE + 40
HALF = 1296


def iota(shape, dim):
    return lax.broadcasted_iota(jnp.int32, shape, dim)


def keep_plane(mask_ref, tiles_ref):
    tile = iota((ROWS, COLS), 1) // TS
    listed = jnp.zeros((ROWS, COLS), F32)
    for slot in range(tiles_ref.shape[-1]):
        listed = jnp.where(tile == tiles_ref[0, 0, slot], 1.0, listed)
    return jnp.where(mask_ref[...] > 0, listed, 0.0)


def edge_kernel(
    states_ref, cot_ref, mask_hbm, tiles_hbm, east_ref, west_ref, x_ref, c_ref, keep_ref,
    mask_ref, tiles_ref, sems,
):
    pairs = [
        (mask_hbm, mask_ref), (tiles_hbm, tiles_ref), (states_ref.at[0], x_ref), (cot_ref.at[0], c_ref),
    ]
    copies = [pltpu.make_async_copy(*pair, sems.at[i]) for i, pair in enumerate(pairs)]
    for copy in copies:
        copy.start()
    copies[0].wait()
    copies[1].wait()
    keep = keep_plane(mask_ref, tiles_ref)
    keep_ref[...] = keep.T
    picks = {}
    for spot in (0, 1, 14, 15):
        pick = iota((ROWS, 256), 1) == iota((ROWS, 256), 0) * 16 + spot
        picks[spot] = pick.astype(F32).astype(BF)

    def column(ref, spot, col):
        part = slice(col - spot, col - spot + 16)
        cells = jnp.concatenate([ref[r, part, :] for r in range(ROWS)], axis=0)
        picked = jnp.dot(picks[spot], cells, preferred_element_type=F32)
        return jnp.where(keep[:, col : col + 1] > 0, picked, 0.0).astype(BF)

    copies[2].wait()
    east_ref[0] = column(x_ref, 14, COLS - 2)
    east_ref[1] = column(x_ref, 15, COLS - 1)
    west_ref[0] = column(x_ref, 0, 0)
    west_ref[1] = column(x_ref, 1, 1)
    copies[3].wait()
    east_ref[2] = column(c_ref, 15, COLS - 1)
    west_ref[2] = column(c_ref, 0, 0)


def mask_kernel(x_in, c_in, keep_ref, x_ref, c_ref):
    keep_t = keep_ref[...]
    for r in range(ROWS):
        x_ref[r] = keep_cells(x_in[r], keep_t[:, r : r + 1])
        c_ref[r] = keep_cells(c_in[r], keep_t[:, r : r + 1])


def halo_chunks(from_west, from_east, size):
    halo = jnp.concatenate(
        [from_west[i] for i in range(3)] + [from_east[i] for i in range(3)], axis=0
    )
    shape = (ROWS * size, 96)
    row = iota(shape, 0) // size
    spot = iota(shape, 0) % size
    source = iota(shape, 1)

    def chunk(at):
        want = jnp.full(shape, -1, jnp.int32)
        for where, plane in at:
            want = jnp.where(spot == where, plane * 16 + row, want)
        pick = (source == want).astype(F32).astype(BF)
        picked = jnp.dot(pick, halo, preferred_element_type=F32)
        return [picked[r * size : r * size + size] for r in range(ROWS)]

    return (
        chunk([(0, 3), (1, 4), (size - 2, 0), (size - 1, 1)]),
        chunk([(0, 5), (size - 1, 2)]),
    )


def keep_cells(cells, column):
    return jnp.where(column > 0, cells.astype(F32), 0.0).astype(BF)


def line_kernel(x_ref, c_ref, from_west, from_east, fold_ref, pair_ref):
    x_chunk, c_chunk = halo_chunks(from_west, from_east, 8)
    even = lax.axis_index("lat") % 2 == 0

    def full(ref, r, chunk):
        return jnp.concatenate([ref[r].astype(F32), chunk[r]], axis=0)

    def pack(one, two, three):
        rest = jnp.concatenate([one[:, 128:], two[:, 128:]], axis=1)
        wide = jnp.concatenate([three[40:, 128:], jnp.zeros((80 - LINE, 64), F32)], axis=0)
        last = jnp.concatenate([three[:40, 128:], wide], axis=1)
        return jnp.concatenate([one[:, :128], two[:, :128], three[:, :128], rest, last], axis=0)

    top = pack(full(x_ref, 15, x_chunk), full(x_ref, 14, x_chunk), full(c_ref, 15, c_chunk))
    bottom = pack(full(x_ref, 0, x_chunk), full(x_ref, 1, x_chunk), full(c_ref, 0, c_chunk))
    fold_ref[...] = jnp.where(even, bottom, top).astype(BF)
    pair_ref[...] = jnp.where(even, top, bottom).astype(BF)


def lay(dest, base, rows):
    low = iota((16, C), 0) < 8
    none = jnp.zeros((16, C), F32)
    tails = [none] + [none if r is None else r[1].astype(F32) for r in rows] + [none]
    for k in range(-1, len(rows)):
        at = base + k * S
        if k >= 0:
            dest[at : at + COLS, :] = jnp.zeros((COLS, C), BF) if rows[k] is None else rows[k][0]
        dest[at + COLS : at + S, :] = jnp.where(low, tails[k + 1], tails[k + 2]).astype(BF)


def window(ref):
    return ref[0:COLS, :], ref[COLS:S, :]


def taps(ref, base, at, size, c, weights, sign, contract):
    total = None
    for r in range(3):
        start = base + at + sign * (r - 1) * S
        term = lax.dot_general(
            ref[start : start + size, :], weights[r](r, c),
            (((1,), (contract,)), ((), ())), preferred_element_type=F32,
        )
        total = term if total is None else total + term
    return total


def shifted(ys, at, size, sign):
    at = at + 8
    return (
        ys[0, at - sign : at - sign + size, :]
        + ys[1, at : at + size, :]
        + ys[2, at + sign : at + sign + size, :]
    )


def weight_terms(xe, base, go, xt, lo, span):
    for r in range(3):
        start = base + lo + (r - 1) * S
        xt[r * C : (r + 1) * C, :] = xe[start : start + span, :].T
    starts = [8 + lo - (c - 1) for c in range(3)]
    return [go[start : start + span, :].astype(BF) for start in starts]


def inner_kernel(
    x_ref, c_ref, kernel_ref, keep_ref, from_west, from_east,
    out_ref, sgrad_ref, part_ref, ga,
    xe, ce, go, ys, xt,
):
    keep_t = keep_ref[...]
    x_chunk, c_chunk = halo_chunks(from_west, from_east, 16)

    def own(ref, chunk):
        return [(ref[r], chunk[r]) for r in range(ROWS)]

    xe[0:LEAD, :] = jnp.zeros((LEAD, C), BF)
    xe[LEAD + ROWS * S :, :] = jnp.zeros((xe.shape[0] - LEAD - ROWS * S, C), BF)
    lay(xe, LEAD, own(x_ref, x_chunk))
    lay(ce, LEAD, own(c_ref, c_chunk))

    def weight(r, c):
        return kernel_ref[3 * r + c]

    plain = [weight] * 3
    for c in range(3):
        for k in range(3):
            at = 48 + k * 384
            ys[c, 8 + at : 8 + at + 384, :] = taps(xe, LEAD, at, 384, c, plain, 1, 0)
        ys[c, 1208:1216, :] = jnp.zeros((8, C), F32)
    go[...] = jnp.zeros_like(go)
    ga[0:64, :] = jnp.zeros((64, C), BF)
    for w in range(15):
        at, size = (w * S, S) if w else (64, 16)
        pre = shifted(ys, at, size, 1)
        s = jax.nn.sigmoid(pre)
        slope = s * (1.0 + pre * (1.0 - s))
        grad = (ce[LEAD + at : LEAD + at + size, :].astype(F32) * slope).astype(BF)
        ga[at : at + size, :] = grad
        if w:
            go[8 + at : 8 + at + COLS, :] = grad[0:COLS].astype(F32)
            kept = keep_t[:, w : w + 1]
            out_ref[0, w] = (kept * pre[0:COLS] * s[0:COLS]).astype(BF)
    for c in range(3):
        for k in range(3):
            at = 112 + k * 336
            ys[c, 8 + at : 8 + at + 336, :] = taps(ga, 0, at, 336, c, plain, -1, 1)
    for r in range(2, 14):
        sgrad_ref[0, r] = keep_cells(shifted(ys, r * S, COLS, -1), keep_t[:, r : r + 1])
    for r in (0, 15):
        out_ref[0, r] = jnp.zeros((COLS, C), BF)
    for r in (0, 1, 14, 15):
        sgrad_ref[0, r] = jnp.zeros((COLS, C), BF)
    moved = weight_terms(xe, LEAD, go, xt, 64, 1152)
    for c in range(3):
        part_ref[c] = jnp.dot(xt[...], moved[c], preferred_element_type=F32)


def far_of(kernel_ref, fold):
    def far_weight(r, c):
        return kernel_ref[jnp.where(fold, 8 - (3 * r + c), 3 * r + c)]

    return far_weight


def border_rows(fold, fold_ref, pair_ref, own_fold, own_pair):
    even = lax.axis_index("lat") % 2 == 0
    down = iota((LINE, LINE), 0)
    across = iota((LINE, LINE), 1)
    turned = ((down + across == COLS - 1) | (down + across == COLS - 1 + LINE)).astype(F32)
    straight = (down == across).astype(F32)
    turn = jnp.where(fold, turned, straight).astype(BF)

    def choose(a, b):
        return jnp.where(even, a[...].astype(F32), b[...].astype(F32))

    def split(message, turned_by=None):
        blocks = [message[i * LINE : (i + 1) * LINE] for i in range(4)]
        last = message[4 * LINE :]
        rows = [
            jnp.concatenate([blocks[0], blocks[3][:, 0:64]], axis=1),
            jnp.concatenate([blocks[1], blocks[3][:, 64:128]], axis=1),
            jnp.concatenate([
                blocks[2], jnp.concatenate([last[:, 0:64], last[0 : LINE - 40, 64:128]], axis=0)
            ], axis=1),
        ]
        if turned_by is not None:
            rows = [
                jnp.dot(turned_by, r.astype(BF), preferred_element_type=F32) for r in rows
            ]
        return [
            (r[0:COLS].astype(BF), jnp.concatenate([r[COLS:LINE], r[COLS:LINE]], axis=0))
            for r in rows
        ]

    south = split(choose(fold_ref, pair_ref))
    north = split(choose(pair_ref, fold_ref), turn)
    top = split(choose(own_pair, own_fold))
    bottom = split(choose(own_fold, own_pair))
    return south, bottom, top, north


def slope_at(ys, at, size):
    pre = shifted(ys, at, size, 1)
    s = jax.nn.sigmoid(pre)
    return pre, s, s * (1.0 + pre * (1.0 - s))


def row_parts(ga, slot):
    low = iota((16, C), 0) < 8
    east = ga[slot * S + COLS : slot * S + S, :].astype(F32)
    west = ga[(slot - 1) * S + COLS : slot * S, :].astype(F32)
    return ga[slot * S : slot * S + COLS, :], jnp.where(low, east, west).astype(BF)


def row_of(ga, slot, dest):
    dest[0:COLS, :], dest[COLS:S, :] = row_parts(ga, slot)


def pack_half(half, xt, moved, part_ref, dest):
    mine = pl.ds(pl.multiple_of(half * 288, 288), 288)
    tails = []
    for c in range(3):
        grad = jnp.dot(xt[mine, :], moved[c], preferred_element_type=F32) + part_ref[c, mine, :]
        dest[c * 288 : (c + 1) * 288, :] = grad[:, 0:128].astype(dest.dtype)
        tails.append(grad[:, 128:C])
    dest[864:1152, :] = jnp.concatenate(tails[0:2], axis=1).astype(dest.dtype)
    rest = jnp.concatenate([tails[2][0:144], tails[2][144:288]], axis=1)
    dest[1152:HALF, :] = rest.astype(dest.dtype)
    if dest.shape[0] > HALF:
        dest[HALF:, :] = jnp.zeros((dest.shape[0] - HALF, 128), dest.dtype)


def border_kernel(
    lat_count,
    fold_ref, pair_ref, own_fold, own_pair, kernel_ref, keep_ref, part_ref,
    edge_ref, gown_ref, give_ref, xt, moved_ref,
    xb, cb, ga, go, ys,
):
    fold = lax.axis_index("lat") == lat_count - 1
    keep_t = keep_ref[...]
    south, bottom, top, north = border_rows(fold, fold_ref, pair_ref, own_fold, own_pair)
    xb[0:S, :] = jnp.zeros((S, C), BF)
    xb[7 * S :, :] = jnp.zeros((xb.shape[0] - 7 * S, C), BF)
    lay(xb, S, [south[0], bottom[0], bottom[1], top[1], top[0], north[0]])
    lay(cb, S, [None, bottom[2], None, None, top[2], None])

    def weight(r, c):
        return kernel_ref[3 * r + c]

    for c in range(3):
        ys[c, 8 + 144 : 8 + 480, :] = taps(xb, 0, 144, 336, c, [weight] * 3, 1, 0)
        ys[c, 144:152, :] = jnp.zeros((8, C), F32)
        ys[c, 488:496, :] = jnp.zeros((8, C), F32)
    go[...] = jnp.zeros_like(go)
    for slot in (1, 2, 4, 5):
        at, size = (slot * S + COLS, 16) if slot in (1, 4) else (slot * S, S)
        pre, s, slope = slope_at(ys, at, size)
        grad = (cb[at : at + size, :].astype(F32) * slope).astype(BF)
        ga[at : at + size, :] = grad
        if slot in (2, 5):
            go[8 + at : 8 + at + COLS, :] = grad[0:COLS].astype(F32)
            r = 0 if slot == 2 else ROWS - 1
            kept = keep_t[:, r : r + 1]
            edge_ref[slot // 5] = (kept * pre[0:COLS] * s[0:COLS]).astype(BF)
    row_of(ga, 2, gown_ref.at[0])
    row_of(ga, 5, gown_ref.at[1])
    moved = weight_terms(xb, 0, go, xt, 144, 384)
    for c in range(3):
        moved_ref[c] = moved[c]
    pack_half(1 - lax.axis_index("core"), xt, moved, part_ref, give_ref)


def ghost_kernel(
    lat_count, fold_ref, pair_ref, own_fold, own_pair, kernel_ref,
    xt, moved_ref, part_ref, edge_ref, out_in,
    ghost_ref, hold_ref, out_ref, xb, cb, ga, ys, sems,
):
    del out_in
    copies = [
        pltpu.make_async_copy(edge_ref.at[i], out_ref.at[0, r], sems.at[i])
        for i, r in enumerate((0, ROWS - 1))
    ]
    for copy in copies:
        copy.start()
    pack_half(lax.axis_index("core"), xt, [moved_ref[c] for c in range(3)], part_ref, hold_ref)
    fold = lax.axis_index("lat") == lat_count - 1
    south, bottom, top, north = border_rows(fold, fold_ref, pair_ref, own_fold, own_pair)
    xb[0:S, :] = jnp.zeros((S, C), BF)
    xb[7 * S :, :] = jnp.zeros((xb.shape[0] - 7 * S, C), BF)
    lay(xb, S, [south[1], south[0], bottom[0], top[0], north[0], north[1]])
    lay(cb, S, [None, south[2], None, None, north[2], None])

    def weight(r, c):
        return kernel_ref[3 * r + c]

    far_weight = far_of(kernel_ref, fold)
    for c in range(3):
        ys[c, 152:248, :] = taps(xb, 0, 144, 96, c, [weight] * 3, 1, 0)
        ys[c, 392:488, :] = taps(xb, 0, 384, 96, c, [far_weight] * 3, 1, 0)
        for at in (144, 248, 384, 488):
            ys[c, at : at + 8, :] = jnp.zeros((8, C), F32)
    for at in (144, 384):
        grad = cb[at : at + 96, :].astype(F32) * slope_at(ys, at, 96)[2]
        ga[at : at + 96, :] = grad.astype(BF)
    row_of(ga, 2, ghost_ref.at[0])
    row_of(ga, 5, ghost_ref.at[1])
    for copy in copies:
        copy.wait()


def state_kernel(
    lat_count, inner_ref, gown_ref, ghost_ref, kernel_ref, keep_ref, sgrad_in,
    sgrad_ref, gb, ys, rows_out, sems,
):
    del sgrad_in
    fold = lax.axis_index("lat") == lat_count - 1
    keep_t = keep_ref[...]
    gb[0:S, :] = jnp.zeros((S, C), BF)
    gb[9 * S :, :] = jnp.zeros((gb.shape[0] - 9 * S, C), BF)
    lay(
        gb, S,
        [
            window(ghost_ref.at[0]), window(gown_ref.at[0]),
            row_parts(inner_ref, 1), row_parts(inner_ref, 2),
            row_parts(inner_ref, 13), row_parts(inner_ref, 14),
            window(gown_ref.at[1]), window(ghost_ref.at[1]),
        ],
    )

    def weight(r, c):
        return kernel_ref[3 * r + c]

    for c in range(3):
        ys[c, 8 + 144 : 8 + 640, :] = taps(gb, 0, 144, 496, c, [weight] * 3, -1, 1)
        edge = taps(gb, 0, 7 * S - 16, 96, c, [far_of(kernel_ref, fold), weight, weight], -1, 1)
        ys[c, 7 * S : 8 + 8 * S, :] = edge[8:]
    copies = []
    for i, (slot, r) in enumerate(((2, 0), (3, 1), (6, 14), (7, 15))):
        total = shifted(ys, slot * S, COLS, -1)
        rows_out[i] = keep_cells(total, keep_t[:, r : r + 1])
        copies.append(pltpu.make_async_copy(rows_out.at[i], sgrad_ref.at[0, r], sems.at[i]))
        copies[-1].start()
    for copy in copies:
        copy.wait()


def add_kernel(hold_ref, came_ref, out_ref):
    out_ref[...] = (hold_ref[...] + came_ref[...].astype(F32)).astype(BF)


def sum_kernel(parts_ref, out_ref):
    total = parts_ref[0].astype(F32)
    for i in range(1, parts_ref.shape[0]):
        total = total + parts_ref[i].astype(F32)
    total = total.astype(BF)
    for i in range(out_ref.shape[0]):
        out_ref[i] = total


def unpack_kernel(scale, mine_ref, other_ref, out_ref, held, sems):
    mine_first = lax.axis_index("core") == 0

    def get(half, at, size):
        a = mine_ref[at : at + size, :].astype(F32)
        b = other_ref[at : at + size, :].astype(F32)
        return jnp.where(mine_first == (half == 0), a, b) * scale

    pieces = (
        ((0, 0, 0, 192),),
        ((0, 192, 0, 96), (1, 0, 96, 96)),
        ((1, 96, 0, 192),),
    )
    one, two = get(0, 1152, 144), get(1, 1152, 144)
    rests = (
        ((0, one[:, 0:64]), (144, one[0:48, 64:128])),
        ((0, one[48:144, 64:128]), (96, two[0:96, 0:64])),
        ((0, two[96:144, 0:64]), (48, two[:, 64:128])),
    )
    copies = []
    for r in range(3):
        for half, source, at, size in pieces[r]:
            to = slice(at, at + size)
            for c in range(3):
                held[r, c, to, 0:128] = get(half, c * 288 + source, size)
            both = get(half, 864 + source, size)
            held[r, 0, to, 128:C] = both[:, 0:64]
            held[r, 1, to, 128:C] = both[:, 64:128]
        for at, rest in rests[r]:
            held[r, 2, at : at + rest.shape[0], 128:C] = rest
        copies.append(pltpu.make_async_copy(held.at[r], out_ref.at[r], sems.at[r]))
        copies[-1].start()
    for copy in copies:
        copy.wait()


def solution(mesh):
    lon_count, lat_count, dp_count = (mesh.shape[n] for n in ("lon", "lat", "dp"))
    z_count = lon_count // 4
    fine = Mesh(
        mesh.devices.reshape(z_count, 2, 2, lat_count, dp_count),
        ("z", "twin", "core", "lat", "dp"),
    )
    lon = ("z", "twin", "core")
    sheet = ("twin", "lat", "dp")
    sheet_count = 2 * lat_count * dp_count
    eastward = [(i, (i + 1) % lon_count) for i in range(lon_count)]
    westward = [(b, a) for a, b in eastward]
    lat_pairs, fold_pairs = [], []
    for b in range(lon_count):
        for a in range(lat_count):
            lat_pairs.append((b * lat_count + a, b * lat_count + (a ^ 1)))
            if a == lat_count - 1:
                fold_pairs.append((b * lat_count + a, (lon_count - 1 - b) * lat_count + a))
            elif a > 0:
                fold_pairs.append((b * lat_count + a, b * lat_count + (a + 1 if a % 2 else a - 1)))
    sheet_order = [[(i + sheet_count * 7 // 8) % sheet_count for i in range(sheet_count)]]
    z_order = [[(i + z_count // 2) % z_count for i in range(z_count)]]
    scale = 1.0 / math.sqrt(dp_count * lat_count * ROWS * lon_count * COLS)
    part = -(-HALF // (8 * sheet_count)) * 8
    half_rows = sheet_count * part
    smem = pl.BlockSpec(memory_space=pltpu.SMEM)
    vmem = pl.BlockSpec(memory_space=pltpu.VMEM)
    hbm = pl.BlockSpec(memory_space=pltpu.HBM)
    whole = jax.ShapeDtypeStruct((1, ROWS, COLS, C), BF)

    def shaped(shape, kind=BF):
        return jax.ShapeDtypeStruct(shape, kind)

    def call(kernel, name, ins, out_shape, outs, scratch=(), aliases=None, cost=0):
        return pl.pallas_call(
            kernel,
            out_shape=out_shape,
            in_specs=ins,
            out_specs=outs,
            scratch_shapes=list(scratch),
            input_output_aliases=aliases or {},
            compiler_params=pltpu.CompilerParams(vmem_limit_bytes=40 * 2**20),
            cost_estimate=pl.CostEstimate(
                flops=cost, bytes_accessed=2**20, transcendentals=0
            ) if cost else None,
            name=name,
        )

    def body(states, cotangent, kernel, land_mask, ocean_tiles):
        taps9 = kernel.reshape(9, C, C)
        cells = shaped((ROWS, COLS, C))
        east, west, x_raw, c_raw, keep = call(
            edge_kernel, "edges", [hbm] * 4,
            (shaped((3, ROWS, C)),) * 2 + (cells, cells, shaped((COLS, ROWS), F32)), (vmem,) * 5,
            scratch=[
                pltpu.VMEM((ROWS, COLS), jnp.int32),
                pltpu.SMEM(ocean_tiles.shape, jnp.int32),
                pltpu.SemaphoreType.DMA((4,)),
            ],
        )(*(pltpu.with_memory_space_constraint(v, pltpu.HBM)
            for v in (states, cotangent, land_mask, ocean_tiles)))
        from_west = lax.ppermute(east, lon, eastward)
        from_east = lax.ppermute(west, lon, westward)
        x, c = call(
            mask_kernel, "mask", [vmem] * 3, (cells, cells), (vmem,) * 2, cost=10**8,
        )(x_raw, c_raw, keep)
        own_fold, own_pair = call(
            line_kernel, "lines", [vmem] * 4, (shaped((MESSAGE, 128)),) * 2, (vmem,) * 2,
        )(x, c, from_west, from_east)
        pair = lax.ppermute(own_pair, lon + ("lat",), lat_pairs)
        fold = lax.ppermute(own_fold, lon + ("lat",), fold_pairs)
        output, state_grad, sums, inner_grad = call(
            inner_kernel, "inner", [vmem] * 6,
            (whole, whole, shaped((3, 576, C), F32), shaped((15 * S, C))), (vmem,) * 4,
            scratch=[
                pltpu.VMEM((LEAD + ROWS * S + 32, C), BF),
                pltpu.VMEM((LEAD + ROWS * S, C), BF),
                pltpu.VMEM((8 + ROWS * S + 16, C), F32),
                pltpu.VMEM((3, ROWS * S + 16, C), F32),
                pltpu.VMEM((576, 1152), BF),
            ],
            cost=2 * 10**9,
        )(x, c, taps9, keep, from_west, from_east)
        lines = (fold, pair, own_fold, own_pair)
        edge, gown, give, xt, moved = call(
            lambda *refs: border_kernel(lat_count, *refs), "border", [vmem] * 7,
            (
                shaped((2, COLS, C)), shaped((2, S, C)), shaped((half_rows, 128)),
                shaped((576, 384)), shaped((3, 384, C)),
            ),
            (vmem,) * 5,
            scratch=[
                pltpu.VMEM((8 * S, C), BF),
                pltpu.VMEM((7 * S, C), BF),
                pltpu.VMEM((7 * S, C), BF),
                pltpu.VMEM((7 * S, C), F32),
                pltpu.VMEM((3, 7 * S + 16, C), F32),
            ],
            cost=5 * 10**8,
        )(*lines, taps9, keep, sums)
        came = lax.ppermute(give, "core", [(0, 1), (1, 0)])
        ghost, hold, output = call(
            lambda *refs: ghost_kernel(lat_count, *refs), "ghost", [vmem] * 9 + [hbm],
            (shaped((2, S, C)), shaped((half_rows, 128), F32), whole), (vmem, vmem, hbm),
            scratch=[
                pltpu.VMEM((8 * S, C), BF),
                pltpu.VMEM((7 * S, C), BF),
                pltpu.VMEM((7 * S, C), BF),
                pltpu.VMEM((3, 7 * S + 16, C), F32),
                pltpu.SemaphoreType.DMA((2,)),
            ],
            aliases={9: 2}, cost=5 * 10**8,
        )(*lines, taps9, xt, moved, sums, edge, output)
        state_grad = call(
            lambda *refs: state_kernel(lat_count, *refs), "state",
            [vmem] * 5 + [hbm], whole, hbm,
            scratch=[
                pltpu.VMEM((10 * S, C), BF),
                pltpu.VMEM((3, 8 * S + 16, C), F32),
                pltpu.VMEM((4, COLS, C), BF),
                pltpu.SemaphoreType.DMA((4,)),
            ],
            aliases={5: 0}, cost=5 * 10**8,
        )(inner_grad, gown, ghost, taps9, keep, state_grad)

        def summed(parts, copies):
            return call(sum_kernel, "sum", [vmem], shaped((copies, part, 128)), vmem)(parts)

        parts = call(add_kernel, "add", [vmem] * 2, shaped((half_rows, 128)), vmem)(hold, came)
        parts = lax.all_to_all(
            parts.reshape(sheet_count, part, 128), sheet, 0, 0, axis_index_groups=sheet_order, tiled=True
        )
        parts = lax.all_to_all(
            summed(parts, z_count), "z", 0, 0, axis_index_groups=z_order, tiled=True
        )
        parts = lax.all_to_all(
            summed(parts, sheet_count), sheet, 0, 0, axis_index_groups=sheet_order, tiled=True
        )
        mine = parts.reshape(half_rows, 128)
        other = lax.ppermute(mine, "core", [(0, 1), (1, 0)])
        weight_grad = call(
            lambda *refs: unpack_kernel(scale, *refs), "unpack", [vmem] * 2,
            shaped((3, 3, C, C), F32), hbm,
            scratch=[pltpu.VMEM((3, 3, C, C), F32), pltpu.SemaphoreType.DMA((3,))],
        )(mine, other)
        return output, state_grad, weight_grad

    cells = P("dp", "lat", lon, None)
    return jax.shard_map(
        body,
        mesh=fine,
        in_specs=(cells, cells, P(), P("lat", lon), P("lat", lon, None)),
        out_specs=(cells, cells, P()),
        check_vma=False,
    )
```

```python
import math

import jax
import jax.numpy as jnp
from jax import lax
from jax.experimental import pallas as pl
from jax.experimental.pallas import tpu as pltpu
from jax.sharding import Mesh
from jax.sharding import PartitionSpec as P

BF = jnp.bfloat16
F32 = jnp.float32
TS = 16
ROWS = 16
COLS = 64
C = 192
S = 80
LEAD = 32
LINE = 72
MESSAGE = 4 * LINE + 40
HALF = 1296


def iota(shape, dim):
    return lax.broadcasted_iota(jnp.int32, shape, dim)


def keep_plane(mask_ref, tiles_ref):
    tile = iota((ROWS, COLS), 1) // TS
    listed = jnp.zeros((ROWS, COLS), F32)
    for slot in range(tiles_ref.shape[-1]):
        listed = jnp.where(tile == tiles_ref[0, 0, slot], 1.0, listed)
    return jnp.where(mask_ref[...] > 0, listed, 0.0)


def edge_kernel(
    states_ref, cot_ref, mask_hbm, tiles_hbm, east_ref, west_ref, x_ref, c_ref, keep_ref,
    mask_ref, tiles_ref, sems,
):
    pairs = [
        (mask_hbm, mask_ref), (tiles_hbm, tiles_ref), (states_ref.at[0], x_ref), (cot_ref.at[0], c_ref),
    ]
    copies = [pltpu.make_async_copy(*pair, sems.at[i]) for i, pair in enumerate(pairs)]
    for copy in copies:
        copy.start()
    copies[0].wait()
    copies[1].wait()
    keep = keep_plane(mask_ref, tiles_ref)
    keep_ref[...] = keep.T
    picks = {}
    for spot in (0, 1, 14, 15):
        pick = iota((ROWS, 256), 1) == iota((ROWS, 256), 0) * 16 + spot
        picks[spot] = pick.astype(F32).astype(BF)

    def column(ref, spot, col):
        part = slice(col - spot, col - spot + 16)
        cells = jnp.concatenate([ref[r, part, :] for r in range(ROWS)], axis=0)
        picked = jnp.dot(picks[spot], cells, preferred_element_type=F32)
        return jnp.where(keep[:, col : col + 1] > 0, picked, 0.0).astype(BF)

    copies[2].wait()
    east_ref[0] = column(x_ref, 14, COLS - 2)
    east_ref[1] = column(x_ref, 15, COLS - 1)
    west_ref[0] = column(x_ref, 0, 0)
    west_ref[1] = column(x_ref, 1, 1)
    copies[3].wait()
    east_ref[2] = column(c_ref, 15, COLS - 1)
    west_ref[2] = column(c_ref, 0, 0)


def mask_kernel(x_in, c_in, keep_ref, x_ref, c_ref):
    keep_t = keep_ref[...]
    for r in range(ROWS):
        x_ref[r] = keep_cells(x_in[r], keep_t[:, r : r + 1])
        c_ref[r] = keep_cells(c_in[r], keep_t[:, r : r + 1])


def halo_chunks(from_west, from_east, size):
    halo = jnp.concatenate(
        [from_west[i] for i in range(3)] + [from_east[i] for i in range(3)], axis=0
    )
    shape = (ROWS * size, 96)
    row = iota(shape, 0) // size
    spot = iota(shape, 0) % size
    source = iota(shape, 1)

    def chunk(at):
        want = jnp.full(shape, -1, jnp.int32)
        for where, plane in at:
            want = jnp.where(spot == where, plane * 16 + row, want)
        pick = (source == want).astype(F32).astype(BF)
        picked = jnp.dot(pick, halo, preferred_element_type=F32)
        return [picked[r * size : r * size + size] for r in range(ROWS)]

    return (
        chunk([(0, 3), (1, 4), (size - 2, 0), (size - 1, 1)]),
        chunk([(0, 5), (size - 1, 2)]),
    )


def keep_cells(cells, column):
    return jnp.where(column > 0, cells.astype(F32), 0.0).astype(BF)


def line_kernel(x_ref, c_ref, from_west, from_east, fold_ref, pair_ref):
    x_chunk, c_chunk = halo_chunks(from_west, from_east, 8)
    even = lax.axis_index("lat") % 2 == 0

    def full(ref, r, chunk):
        return jnp.concatenate([ref[r].astype(F32), chunk[r]], axis=0)

    def pack(one, two, three):
        rest = jnp.concatenate([one[:, 128:], two[:, 128:]], axis=1)
        wide = jnp.concatenate([three[40:, 128:], jnp.zeros((80 - LINE, 64), F32)], axis=0)
        last = jnp.concatenate([three[:40, 128:], wide], axis=1)
        return jnp.concatenate([one[:, :128], two[:, :128], three[:, :128], rest, last], axis=0)

    top = pack(full(x_ref, 15, x_chunk), full(x_ref, 14, x_chunk), full(c_ref, 15, c_chunk))
    bottom = pack(full(x_ref, 0, x_chunk), full(x_ref, 1, x_chunk), full(c_ref, 0, c_chunk))
    fold_ref[...] = jnp.where(even, bottom, top).astype(BF)
    pair_ref[...] = jnp.where(even, top, bottom).astype(BF)


def lay(dest, base, rows):
    low = iota((16, C), 0) < 8
    none = jnp.zeros((16, C), F32)
    tails = [none] + [none if r is None else r[1].astype(F32) for r in rows] + [none]
    for k in range(-1, len(rows)):
        at = base + k * S
        if k >= 0:
            dest[at : at + COLS, :] = jnp.zeros((COLS, C), BF) if rows[k] is None else rows[k][0]
        dest[at + COLS : at + S, :] = jnp.where(low, tails[k + 1], tails[k + 2]).astype(BF)


def window(ref):
    return ref[0:COLS, :], ref[COLS:S, :]


def taps(ref, base, at, size, c, weights, sign, contract):
    total = None
    for r in range(3):
        start = base + at + sign * (r - 1) * S
        term = lax.dot_general(
            ref[start : start + size, :], weights[r](r, c),
            (((1,), (contract,)), ((), ())), preferred_element_type=F32,
        )
        total = term if total is None else total + term
    return total


def shifted(ys, at, size, sign):
    at = at + 8
    return (
        ys[0, at - sign : at - sign + size, :]
        + ys[1, at : at + size, :]
        + ys[2, at + sign : at + sign + size, :]
    )


def weight_terms(xe, base, go, xt, lo, span):
    for r in range(3):
        start = base + lo + (r - 1) * S
        xt[r * C : (r + 1) * C, :] = xe[start : start + span, :].T
    starts = [8 + lo - (c - 1) for c in range(3)]
    return [go[start : start + span, :].astype(BF) for start in starts]


def inner_kernel(
    x_ref, c_ref, kernel_ref, keep_ref, from_west, from_east,
    out_ref, sgrad_ref, part_ref, ga,
    xe, ce, go, ys, xt,
):
    keep_t = keep_ref[...]
    x_chunk, c_chunk = halo_chunks(from_west, from_east, 16)

    def own(ref, chunk):
        return [(ref[r], chunk[r]) for r in range(ROWS)]

    xe[0:LEAD, :] = jnp.zeros((LEAD, C), BF)
    xe[LEAD + ROWS * S :, :] = jnp.zeros((xe.shape[0] - LEAD - ROWS * S, C), BF)
    lay(xe, LEAD, own(x_ref, x_chunk))
    lay(ce, LEAD, own(c_ref, c_chunk))

    def weight(r, c):
        return kernel_ref[3 * r + c]

    plain = [weight] * 3
    for c in range(3):
        for k in range(3):
            at = 48 + k * 384
            ys[c, 8 + at : 8 + at + 384, :] = taps(xe, LEAD, at, 384, c, plain, 1, 0)
        ys[c, 1208:1216, :] = jnp.zeros((8, C), F32)
    go[...] = jnp.zeros_like(go)
    ga[0:64, :] = jnp.zeros((64, C), BF)
    for w in range(15):
        at, size = (w * S, S) if w else (64, 16)
        pre = shifted(ys, at, size, 1)
        s = jax.nn.sigmoid(pre)
        slope = s * (1.0 + pre * (1.0 - s))
        grad = (ce[LEAD + at : LEAD + at + size, :].astype(F32) * slope).astype(BF)
        ga[at : at + size, :] = grad
        if w:
            go[8 + at : 8 + at + COLS, :] = grad[0:COLS].astype(F32)
            kept = keep_t[:, w : w + 1]
            out_ref[0, w] = (kept * pre[0:COLS] * s[0:COLS]).astype(BF)
    for c in range(3):
        for k in range(3):
            at = 112 + k * 336
            ys[c, 8 + at : 8 + at + 336, :] = taps(ga, 0, at, 336, c, plain, -1, 1)
    for r in range(2, 14):
        sgrad_ref[0, r] = keep_cells(shifted(ys, r * S, COLS, -1), keep_t[:, r : r + 1])
    for r in (0, 15):
        out_ref[0, r] = jnp.zeros((COLS, C), BF)
    for r in (0, 1, 14, 15):
        sgrad_ref[0, r] = jnp.zeros((COLS, C), BF)
    moved = weight_terms(xe, LEAD, go, xt, 64, 1152)
    for c in range(3):
        part_ref[c] = jnp.dot(xt[...], moved[c], preferred_element_type=F32)


def far_of(kernel_ref, fold):
    def far_weight(r, c):
        return kernel_ref[jnp.where(fold, 8 - (3 * r + c), 3 * r + c)]

    return far_weight


def border_rows(fold, fold_ref, pair_ref, own_fold, own_pair):
    even = lax.axis_index("lat") % 2 == 0
    down = iota((LINE, LINE), 0)
    across = iota((LINE, LINE), 1)
    turned = ((down + across == COLS - 1) | (down + across == COLS - 1 + LINE)).astype(F32)
    straight = (down == across).astype(F32)
    turn = jnp.where(fold, turned, straight).astype(BF)

    def choose(a, b):
        return jnp.where(even, a[...].astype(F32), b[...].astype(F32))

    def split(message, turned_by=None):
        blocks = [message[i * LINE : (i + 1) * LINE] for i in range(4)]
        last = message[4 * LINE :]
        rows = [
            jnp.concatenate([blocks[0], blocks[3][:, 0:64]], axis=1),
            jnp.concatenate([blocks[1], blocks[3][:, 64:128]], axis=1),
            jnp.concatenate([
                blocks[2], jnp.concatenate([last[:, 0:64], last[0 : LINE - 40, 64:128]], axis=0)
            ], axis=1),
        ]
        if turned_by is not None:
            rows = [
                jnp.dot(turned_by, r.astype(BF), preferred_element_type=F32) for r in rows
            ]
        return [
            (r[0:COLS].astype(BF), jnp.concatenate([r[COLS:LINE], r[COLS:LINE]], axis=0))
            for r in rows
        ]

    south = split(choose(fold_ref, pair_ref))
    north = split(choose(pair_ref, fold_ref), turn)
    top = split(choose(own_pair, own_fold))
    bottom = split(choose(own_fold, own_pair))
    return south, bottom, top, north


def slope_at(ys, at, size):
    pre = shifted(ys, at, size, 1)
    s = jax.nn.sigmoid(pre)
    return pre, s, s * (1.0 + pre * (1.0 - s))


def row_parts(ga, slot):
    low = iota((16, C), 0) < 8
    east = ga[slot * S + COLS : slot * S + S, :].astype(F32)
    west = ga[(slot - 1) * S + COLS : slot * S, :].astype(F32)
    return ga[slot * S : slot * S + COLS, :], jnp.where(low, east, west).astype(BF)


def row_of(ga, slot, dest):
    dest[0:COLS, :], dest[COLS:S, :] = row_parts(ga, slot)


def pack_half(half, xt, moved, part_ref, dest):
    mine = pl.ds(pl.multiple_of(half * 288, 288), 288)
    tails = []
    for c in range(3):
        grad = jnp.dot(xt[mine, :], moved[c], preferred_element_type=F32) + part_ref[c, mine, :]
        dest[c * 288 : (c + 1) * 288, :] = grad[:, 0:128].astype(dest.dtype)
        tails.append(grad[:, 128:C])
    dest[864:1152, :] = jnp.concatenate(tails[0:2], axis=1).astype(dest.dtype)
    rest = jnp.concatenate([tails[2][0:144], tails[2][144:288]], axis=1)
    dest[1152:HALF, :] = rest.astype(dest.dtype)
    if dest.shape[0] > HALF:
        dest[HALF:, :] = jnp.zeros((dest.shape[0] - HALF, 128), dest.dtype)


def border_kernel(
    lat_count,
    fold_ref, pair_ref, own_fold, own_pair, kernel_ref, keep_ref, part_ref,
    edge_ref, gown_ref, give_ref, xt, moved_ref,
    xb, cb, ga, go, ys,
):
    fold = lax.axis_index("lat") == lat_count - 1
    keep_t = keep_ref[...]
    south, bottom, top, north = border_rows(fold, fold_ref, pair_ref, own_fold, own_pair)
    xb[0:S, :] = jnp.zeros((S, C), BF)
    xb[7 * S :, :] = jnp.zeros((xb.shape[0] - 7 * S, C), BF)
    lay(xb, S, [south[0], bottom[0], bottom[1], top[1], top[0], north[0]])
    lay(cb, S, [None, bottom[2], None, None, top[2], None])

    def weight(r, c):
        return kernel_ref[3 * r + c]

    for c in range(3):
        ys[c, 8 + 144 : 8 + 480, :] = taps(xb, 0, 144, 336, c, [weight] * 3, 1, 0)
        ys[c, 144:152, :] = jnp.zeros((8, C), F32)
        ys[c, 488:496, :] = jnp.zeros((8, C), F32)
    go[...] = jnp.zeros_like(go)
    for slot in (1, 2, 4, 5):
        at, size = (slot * S + COLS, 16) if slot in (1, 4) else (slot * S, S)
        pre, s, slope = slope_at(ys, at, size)
        grad = (cb[at : at + size, :].astype(F32) * slope).astype(BF)
        ga[at : at + size, :] = grad
        if slot in (2, 5):
            go[8 + at : 8 + at + COLS, :] = grad[0:COLS].astype(F32)
            r = 0 if slot == 2 else ROWS - 1
            kept = keep_t[:, r : r + 1]
            edge_ref[slot // 5] = (kept * pre[0:COLS] * s[0:COLS]).astype(BF)
    row_of(ga, 2, gown_ref.at[0])
    row_of(ga, 5, gown_ref.at[1])
    moved = weight_terms(xb, 0, go, xt, 144, 384)
    for c in range(3):
        moved_ref[c] = moved[c]
    pack_half(1 - lax.axis_index("core"), xt, moved, part_ref, give_ref)


def ghost_kernel(
    lat_count, fold_ref, pair_ref, own_fold, own_pair, kernel_ref,
    xt, moved_ref, part_ref, edge_ref, out_in,
    ghost_ref, hold_ref, out_ref, xb, cb, ga, ys, sems,
):
    del out_in
    copies = [
        pltpu.make_async_copy(edge_ref.at[i], out_ref.at[0, r], sems.at[i])
        for i, r in enumerate((0, ROWS - 1))
    ]
    for copy in copies:
        copy.start()
    pack_half(lax.axis_index("core"), xt, [moved_ref[c] for c in range(3)], part_ref, hold_ref)
    fold = lax.axis_index("lat") == lat_count - 1
    south, bottom, top, north = border_rows(fold, fold_ref, pair_ref, own_fold, own_pair)
    xb[0:S, :] = jnp.zeros((S, C), BF)
    xb[7 * S :, :] = jnp.zeros((xb.shape[0] - 7 * S, C), BF)
    lay(xb, S, [south[1], south[0], bottom[0], top[0], north[0], north[1]])
    lay(cb, S, [None, south[2], None, None, north[2], None])

    def weight(r, c):
        return kernel_ref[3 * r + c]

    far_weight = far_of(kernel_ref, fold)
    for c in range(3):
        ys[c, 152:248, :] = taps(xb, 0, 144, 96, c, [weight] * 3, 1, 0)
        ys[c, 392:488, :] = taps(xb, 0, 384, 96, c, [far_weight] * 3, 1, 0)
        for at in (144, 248, 384, 488):
            ys[c, at : at + 8, :] = jnp.zeros((8, C), F32)
    for at in (144, 384):
        grad = cb[at : at + 96, :].astype(F32) * slope_at(ys, at, 96)[2]
        ga[at : at + 96, :] = grad.astype(BF)
    row_of(ga, 2, ghost_ref.at[0])
    row_of(ga, 5, ghost_ref.at[1])
    for copy in copies:
        copy.wait()


def state_rows(
    lat_count, inner_ref, gown_ref, ghost_ref, kernel_ref, keep_ref, sgrad_ref, gb, ys, rows_out,
    sems,
):
    fold = lax.axis_index("lat") == lat_count - 1
    keep_t = keep_ref[...]
    gb[0:S, :] = jnp.zeros((S, C), BF)
    gb[9 * S :, :] = jnp.zeros((gb.shape[0] - 9 * S, C), BF)
    lay(
        gb, S,
        [
            window(ghost_ref.at[0]), window(gown_ref.at[0]),
            row_parts(inner_ref, 1), row_parts(inner_ref, 2),
            row_parts(inner_ref, 13), row_parts(inner_ref, 14),
            window(gown_ref.at[1]), window(ghost_ref.at[1]),
        ],
    )

    def weight(r, c):
        return kernel_ref[3 * r + c]

    for c in range(3):
        ys[c, 8 + 144 : 8 + 640, :] = taps(gb, 0, 144, 496, c, [weight] * 3, -1, 1)
        edge = taps(gb, 0, 7 * S - 16, 96, c, [far_of(kernel_ref, fold), weight, weight], -1, 1)
        ys[c, 7 * S : 8 + 8 * S, :] = edge[8:]
    copies = []
    for i, (slot, r) in enumerate(((2, 0), (3, 1), (6, 14), (7, 15))):
        total = shifted(ys, slot * S, COLS, -1)
        rows_out[i] = keep_cells(total, keep_t[:, r : r + 1])
        copies.append(pltpu.make_async_copy(rows_out.at[i], sgrad_ref.at[0, r], sems.at[i]))
        copies[-1].start()
    for copy in copies:
        copy.wait()


def state_kernel(
    lat_count, turn, inner_ref, gown_ref, ghost_ref, kernel_ref, keep_ref, after_ref, sgrad_in,
    sgrad_ref, done_ref, *scratch,
):
    del after_ref, sgrad_in
    done_ref[...] = jnp.zeros_like(done_ref)

    @pl.when(lax.axis_index("core") == turn)
    def _():
        state_rows(
            lat_count, inner_ref, gown_ref, ghost_ref, kernel_ref, keep_ref, sgrad_ref, *scratch
        )


def add_kernel(hold_ref, came_ref, after_ref, out_ref):
    del after_ref
    out_ref[...] = (hold_ref[...] + came_ref[...].astype(F32)).astype(BF)


def sum_kernel(parts_ref, out_ref):
    total = parts_ref[0].astype(F32)
    for i in range(1, parts_ref.shape[0]):
        total = total + parts_ref[i].astype(F32)
    total = total.astype(BF)
    for i in range(out_ref.shape[0]):
        out_ref[i] = total


def unpack_kernel(scale, mine_ref, other_ref, out_ref, held, sems):
    mine_first = lax.axis_index("core") == 0

    def get(half, at, size):
        a = mine_ref[at : at + size, :].astype(F32)
        b = other_ref[at : at + size, :].astype(F32)
        return jnp.where(mine_first == (half == 0), a, b) * scale

    pieces = (
        ((0, 0, 0, 192),),
        ((0, 192, 0, 96), (1, 0, 96, 96)),
        ((1, 96, 0, 192),),
    )
    one, two = get(0, 1152, 144), get(1, 1152, 144)
    rests = (
        ((0, one[:, 0:64]), (144, one[0:48, 64:128])),
        ((0, one[48:144, 64:128]), (96, two[0:96, 0:64])),
        ((0, two[96:144, 0:64]), (48, two[:, 64:128])),
    )
    copies = []
    for r in range(3):
        for half, source, at, size in pieces[r]:
            to = slice(at, at + size)
            for c in range(3):
                held[r, c, to, 0:128] = get(half, c * 288 + source, size)
            both = get(half, 864 + source, size)
            held[r, 0, to, 128:C] = both[:, 0:64]
            held[r, 1, to, 128:C] = both[:, 64:128]
        for at, rest in rests[r]:
            held[r, 2, at : at + rest.shape[0], 128:C] = rest
        copies.append(pltpu.make_async_copy(held.at[r], out_ref.at[r], sems.at[r]))
        copies[-1].start()
    for copy in copies:
        copy.wait()


def solution(mesh):
    lon_count, lat_count, dp_count = (mesh.shape[n] for n in ("lon", "lat", "dp"))
    z_count = lon_count // 4
    fine = Mesh(
        mesh.devices.reshape(z_count, 2, 2, lat_count, dp_count),
        ("z", "twin", "core", "lat", "dp"),
    )
    lon = ("z", "twin", "core")
    sheet = ("twin", "lat", "dp")
    sheet_count = 2 * lat_count * dp_count
    eastward = [(i, (i + 1) % lon_count) for i in range(lon_count)]
    westward = [(b, a) for a, b in eastward]
    lat_pairs, fold_pairs = [], []
    for b in range(lon_count):
        for a in range(lat_count):
            lat_pairs.append((b * lat_count + a, b * lat_count + (a ^ 1)))
            if a == lat_count - 1:
                fold_pairs.append((b * lat_count + a, (lon_count - 1 - b) * lat_count + a))
            elif a > 0:
                fold_pairs.append((b * lat_count + a, b * lat_count + (a + 1 if a % 2 else a - 1)))
    sheet_order = [[(i + sheet_count * 7 // 8) % sheet_count for i in range(sheet_count)]]
    z_order = [[(i + z_count // 2) % z_count for i in range(z_count)]]
    scale = 1.0 / math.sqrt(dp_count * lat_count * ROWS * lon_count * COLS)
    part = -(-HALF // (8 * sheet_count)) * 8
    half_rows = sheet_count * part
    smem = pl.BlockSpec(memory_space=pltpu.SMEM)
    vmem = pl.BlockSpec(memory_space=pltpu.VMEM)
    hbm = pl.BlockSpec(memory_space=pltpu.HBM)
    whole = jax.ShapeDtypeStruct((1, ROWS, COLS, C), BF)

    def shaped(shape, kind=BF):
        return jax.ShapeDtypeStruct(shape, kind)

    def call(kernel, name, ins, out_shape, outs, scratch=(), aliases=None, cost=0):
        return pl.pallas_call(
            kernel,
            out_shape=out_shape,
            in_specs=ins,
            out_specs=outs,
            scratch_shapes=list(scratch),
            input_output_aliases=aliases or {},
            compiler_params=pltpu.CompilerParams(vmem_limit_bytes=40 * 2**20),
            cost_estimate=pl.CostEstimate(
                flops=cost, bytes_accessed=2**20, transcendentals=0
            ) if cost else None,
            name=name,
        )

    def body(states, cotangent, kernel, land_mask, ocean_tiles):
        taps9 = kernel.reshape(9, C, C)
        cells = shaped((ROWS, COLS, C))
        east, west, x_raw, c_raw, keep = call(
            edge_kernel, "edges", [hbm] * 4,
            (shaped((3, ROWS, C)),) * 2 + (cells, cells, shaped((COLS, ROWS), F32)), (vmem,) * 5,
            scratch=[
                pltpu.VMEM((ROWS, COLS), jnp.int32),
                pltpu.SMEM(ocean_tiles.shape, jnp.int32),
                pltpu.SemaphoreType.DMA((4,)),
            ],
        )(*(pltpu.with_memory_space_constraint(v, pltpu.HBM)
            for v in (states, cotangent, land_mask, ocean_tiles)))
        from_west = lax.ppermute(east, lon, eastward)
        from_east = lax.ppermute(west, lon, westward)
        x, c = call(
            mask_kernel, "mask", [vmem] * 3, (cells, cells), (vmem,) * 2, cost=10**8,
        )(x_raw, c_raw, keep)
        own_fold, own_pair = call(
            line_kernel, "lines", [vmem] * 4, (shaped((MESSAGE, 128)),) * 2, (vmem,) * 2,
        )(x, c, from_west, from_east)
        pair = lax.ppermute(own_pair, lon + ("lat",), lat_pairs)
        fold = lax.ppermute(own_fold, lon + ("lat",), fold_pairs)
        output, state_grad, sums, inner_grad = call(
            inner_kernel, "inner", [vmem] * 6,
            (whole, whole, shaped((3, 576, C), F32), shaped((15 * S, C))), (vmem,) * 4,
            scratch=[
                pltpu.VMEM((LEAD + ROWS * S + 32, C), BF),
                pltpu.VMEM((LEAD + ROWS * S, C), BF),
                pltpu.VMEM((8 + ROWS * S + 16, C), F32),
                pltpu.VMEM((3, ROWS * S + 16, C), F32),
                pltpu.VMEM((576, 1152), BF),
            ],
            cost=2 * 10**9,
        )(x, c, taps9, keep, from_west, from_east)
        lines = (fold, pair, own_fold, own_pair)
        edge, gown, give, xt, moved = call(
            lambda *refs: border_kernel(lat_count, *refs), "border", [vmem] * 7,
            (
                shaped((2, COLS, C)), shaped((2, S, C)), shaped((half_rows, 128)),
                shaped((576, 384)), shaped((3, 384, C)),
            ),
            (vmem,) * 5,
            scratch=[
                pltpu.VMEM((8 * S, C), BF),
                pltpu.VMEM((7 * S, C), BF),
                pltpu.VMEM((7 * S, C), BF),
                pltpu.VMEM((7 * S, C), F32),
                pltpu.VMEM((3, 7 * S + 16, C), F32),
            ],
            cost=5 * 10**8,
        )(*lines, taps9, keep, sums)
        came = lax.ppermute(give, "core", [(0, 1), (1, 0)])
        ghost, hold, output = call(
            lambda *refs: ghost_kernel(lat_count, *refs), "ghost", [vmem] * 9 + [hbm],
            (shaped((2, S, C)), shaped((half_rows, 128), F32), whole), (vmem, vmem, hbm),
            scratch=[
                pltpu.VMEM((8 * S, C), BF),
                pltpu.VMEM((7 * S, C), BF),
                pltpu.VMEM((7 * S, C), BF),
                pltpu.VMEM((3, 7 * S + 16, C), F32),
                pltpu.SemaphoreType.DMA((2,)),
            ],
            aliases={9: 2}, cost=5 * 10**8,
        )(*lines, taps9, xt, moved, sums, edge, output)
        def bordered(turn, after, state_grad):
            return call(
                lambda *refs: state_kernel(lat_count, turn, *refs), "state", [vmem] * 6 + [hbm],
                (whole, shaped((8, 128), F32)), (hbm, vmem),
                scratch=[
                    pltpu.VMEM((10 * S, C), BF),
                    pltpu.VMEM((3, 8 * S + 16, C), F32),
                    pltpu.VMEM((4, COLS, C), BF),
                    pltpu.SemaphoreType.DMA((4,)),
                ],
                aliases={6: 0}, cost=5 * 10**8,
            )(inner_grad, gown, ghost, taps9, keep, after, state_grad)

        state_grad, done = bordered(1, keep, state_grad)

        def summed(parts, copies):
            return call(sum_kernel, "sum", [vmem], shaped((copies, part, 128)), vmem)(parts)

        parts = call(add_kernel, "add", [vmem] * 3, shaped((half_rows, 128)), vmem)(hold, came, done)
        parts = lax.all_to_all(
            parts.reshape(sheet_count, part, 128), sheet, 0, 0, axis_index_groups=sheet_order, tiled=True
        )
        parts = lax.all_to_all(
            summed(parts, z_count), "z", 0, 0, axis_index_groups=z_order, tiled=True
        )
        parts = lax.all_to_all(
            summed(parts, sheet_count), sheet, 0, 0, axis_index_groups=sheet_order, tiled=True
        )
        mine = parts.reshape(half_rows, 128)
        other = lax.ppermute(mine, "core", [(0, 1), (1, 0)])
        state_grad, _ = bordered(0, mine, state_grad)
        weight_grad = call(
            lambda *refs: unpack_kernel(scale, *refs), "unpack", [vmem] * 2,
            shaped((3, 3, C, C), F32), hbm,
            scratch=[pltpu.VMEM((3, 3, C, C), F32), pltpu.SemaphoreType.DMA((3,))],
        )(mine, other)
        return output, state_grad, weight_grad

    cells = P("dp", "lat", lon, None)
    return jax.shard_map(
        body,
        mesh=fine,
        in_specs=(cells, cells, P(), P("lat", lon), P("lat", lon, None)),
        out_specs=(cells, cells, P()),
        check_vma=False,
    )
```

```python
import math

import jax
import jax.numpy as jnp
from jax import lax
from jax.experimental import pallas as pl
from jax.experimental.pallas import tpu as pltpu
from jax.sharding import Mesh
from jax.sharding import PartitionSpec as P

BF = jnp.bfloat16
F32 = jnp.float32
TS = 16
ROWS = 16
COLS = 64
C = 192
S = 80
LEAD = 32
LINE = 72
MESSAGE = 4 * LINE + 40
HALF = 1296


def iota(shape, dim):
    return lax.broadcasted_iota(jnp.int32, shape, dim)


def keep_plane(mask_ref, tiles_ref):
    tile = iota((ROWS, COLS), 1) // TS
    listed = jnp.zeros((ROWS, COLS), F32)
    for slot in range(tiles_ref.shape[-1]):
        listed = jnp.where(tile == tiles_ref[0, 0, slot], 1.0, listed)
    return jnp.where(mask_ref[...] > 0, listed, 0.0)


def edge_kernel(
    states_ref, cot_ref, mask_hbm, tiles_hbm, east_ref, west_ref, x_ref, c_ref, keep_ref,
    mask_ref, tiles_ref, sems,
):
    pairs = [
        (mask_hbm, mask_ref), (tiles_hbm, tiles_ref), (states_ref.at[0], x_ref), (cot_ref.at[0], c_ref),
    ]
    copies = [pltpu.make_async_copy(*pair, sems.at[i]) for i, pair in enumerate(pairs)]
    for copy in copies:
        copy.start()
    copies[0].wait()
    copies[1].wait()
    keep = keep_plane(mask_ref, tiles_ref)
    keep_ref[...] = keep.T
    picks = {}
    for spot in (0, 1, 14, 15):
        pick = iota((ROWS, 256), 1) == iota((ROWS, 256), 0) * 16 + spot
        picks[spot] = pick.astype(F32).astype(BF)

    def column(ref, spot, col):
        part = slice(col - spot, col - spot + 16)
        cells = jnp.concatenate([ref[r, part, :] for r in range(ROWS)], axis=0)
        picked = jnp.dot(picks[spot], cells, preferred_element_type=F32)
        return jnp.where(keep[:, col : col + 1] > 0, picked, 0.0).astype(BF)

    copies[2].wait()
    east_ref[0] = column(x_ref, 14, COLS - 2)
    east_ref[1] = column(x_ref, 15, COLS - 1)
    west_ref[0] = column(x_ref, 0, 0)
    west_ref[1] = column(x_ref, 1, 1)
    copies[3].wait()
    east_ref[2] = column(c_ref, 15, COLS - 1)
    west_ref[2] = column(c_ref, 0, 0)


def mask_kernel(x_in, c_in, keep_ref, x_ref, c_ref):
    keep_t = keep_ref[...]
    for r in range(ROWS):
        x_ref[r] = keep_cells(x_in[r], keep_t[:, r : r + 1])
        c_ref[r] = keep_cells(c_in[r], keep_t[:, r : r + 1])


def halo_chunks(from_west, from_east, size):
    halo = jnp.concatenate(
        [from_west[i] for i in range(3)] + [from_east[i] for i in range(3)], axis=0
    )
    shape = (ROWS * size, 96)
    row = iota(shape, 0) // size
    spot = iota(shape, 0) % size
    source = iota(shape, 1)

    def chunk(at):
        want = jnp.full(shape, -1, jnp.int32)
        for where, plane in at:
            want = jnp.where(spot == where, plane * 16 + row, want)
        pick = (source == want).astype(F32).astype(BF)
        picked = jnp.dot(pick, halo, preferred_element_type=F32)
        return [picked[r * size : r * size + size] for r in range(ROWS)]

    return (
        chunk([(0, 3), (1, 4), (size - 2, 0), (size - 1, 1)]),
        chunk([(0, 5), (size - 1, 2)]),
    )


def keep_cells(cells, column):
    return jnp.where(column > 0, cells.astype(F32), 0.0).astype(BF)


def line_kernel(x_ref, c_ref, from_west, from_east, fold_ref, pair_ref):
    x_chunk, c_chunk = halo_chunks(from_west, from_east, 8)
    even = lax.axis_index("lat") % 2 == 0

    def full(ref, r, chunk):
        return jnp.concatenate([ref[r].astype(F32), chunk[r]], axis=0)

    def pack(one, two, three):
        rest = jnp.concatenate([one[:, 128:], two[:, 128:]], axis=1)
        wide = jnp.concatenate([three[40:, 128:], jnp.zeros((80 - LINE, 64), F32)], axis=0)
        last = jnp.concatenate([three[:40, 128:], wide], axis=1)
        return jnp.concatenate([one[:, :128], two[:, :128], three[:, :128], rest, last], axis=0)

    top = pack(full(x_ref, 15, x_chunk), full(x_ref, 14, x_chunk), full(c_ref, 15, c_chunk))
    bottom = pack(full(x_ref, 0, x_chunk), full(x_ref, 1, x_chunk), full(c_ref, 0, c_chunk))
    fold_ref[...] = jnp.where(even, bottom, top).astype(BF)
    pair_ref[...] = jnp.where(even, top, bottom).astype(BF)


def lay(dest, base, rows):
    low = iota((16, C), 0) < 8
    none = jnp.zeros((16, C), F32)
    tails = [none] + [none if r is None else r[1].astype(F32) for r in rows] + [none]
    for k in range(-1, len(rows)):
        at = base + k * S
        if k >= 0:
            dest[at : at + COLS, :] = jnp.zeros((COLS, C), BF) if rows[k] is None else rows[k][0]
        dest[at + COLS : at + S, :] = jnp.where(low, tails[k + 1], tails[k + 2]).astype(BF)


def window(ref):
    return ref[0:COLS, :], ref[COLS:S, :]


def taps(ref, base, at, size, c, weights, sign, contract):
    total = None
    for r in range(3):
        start = base + at + sign * (r - 1) * S
        term = lax.dot_general(
            ref[start : start + size, :], weights[r](r, c),
            (((1,), (contract,)), ((), ())), preferred_element_type=F32,
        )
        total = term if total is None else total + term
    return total


def shifted(ys, at, size, sign):
    at = at + 8
    return (
        ys[0, at - sign : at - sign + size, :]
        + ys[1, at : at + size, :]
        + ys[2, at + sign : at + sign + size, :]
    )


def weight_terms(xe, base, go, xt, lo, span):
    for r in range(3):
        start = base + lo + (r - 1) * S
        xt[r * C : (r + 1) * C, :] = xe[start : start + span, :].T
    starts = [8 + lo - (c - 1) for c in range(3)]
    return [go[start : start + span, :].astype(BF) for start in starts]


def inner_kernel(
    x_ref, c_ref, kernel_ref, keep_ref, from_west, from_east,
    out_ref, sgrad_ref, part_ref, ga,
    xe, ce, go, ys, xt,
):
    keep_t = keep_ref[...]
    x_chunk, c_chunk = halo_chunks(from_west, from_east, 16)

    def own(ref, chunk):
        return [(ref[r], chunk[r]) for r in range(ROWS)]

    xe[0:LEAD, :] = jnp.zeros((LEAD, C), BF)
    xe[LEAD + ROWS * S :, :] = jnp.zeros((xe.shape[0] - LEAD - ROWS * S, C), BF)
    lay(xe, LEAD, own(x_ref, x_chunk))
    lay(ce, LEAD, own(c_ref, c_chunk))

    def weight(r, c):
        return kernel_ref[3 * r + c]

    plain = [weight] * 3
    for c in range(3):
        for k in range(3):
            at = 48 + k * 384
            ys[c, 8 + at : 8 + at + 384, :] = taps(xe, LEAD, at, 384, c, plain, 1, 0)
        ys[c, 1208:1216, :] = jnp.zeros((8, C), F32)
    go[...] = jnp.zeros_like(go)
    ga[0:64, :] = jnp.zeros((64, C), BF)
    for w in range(15):
        at, size = (w * S, S) if w else (64, 16)
        pre = shifted(ys, at, size, 1)
        s = jax.nn.sigmoid(pre)
        slope = s * (1.0 + pre * (1.0 - s))
        grad = (ce[LEAD + at : LEAD + at + size, :].astype(F32) * slope).astype(BF)
        ga[at : at + size, :] = grad
        if w:
            go[8 + at : 8 + at + COLS, :] = grad[0:COLS].astype(F32)
            kept = keep_t[:, w : w + 1]
            out_ref[0, w] = (kept * pre[0:COLS] * s[0:COLS]).astype(BF)
    for c in range(3):
        for k in range(3):
            at = 112 + k * 336
            ys[c, 8 + at : 8 + at + 336, :] = taps(ga, 0, at, 336, c, plain, -1, 1)
    for r in range(2, 14):
        sgrad_ref[0, r] = keep_cells(shifted(ys, r * S, COLS, -1), keep_t[:, r : r + 1])
    for r in (0, 15):
        out_ref[0, r] = jnp.zeros((COLS, C), BF)
    for r in (0, 1, 14, 15):
        sgrad_ref[0, r] = jnp.zeros((COLS, C), BF)
    moved = weight_terms(xe, LEAD, go, xt, 64, 1152)
    for c in range(3):
        part_ref[c] = jnp.dot(xt[...], moved[c], preferred_element_type=F32)


def far_of(kernel_ref, fold):
    def far_weight(r, c):
        return kernel_ref[jnp.where(fold, 8 - (3 * r + c), 3 * r + c)]

    return far_weight


def border_rows(fold, fold_ref, pair_ref, own_fold, own_pair):
    even = lax.axis_index("lat") % 2 == 0
    down = iota((LINE, LINE), 0)
    across = iota((LINE, LINE), 1)
    turned = ((down + across == COLS - 1) | (down + across == COLS - 1 + LINE)).astype(F32)
    straight = (down == across).astype(F32)
    turn = jnp.where(fold, turned, straight).astype(BF)

    def choose(a, b):
        return jnp.where(even, a[...].astype(F32), b[...].astype(F32))

    def split(message, turned_by=None):
        blocks = [message[i * LINE : (i + 1) * LINE] for i in range(4)]
        last = message[4 * LINE :]
        rows = [
            jnp.concatenate([blocks[0], blocks[3][:, 0:64]], axis=1),
            jnp.concatenate([blocks[1], blocks[3][:, 64:128]], axis=1),
            jnp.concatenate([
                blocks[2], jnp.concatenate([last[:, 0:64], last[0 : LINE - 40, 64:128]], axis=0)
            ], axis=1),
        ]
        if turned_by is not None:
            rows = [
                jnp.dot(turned_by, r.astype(BF), preferred_element_type=F32) for r in rows
            ]
        return [
            (r[0:COLS].astype(BF), jnp.concatenate([r[COLS:LINE], r[COLS:LINE]], axis=0))
            for r in rows
        ]

    south = split(choose(fold_ref, pair_ref))
    north = split(choose(pair_ref, fold_ref), turn)
    top = split(choose(own_pair, own_fold))
    bottom = split(choose(own_fold, own_pair))
    return south, bottom, top, north


def slope_at(ys, at, size):
    pre = shifted(ys, at, size, 1)
    s = jax.nn.sigmoid(pre)
    return pre, s, s * (1.0 + pre * (1.0 - s))


def row_parts(ga, slot):
    low = iota((16, C), 0) < 8
    east = ga[slot * S + COLS : slot * S + S, :].astype(F32)
    west = ga[(slot - 1) * S + COLS : slot * S, :].astype(F32)
    return ga[slot * S : slot * S + COLS, :], jnp.where(low, east, west).astype(BF)


def row_of(ga, slot, dest):
    dest[0:COLS, :], dest[COLS:S, :] = row_parts(ga, slot)


def pack_half(half, xt, moved, part_ref, dest):
    mine = pl.ds(pl.multiple_of(half * 288, 288), 288)
    tails = []
    for c in range(3):
        grad = jnp.dot(xt[mine, :], moved[c], preferred_element_type=F32) + part_ref[c, mine, :]
        dest[c * 288 : (c + 1) * 288, :] = grad[:, 0:128].astype(dest.dtype)
        tails.append(grad[:, 128:C])
    dest[864:1152, :] = jnp.concatenate(tails[0:2], axis=1).astype(dest.dtype)
    rest = jnp.concatenate([tails[2][0:144], tails[2][144:288]], axis=1)
    dest[1152:HALF, :] = rest.astype(dest.dtype)
    if dest.shape[0] > HALF:
        dest[HALF:, :] = jnp.zeros((dest.shape[0] - HALF, 128), dest.dtype)


def border_kernel(
    lat_count,
    fold_ref, pair_ref, own_fold, own_pair, kernel_ref, keep_ref, part_ref,
    edge_ref, gown_ref, give_ref, xt, moved_ref,
    xb, cb, ga, go, ys,
):
    fold = lax.axis_index("lat") == lat_count - 1
    keep_t = keep_ref[...]
    south, bottom, top, north = border_rows(fold, fold_ref, pair_ref, own_fold, own_pair)
    xb[0:S, :] = jnp.zeros((S, C), BF)
    xb[7 * S :, :] = jnp.zeros((xb.shape[0] - 7 * S, C), BF)
    lay(xb, S, [south[0], bottom[0], bottom[1], top[1], top[0], north[0]])
    lay(cb, S, [None, bottom[2], None, None, top[2], None])

    def weight(r, c):
        return kernel_ref[3 * r + c]

    for c in range(3):
        ys[c, 8 + 144 : 8 + 480, :] = taps(xb, 0, 144, 336, c, [weight] * 3, 1, 0)
        ys[c, 144:152, :] = jnp.zeros((8, C), F32)
        ys[c, 488:496, :] = jnp.zeros((8, C), F32)
    go[...] = jnp.zeros_like(go)
    for slot in (1, 2, 4, 5):
        at, size = (slot * S + COLS, 16) if slot in (1, 4) else (slot * S, S)
        pre, s, slope = slope_at(ys, at, size)
        grad = (cb[at : at + size, :].astype(F32) * slope).astype(BF)
        ga[at : at + size, :] = grad
        if slot in (2, 5):
            go[8 + at : 8 + at + COLS, :] = grad[0:COLS].astype(F32)
            r = 0 if slot == 2 else ROWS - 1
            kept = keep_t[:, r : r + 1]
            edge_ref[slot // 5] = (kept * pre[0:COLS] * s[0:COLS]).astype(BF)
    row_of(ga, 2, gown_ref.at[0])
    row_of(ga, 5, gown_ref.at[1])
    moved = weight_terms(xb, 0, go, xt, 144, 384)
    for c in range(3):
        moved_ref[c] = moved[c]
    pack_half(1 - lax.axis_index("core"), xt, moved, part_ref, give_ref)


def ghost_kernel(
    lat_count, fold_ref, pair_ref, own_fold, own_pair, kernel_ref,
    xt, moved_ref, part_ref, edge_ref, out_in,
    ghost_ref, hold_ref, out_ref, xb, cb, ga, ys, sems,
):
    del out_in
    copies = [
        pltpu.make_async_copy(edge_ref.at[i], out_ref.at[0, r], sems.at[i])
        for i, r in enumerate((0, ROWS - 1))
    ]
    for copy in copies:
        copy.start()
    pack_half(lax.axis_index("core"), xt, [moved_ref[c] for c in range(3)], part_ref, hold_ref)
    fold = lax.axis_index("lat") == lat_count - 1
    south, bottom, top, north = border_rows(fold, fold_ref, pair_ref, own_fold, own_pair)
    xb[0:S, :] = jnp.zeros((S, C), BF)
    xb[7 * S :, :] = jnp.zeros((xb.shape[0] - 7 * S, C), BF)
    lay(xb, S, [south[1], south[0], bottom[0], top[0], north[0], north[1]])
    lay(cb, S, [None, south[2], None, None, north[2], None])

    def weight(r, c):
        return kernel_ref[3 * r + c]

    far_weight = far_of(kernel_ref, fold)
    for c in range(3):
        ys[c, 152:248, :] = taps(xb, 0, 144, 96, c, [weight] * 3, 1, 0)
        ys[c, 392:488, :] = taps(xb, 0, 384, 96, c, [far_weight] * 3, 1, 0)
        for at in (144, 248, 384, 488):
            ys[c, at : at + 8, :] = jnp.zeros((8, C), F32)
    for at in (144, 384):
        grad = cb[at : at + 96, :].astype(F32) * slope_at(ys, at, 96)[2]
        ga[at : at + 96, :] = grad.astype(BF)
    row_of(ga, 2, ghost_ref.at[0])
    row_of(ga, 5, ghost_ref.at[1])
    for copy in copies:
        copy.wait()


def state_kernel(
    lat_count, inner_ref, gown_ref, ghost_ref, kernel_ref, keep_ref, sgrad_in,
    sgrad_ref, gb, ys, rows_out, sems,
):
    del sgrad_in
    fold = lax.axis_index("lat") == lat_count - 1
    keep_t = keep_ref[...]
    gb[0:S, :] = jnp.zeros((S, C), BF)
    gb[9 * S :, :] = jnp.zeros((gb.shape[0] - 9 * S, C), BF)
    lay(
        gb, S,
        [
            window(ghost_ref.at[0]), window(gown_ref.at[0]),
            row_parts(inner_ref, 1), row_parts(inner_ref, 2),
            row_parts(inner_ref, 13), row_parts(inner_ref, 14),
            window(gown_ref.at[1]), window(ghost_ref.at[1]),
        ],
    )

    def weight(r, c):
        return kernel_ref[3 * r + c]

    for c in range(3):
        ys[c, 8 + 144 : 8 + 640, :] = taps(gb, 0, 144, 496, c, [weight] * 3, -1, 1)
        edge = taps(gb, 0, 7 * S - 16, 96, c, [far_of(kernel_ref, fold), weight, weight], -1, 1)
        ys[c, 7 * S : 8 + 8 * S, :] = edge[8:]
    copies = []
    for i, (slot, r) in enumerate(((2, 0), (3, 1), (6, 14), (7, 15))):
        total = shifted(ys, slot * S, COLS, -1)
        rows_out[i] = keep_cells(total, keep_t[:, r : r + 1])
        copies.append(pltpu.make_async_copy(rows_out.at[i], sgrad_ref.at[0, r], sems.at[i]))
        copies[-1].start()
    for copy in copies:
        copy.wait()


def add_kernel(hold_ref, came_ref, out_ref):
    out_ref[...] = (hold_ref[...] + came_ref[...].astype(F32)).astype(BF)


def sum_kernel(parts_ref, out_ref):
    total = parts_ref[0].astype(F32)
    for i in range(1, parts_ref.shape[0]):
        total = total + parts_ref[i].astype(F32)
    total = total.astype(BF)
    for i in range(out_ref.shape[0]):
        out_ref[i] = total


def unpack_kernel(scale, mine_ref, other_ref, out_ref, held, sems):
    mine_first = lax.axis_index("core") == 0

    def get(half, at, size):
        a = mine_ref[at : at + size, :].astype(F32)
        b = other_ref[at : at + size, :].astype(F32)
        return jnp.where(mine_first == (half == 0), a, b) * scale

    pieces = (
        ((0, 0, 0, 192),),
        ((0, 192, 0, 96), (1, 0, 96, 96)),
        ((1, 96, 0, 192),),
    )
    one, two = get(0, 1152, 144), get(1, 1152, 144)
    rests = (
        ((0, one[:, 0:64]), (144, one[0:48, 64:128])),
        ((0, one[48:144, 64:128]), (96, two[0:96, 0:64])),
        ((0, two[96:144, 0:64]), (48, two[:, 64:128])),
    )
    copies = []
    for r in range(3):
        for half, source, at, size in pieces[r]:
            to = slice(at, at + size)
            for c in range(3):
                held[r, c, to, 0:128] = get(half, c * 288 + source, size)
            both = get(half, 864 + source, size)
            held[r, 0, to, 128:C] = both[:, 0:64]
            held[r, 1, to, 128:C] = both[:, 64:128]
        for at, rest in rests[r]:
            held[r, 2, at : at + rest.shape[0], 128:C] = rest
        copies.append(pltpu.make_async_copy(held.at[r], out_ref.at[r], sems.at[r]))
        copies[-1].start()
    for copy in copies:
        copy.wait()


def solution(mesh):
    lon_count, lat_count, dp_count = (mesh.shape[n] for n in ("lon", "lat", "dp"))
    z_count = lon_count // 4
    fine = Mesh(
        mesh.devices.reshape(z_count, 2, 2, lat_count, dp_count),
        ("z", "twin", "core", "lat", "dp"),
    )
    lon = ("z", "twin", "core")
    sheet = ("twin", "lat", "dp")
    sheet_count = 2 * lat_count * dp_count
    eastward = [(i, (i + 1) % lon_count) for i in range(lon_count)]
    westward = [(b, a) for a, b in eastward]
    lat_pairs, fold_pairs = [], []
    for b in range(lon_count):
        for a in range(lat_count):
            lat_pairs.append((b * lat_count + a, b * lat_count + (a ^ 1)))
            if a == lat_count - 1:
                fold_pairs.append((b * lat_count + a, (lon_count - 1 - b) * lat_count + a))
            elif a > 0:
                fold_pairs.append((b * lat_count + a, b * lat_count + (a + 1 if a % 2 else a - 1)))
    sheet_order = [[(i + sheet_count * 7 // 8) % sheet_count for i in range(sheet_count)]]
    z_order = [[(i + z_count * 3 // 8) % z_count for i in range(z_count)]]
    scale = 1.0 / math.sqrt(dp_count * lat_count * ROWS * lon_count * COLS)
    part = -(-HALF // (8 * sheet_count)) * 8
    half_rows = sheet_count * part
    smem = pl.BlockSpec(memory_space=pltpu.SMEM)
    vmem = pl.BlockSpec(memory_space=pltpu.VMEM)
    hbm = pl.BlockSpec(memory_space=pltpu.HBM)
    whole = jax.ShapeDtypeStruct((1, ROWS, COLS, C), BF)

    def shaped(shape, kind=BF):
        return jax.ShapeDtypeStruct(shape, kind)

    def call(kernel, name, ins, out_shape, outs, scratch=(), aliases=None, cost=0):
        return pl.pallas_call(
            kernel,
            out_shape=out_shape,
            in_specs=ins,
            out_specs=outs,
            scratch_shapes=list(scratch),
            input_output_aliases=aliases or {},
            compiler_params=pltpu.CompilerParams(vmem_limit_bytes=40 * 2**20),
            cost_estimate=pl.CostEstimate(
                flops=cost, bytes_accessed=2**20, transcendentals=0
            ) if cost else None,
            name=name,
        )

    def body(states, cotangent, kernel, land_mask, ocean_tiles):
        taps9 = kernel.reshape(9, C, C)
        cells = shaped((ROWS, COLS, C))
        east, west, x_raw, c_raw, keep = call(
            edge_kernel, "edges", [hbm] * 4,
            (shaped((3, ROWS, C)),) * 2 + (cells, cells, shaped((COLS, ROWS), F32)), (vmem,) * 5,
            scratch=[
                pltpu.VMEM((ROWS, COLS), jnp.int32),
                pltpu.SMEM(ocean_tiles.shape, jnp.int32),
                pltpu.SemaphoreType.DMA((4,)),
            ],
        )(*(pltpu.with_memory_space_constraint(v, pltpu.HBM)
            for v in (states, cotangent, land_mask, ocean_tiles)))
        from_west = lax.ppermute(east, lon, eastward)
        from_east = lax.ppermute(west, lon, westward)
        x, c = call(
            mask_kernel, "mask", [vmem] * 3, (cells, cells), (vmem,) * 2, cost=10**8,
        )(x_raw, c_raw, keep)
        own_fold, own_pair = call(
            line_kernel, "lines", [vmem] * 4, (shaped((MESSAGE, 128)),) * 2, (vmem,) * 2,
        )(x, c, from_west, from_east)
        pair = lax.ppermute(own_pair, lon + ("lat",), lat_pairs)
        fold = lax.ppermute(own_fold, lon + ("lat",), fold_pairs)
        output, state_grad, sums, inner_grad = call(
            inner_kernel, "inner", [vmem] * 6,
            (whole, whole, shaped((3, 576, C), F32), shaped((15 * S, C))), (vmem,) * 4,
            scratch=[
                pltpu.VMEM((LEAD + ROWS * S + 32, C), BF),
                pltpu.VMEM((LEAD + ROWS * S, C), BF),
                pltpu.VMEM((8 + ROWS * S + 16, C), F32),
                pltpu.VMEM((3, ROWS * S + 16, C), F32),
                pltpu.VMEM((576, 1152), BF),
            ],
            cost=2 * 10**9,
        )(x, c, taps9, keep, from_west, from_east)
        lines = (fold, pair, own_fold, own_pair)
        edge, gown, give, xt, moved = call(
            lambda *refs: border_kernel(lat_count, *refs), "border", [vmem] * 7,
            (
                shaped((2, COLS, C)), shaped((2, S, C)), shaped((half_rows, 128)),
                shaped((576, 384)), shaped((3, 384, C)),
            ),
            (vmem,) * 5,
            scratch=[
                pltpu.VMEM((8 * S, C), BF),
                pltpu.VMEM((7 * S, C), BF),
                pltpu.VMEM((7 * S, C), BF),
                pltpu.VMEM((7 * S, C), F32),
                pltpu.VMEM((3, 7 * S + 16, C), F32),
            ],
            cost=5 * 10**8,
        )(*lines, taps9, keep, sums)
        came = lax.ppermute(give, "core", [(0, 1), (1, 0)])
        ghost, hold, output = call(
            lambda *refs: ghost_kernel(lat_count, *refs), "ghost", [vmem] * 9 + [hbm],
            (shaped((2, S, C)), shaped((half_rows, 128), F32), whole), (vmem, vmem, hbm),
            scratch=[
                pltpu.VMEM((8 * S, C), BF),
                pltpu.VMEM((7 * S, C), BF),
                pltpu.VMEM((7 * S, C), BF),
                pltpu.VMEM((3, 7 * S + 16, C), F32),
                pltpu.SemaphoreType.DMA((2,)),
            ],
            aliases={9: 2}, cost=5 * 10**8,
        )(*lines, taps9, xt, moved, sums, edge, output)
        state_grad = call(
            lambda *refs: state_kernel(lat_count, *refs), "state",
            [vmem] * 5 + [hbm], whole, hbm,
            scratch=[
                pltpu.VMEM((10 * S, C), BF),
                pltpu.VMEM((3, 8 * S + 16, C), F32),
                pltpu.VMEM((4, COLS, C), BF),
                pltpu.SemaphoreType.DMA((4,)),
            ],
            aliases={5: 0}, cost=5 * 10**8,
        )(inner_grad, gown, ghost, taps9, keep, state_grad)

        def summed(parts, copies):
            return call(sum_kernel, "sum", [vmem], shaped((copies, part, 128)), vmem)(parts)

        parts = call(add_kernel, "add", [vmem] * 2, shaped((half_rows, 128)), vmem)(hold, came)
        parts = lax.all_to_all(
            parts.reshape(sheet_count, part, 128), sheet, 0, 0, axis_index_groups=sheet_order, tiled=True
        )
        parts = lax.all_to_all(
            summed(parts, z_count), "z", 0, 0, axis_index_groups=z_order, tiled=True
        )
        parts = lax.all_to_all(
            summed(parts, sheet_count), sheet, 0, 0, axis_index_groups=sheet_order, tiled=True
        )
        mine = parts.reshape(half_rows, 128)
        other = lax.ppermute(mine, "core", [(0, 1), (1, 0)])
        weight_grad = call(
            lambda *refs: unpack_kernel(scale, *refs), "unpack", [vmem] * 2,
            shaped((3, 3, C, C), F32), hbm,
            scratch=[pltpu.VMEM((3, 3, C, C), F32), pltpu.SemaphoreType.DMA((3,))],
        )(mine, other)
        return output, state_grad, weight_grad

    cells = P("dp", "lat", lon, None)
    return jax.shard_map(
        body,
        mesh=fine,
        in_specs=(cells, cells, P(), P("lat", lon), P("lat", lon, None)),
        out_specs=(cells, cells, P()),
        check_vma=False,
    )
```
